32 devices in a mesh: section: 2 (over core), shard: 4 (over z), replica: 4 (over y, x).
Axes of the slice: x: 2, y: 2, z: 4, core: 2. Of those that a mesh axis runs over, the one named last changes fastest.
Arguments:
- frames: bfloat16 [16384, 768], P(('shard', 'replica')), may hold values from -6 to 6
- cotangent: bfloat16 [16384, 768], P(('shard', 'replica')), may hold values from -6 to 6
- segments: int32 [16384], P(('shard', 'replica')), may hold values from -1 to 15, as said below
- layer_keep: int32 [2, 32], P('section', ('shard', 'replica')), may hold values 0 or 1
- joint_weight: bfloat16 [2, 768, 2304], P('section'), may hold values from -0.21875 to 0.21875
- output_weight: bfloat16 [2, 768, 768], P('section'), may hold values from -0.875 to 0.875
- up_weight: bfloat16 [2, 768, 3072], P('section'), may hold values from -0.21875 to 0.21875
- down_weight: bfloat16 [2, 3072, 768], P('section'), may hold values from -0.109375 to 0.109375
- width_bias: float32 [2, 4, 768], P('section'), may hold values from -3 to 3
- hidden_bias: float32 [2, 3072], P('section'), may hold values from -3 to 3
- norm_gain: float32 [2, 2, 768], P('section'), may hold values from 0.25 to 1.75
- norm_shift: float32 [2, 2, 768], P('section'), may hold values from -3 to 3
Outputs:
- layer_out: bfloat16 [2, 16384, 768], P('section', ('shard', 'replica'))
- input_gradient: float32 [2, 16384, 768], P('section', ('shard', 'replica'))
- joint_gradient: float32 [2, 768, 2304], P('section', 'shard')
- output_gradient: float32 [2, 768, 768], P('section', 'shard')
- up_gradient: float32 [2, 768, 3072], P('section', 'shard')
- down_gradient: float32 [2, 3072, 768], P('section', None, 'shard')
- width_gradient: float32 [2, 4, 768], P('section', None, 'shard')
- hidden_gradient: float32 [2, 3072], P('section', 'shard')
- gain_gradient: float32 [2, 2, 768], P('section', None, 'shard')
- shift_gradient: float32 [2, 2, 768], P('section', None, 'shard')
The draws below stay inside these ranges and needn't reach their ends.
Inputs may be any that keep to these rules, and one draw needn't show every extreme that they name: `segments`: within each aligned block of 512 slots (one micro-batch of one device) an utterance's frames are consecutive and share one number; utterances are numbered 0, 1, 2, ... in order, at most 16 a block; padding (-1) comes after the utterances of its block. Some block holds a single utterance of 512 frames, some block holds 16 utterances of equal length, and some block ends in padding.
All inputs are finite; a program needn't handle non-finite values. No bound on the sum of `layer_keep` on one device may be relied on, other than what follows from the above.
Results may differ from the reference program's by a relative error of at most 0.019.
Values may be sent and summed in bfloat16 or wider, within the bound.
A program may use at most 320 MiB of HBM per device.

```python
import jax
import jax.numpy as jnp
from jax import lax

D = 768
HEADS = 12
HEAD_SIZE = 64
FF = 3072
BATCH_ROWS = 512
TOKENS = 16384
ALL_BATCHES = 32


def draw_segments(key, part):
    key = jax.random.fold_in(key, 11)
    blocks = TOKENS // BATCH_ROWS
    slots = 16
    first_key, second_key, third_key = jax.random.split(key, 3)
    power = jax.random.randint(first_key, (blocks, slots), 0, 6)
    upper = jnp.maximum(jnp.right_shift(jnp.full((blocks, slots), BATCH_ROWS, jnp.int32), power), 4)
    lengths = jax.random.randint(second_key, (blocks, slots), upper // 2, upper + 1)
    chosen = jax.random.randint(third_key, (), 0, blocks)
    order = jnp.arange(blocks)
    leading = jnp.where(order == chosen, BATCH_ROWS, lengths[:, 0])
    leading = jnp.where(order == (chosen + 1) % blocks, BATCH_ROWS - 1, leading)
    lengths = jnp.concatenate([leading[:, None], lengths[:, 1:]], axis=1)
    even_block = (order == (chosen + 2) % blocks)[:, None]
    lengths = jnp.where(even_block, BATCH_ROWS // slots, lengths)
    ends = jnp.cumsum(lengths, axis=1)
    places = jnp.arange(BATCH_ROWS)
    number = jnp.sum((ends[:, None, :] <= places[None, :, None]).astype(jnp.int32), axis=-1)
    closing = jnp.take_along_axis(ends, jnp.minimum(number, slots - 1), axis=1)
    fitting = (number < slots) & (closing <= BATCH_ROWS)
    return jnp.where(fitting, number, -1).astype(jnp.int32).reshape(TOKENS)


def touch_ends(values, stream_key, smallest, high):
    place = [jax.random.randint(jax.random.fold_in(stream_key, axis), (), 0, length) for axis, length in enumerate(values.shape)]
    main_axis = values.shape.index(max(values.shape))
    neighbour = place[:main_axis] + [(place[main_axis] + 1) % values.shape[main_axis]] + place[main_axis + 1:]
    return values.at[tuple(place)].set(smallest).at[tuple(neighbour)].set(high)


def strengthened(values, stream_key, source, target, shards_of, factor):
    def block_of(axis_at):
        return (jnp.arange(values.shape[axis_at]) // (values.shape[axis_at] // shards_of)).reshape((-1,) + (1,) * (values.ndim - 1 - axis_at))

    near = jax.random.permutation(stream_key, shards_of)[block_of(target)]
    other_side = (block_of(target) + shards_of // 2) % shards_of
    return jnp.where((block_of(source) == near) | (block_of(source) == other_side), factor * values, values)


def level_of(rng, shape, cuts, least, top_value):
    def one(position, parts):
        heights = jax.random.uniform(jax.random.fold_in(jax.random.fold_in(rng, 6), position), (parts,), jnp.float32, least / len(cuts), top_value / len(cuts))
        return jnp.repeat(jnp.exp(heights), shape[position] // parts).reshape((-1,) + (1,) * (len(shape) - position - 1))

    loudness = one(*cuts[0])
    for cut in cuts[1:]:
        loudness = loudness * one(*cut)
    return loudness


def bell_draw(own_key, dims, scale, most, pieces=(), kind=jnp.bfloat16):
    level = level_of(own_key, dims, pieces, -0.22, 0.18) if pieces else 1.0
    values = jax.random.normal(own_key, dims, jnp.float32) * scale * level
    return jnp.minimum(jnp.maximum(values, -most), most).astype(kind)


def gaussian_with(rng, dims, scale, most, pieces, heavy, dtype=jnp.bfloat16):
    entries = scale * jax.random.normal(rng, dims, jnp.float32)
    if pieces:
        entries = entries * level_of(rng, dims, pieces, -0.22, 0.18)
    return jnp.clip(strengthened(entries, jax.random.fold_in(rng, 3), *heavy), -most, most).astype(dtype)


def setup_inputs(seed: int = 0) -> dict:
    splits = jax.random.split(jax.random.key(seed), 13)
    frames = bell_draw(splits[0], (TOKENS, D), 1.0, 6.0, ((0, 16),))
    cotangent = gaussian_with(splits[1], (TOKENS, D), 1.0, 6.0, ((0, 16),), (0, 1, 16, 2.0))
    segments = draw_segments(jax.random.fold_in(splits[12], 71), 0)
    layer_keep = touch_ends((jax.random.randint(splits[3], (2, ALL_BATCHES), 0, 4) < 3).astype(jnp.int32), jax.random.fold_in(splits[3], 1), 0, 1)
    joint_weight = bell_draw(splits[4], (2, D, 3 * D), D ** -0.5, 0.21875, ((0, 2),))
    output_weight = bell_draw(splits[5], (2, D, D), (D // 16) ** -0.5, 0.875, ((0, 2),))
    up_weight = bell_draw(splits[6], (2, D, FF), D ** -0.5, 0.21875, ((0, 2),))
    down_weight = bell_draw(splits[7], (2, FF, D), FF ** -0.5, 0.109375, ((0, 2),))
    width_bias = bell_draw(splits[8], (2, 4, D), 0.5, 3.0, ((0, 2),), jnp.float32)
    hidden_bias = bell_draw(splits[9], (2, FF), 0.5, 3.0, ((0, 2),), jnp.float32)
    norm_gain = jnp.clip(1.0 + 0.15 * jax.random.normal(splits[10], (2, 2, D), jnp.float32), 0.25, 1.75)
    norm_shift = bell_draw(splits[11], (2, 2, D), 0.5, 3.0, ((0, 2),), jnp.float32)
    return dict(frames=frames, cotangent=cotangent, segments=segments, layer_keep=layer_keep, joint_weight=joint_weight, output_weight=output_weight, up_weight=up_weight, down_weight=down_weight, width_bias=width_bias, hidden_bias=hidden_bias, norm_gain=norm_gain, norm_shift=norm_shift)


@jax.custom_vjp
def low(v):
    return lax.optimization_barrier(v.astype(jnp.bfloat16)).astype(jnp.float32)

@jax.custom_vjp
def low_back(v):
    return v

def low_keep(v):
    return (low(v), None)

def low_pass(kept, grad):
    return (grad,)

def back_keep(v):
    return (v, None)

def back_low(kept, grad):
    return (low(grad),)
low.defvjp(low_keep, low_pass)
low_back.defvjp(back_keep, back_low)
highest = lax.Precision.HIGHEST
epsilon = 1e-05
masked_score = -1e+30

def product(left, right):
    return jnp.dot(left, right, precision=highest, preferred_element_type=jnp.float32)

def layer_norm(value, gain, shift):
    centre = value - lax.optimization_barrier(jnp.mean(value, axis=-1, keepdims=True))
    spread = lax.optimization_barrier(jnp.mean(centre * centre, axis=-1, keepdims=True))
    return centre * lax.rsqrt(spread + epsilon) * gain + shift

def attend(query, keys, values, labels):
    scores = jnp.einsum('qhd,khd->hqk', query, keys, precision=highest) * HEAD_SIZE ** (-0.5)
    scores = low_back(scores)
    allowed = labels[:, None] == labels[None, :]
    scores = jnp.where(allowed[None], scores, masked_score)
    probs = low(jax.nn.softmax(scores, axis=-1))
    return jnp.einsum('hqk,khd->qhd', probs, values, precision=highest)

def block_layer(params, inputs, labels, flag):
    joint_weight, output_weight, up_weight, down_weight, width_bias, hidden_bias, norm_gain, norm_shift = params
    rows = inputs.shape[0]
    width = inputs.shape[1]
    joint_bias = jnp.concatenate([width_bias[0], jnp.zeros((width,), jnp.float32), width_bias[1]])
    inputs_low = low(inputs)
    joint = low_back(low(product(inputs_low, joint_weight) + joint_bias))
    query = joint[:, :width].reshape(rows, HEADS, HEAD_SIZE)
    keys = joint[:, width:2 * width].reshape(rows, HEADS, HEAD_SIZE)
    values = joint[:, 2 * width:].reshape(rows, HEADS, HEAD_SIZE)
    mixed = low_back(low(attend(query, keys, values, labels).reshape(rows, width)))
    first_sum = inputs + low_back(product(mixed, output_weight) + width_bias[2])
    hidden = layer_norm(first_sum, norm_gain[0], norm_shift[0])
    up_value = low_back(product(low(hidden), up_weight) + hidden_bias)
    active = low(jax.nn.gelu(up_value, approximate=False))
    second_sum = hidden + low_back(product(active, down_weight) + width_bias[3])
    result = layer_norm(second_sum, norm_gain[1], norm_shift[1])
    valid = (labels >= 0).astype(jnp.float32)[:, None]
    return low(valid * (flag * result + (1.0 - flag) * inputs))

def layer(inputs, labels, flags, params):
    width = inputs.shape[1]
    blocks = inputs.shape[0] // BATCH_ROWS

    def one_block(items):
        return block_layer(params, items[0], items[1], items[2])
    outputs = lax.map(jax.checkpoint(one_block), (inputs.reshape(blocks, BATCH_ROWS, width), labels.reshape(blocks, BATCH_ROWS), flags))
    return outputs.reshape(blocks * BATCH_ROWS, width)

def reference(frames, cotangent, segments, layer_keep, joint_weight, output_weight, up_weight, down_weight, width_bias, hidden_bias, norm_gain, norm_shift):
    arrays = (joint_weight, output_weight, up_weight, down_weight, width_bias, hidden_bias, norm_gain, norm_shift)

    def run(level, inputs):
        flags = layer_keep[level].astype(jnp.float32)
        params = tuple((array[level].astype(jnp.float32) for array in arrays))

        def apply(value, *weights):
            return layer(value, segments, flags, weights)
        return jax.vjp(apply, inputs, *params)
    first_out, first_back = run(0, frames.astype(jnp.float32))
    second_out, second_back = run(1, first_out)
    second_grads = second_back(cotangent.astype(jnp.float32))
    first_grads = first_back(second_grads[0])
    layer_out = jnp.stack([first_out, second_out]).astype(jnp.bfloat16)
    input_gradient = jnp.stack([first_grads[0], second_grads[0]])
    stacked = [jnp.stack([first_grads[index], second_grads[index]]) for index in range(1, 9)]
    return (layer_out, input_gradient, stacked[0], stacked[1], stacked[2], stacked[3], stacked[4], stacked[5], stacked[6], stacked[7])
```

```python
import functools

import jax
import jax.numpy as jnp
from jax import lax
from jax.experimental import pallas as pl
from jax.experimental.pallas import tpu as pltpu
from jax.sharding import PartitionSpec as P

SECTION_AXIS, SHARD_AXIS, REPLICA_AXIS = "section", "shard", "replica"
QKV, DOWN = "qkv", "down"

HEADS = 12
HEAD_SIZE = 64
BATCH_ROWS = 512
BATCHES = 2


epsilon = 1e-05
masked_score = -1e30


def shifted(block, axis, distance):
    devices = range(lax.axis_size(axis))
    route = [(i - distance, i) for i in devices if i - distance in devices]
    return lax.ppermute(block, axis, route)


def layer_norm(value, gain, shift):
    centre = value - jnp.mean(value, axis=-1, keepdims=True)
    spread = jnp.mean(centre * centre, axis=-1, keepdims=True)
    return centre * lax.rsqrt(spread + epsilon) * gain + shift


def exact_gelu(value):
    return jax.nn.gelu(value, approximate=False)


def over_rows(left, right):
    return lax.dot_general(
        left, right, (((0,), (0,)), ((), ())), preferred_element_type=jnp.float32
    )


def against(left, right):
    return lax.dot_general(
        left, right, (((1,), (1,)), ((), ())), preferred_element_type=jnp.float32
    )


def split_heads(joint_low):
    rows = joint_low.shape[0]
    width = joint_low.shape[1] // 3
    query = joint_low[:, :width].reshape(rows, HEADS, HEAD_SIZE)
    keys = joint_low[:, width : 2 * width].reshape(rows, HEADS, HEAD_SIZE)
    values = joint_low[:, 2 * width :].reshape(rows, HEADS, HEAD_SIZE)
    return (query, keys, values)


def block_scores(query_part, keys, label_part, labels):
    scores = jnp.einsum(
        "qhd,khd->hqk", query_part, keys, preferred_element_type=jnp.float32
    ) * HEAD_SIZE ** (-0.5)
    allowed = label_part[:, None] == labels[None, :]
    return jnp.where(allowed[None], scores, masked_score)


def attend_forward(joint_low, labels):
    query, keys, values = split_heads(joint_low)
    rows = query.shape[0]
    block = min(512, rows)

    def one_block(start):
        scores = block_scores(query, keys, labels, labels)
        peak = jnp.max(scores, axis=-1, keepdims=True)
        raised = jnp.exp(scores - peak)
        total = jnp.sum(raised, axis=-1, keepdims=True)
        probs_low = (raised / total).astype(jnp.bfloat16)
        mixed = jnp.einsum("hqk,khd->qhd", probs_low, values, preferred_element_type=jnp.float32)
        return (mixed.reshape(block, HEADS * HEAD_SIZE), (peak + jnp.log(total))[..., 0])

    starts = jnp.arange(rows // block, dtype=jnp.int32) * block
    mixed, log_totals = lax.map(one_block, starts)
    return (mixed.reshape(rows, HEADS * HEAD_SIZE), log_totals)


def attend_backward(joint_low, labels, log_totals, mixed_back):
    query, keys, values = split_heads(joint_low)
    rows = query.shape[0]
    block = min(512, rows)
    back_heads = mixed_back.reshape(rows, HEADS, HEAD_SIZE)
    factor = HEAD_SIZE ** (-0.5)

    def one_block(carry, items):
        key_sum, value_sum = carry
        start, log_part = items
        scores = block_scores(query, keys, labels, labels)
        probs = jnp.exp(scores - log_part[..., None])
        probs_low = probs.astype(jnp.bfloat16)
        prob_back = jnp.einsum(
            "qhd,khd->hqk", back_heads, values, preferred_element_type=jnp.float32
        )
        inner = jnp.sum(prob_back * probs, axis=-1, keepdims=True)
        score_back = (probs * (prob_back - inner)).astype(jnp.bfloat16)
        query_back = (
            jnp.einsum("hqk,khd->qhd", score_back, keys, preferred_element_type=jnp.float32)
            * factor
        )
        key_sum = (
            key_sum
            + jnp.einsum("hqk,qhd->khd", score_back, query, preferred_element_type=jnp.float32)
            * factor
        )
        value_sum = value_sum + jnp.einsum(
            "hqk,qhd->khd", probs_low, back_heads, preferred_element_type=jnp.float32
        )
        return ((key_sum, value_sum), query_back.reshape(block, HEADS * HEAD_SIZE))

    starts = jnp.arange(rows // block, dtype=jnp.int32) * block
    empty = jnp.zeros((rows, HEADS, HEAD_SIZE), jnp.float32)
    (key_sum, value_sum), query_back = lax.scan(one_block, (empty, empty), (starts, log_totals))
    width = HEADS * HEAD_SIZE
    return jnp.concatenate(
        [
            query_back.reshape(rows, width),
            key_sum.reshape(rows, width),
            value_sum.reshape(rows, width),
        ],
        axis=1,
    )


def layer_forward(inputs, labels, params):
    (
        joint_weight,
        output_weight,
        up_weight,
        down_weight,
        width_bias,
        hidden_bias,
        norm_gain,
        norm_shift,
    ) = params
    width = inputs.shape[1]
    joint_bias = jnp.concatenate([width_bias[0], jnp.zeros((width,), jnp.float32), width_bias[1]])
    joint_low = (
        jnp.dot(inputs, joint_weight, preferred_element_type=jnp.float32) + joint_bias
    ).astype(jnp.bfloat16)
    mixed, log_totals = attend_forward(joint_low, labels)
    mixed_low = mixed.astype(jnp.bfloat16)
    first_sum = inputs.astype(jnp.float32) + (
        jnp.dot(mixed_low, output_weight, preferred_element_type=jnp.float32) + width_bias[2]
    )
    hidden = layer_norm(first_sum, norm_gain[0], norm_shift[0])
    hidden_low = hidden.astype(jnp.bfloat16)
    up_value = jnp.dot(hidden_low, up_weight, preferred_element_type=jnp.float32) + hidden_bias
    active_low = exact_gelu(up_value).astype(jnp.bfloat16)
    second_sum = hidden + (
        jnp.dot(active_low, down_weight, preferred_element_type=jnp.float32) + width_bias[3]
    )
    result = layer_norm(second_sum, norm_gain[1], norm_shift[1])
    return (
        result,
        (joint_low, log_totals, mixed_low, first_sum, hidden_low, up_value, active_low, second_sum),
    )


def empty_kept(rows, width, hidden_width):
    block = min(512, rows)
    return (
        jnp.zeros((rows, 3 * width), jnp.bfloat16),
        jnp.zeros((rows // block, HEADS, block), jnp.float32),
        jnp.zeros((rows, width), jnp.bfloat16),
        jnp.zeros((rows, width), jnp.float32),
        jnp.zeros((rows, width), jnp.bfloat16),
        jnp.zeros((rows, hidden_width), jnp.float32),
        jnp.zeros((rows, hidden_width), jnp.bfloat16),
        jnp.zeros((rows, width), jnp.float32),
    )


def layer_backward(inputs, labels, params, kept, upstream):
    (
        joint_weight,
        output_weight,
        up_weight,
        down_weight,
        width_bias,
        hidden_bias,
        norm_gain,
        norm_shift,
    ) = params
    joint_low, log_totals, mixed_low, first_sum, hidden_low, up_value, active_low, second_sum = kept
    width = inputs.shape[1]
    second_norm, second_pull = jax.vjp(layer_norm, second_sum, norm_gain[1], norm_shift[1])
    second_back, second_gain, second_shift = second_pull(upstream)
    branch_back = second_back.astype(jnp.bfloat16)
    down_part = over_rows(active_low, branch_back)
    down_bias = jnp.sum(branch_back.astype(jnp.float32), axis=0)
    active_back = against(branch_back, down_weight)
    gelu_value, gelu_pull = jax.vjp(exact_gelu, up_value)
    up_back = gelu_pull(active_back)[0].astype(jnp.bfloat16)
    up_part = over_rows(hidden_low, up_back)
    up_bias = jnp.sum(up_back.astype(jnp.float32), axis=0)
    hidden_back = second_back + against(up_back, up_weight)
    first_norm, first_pull = jax.vjp(layer_norm, first_sum, norm_gain[0], norm_shift[0])
    first_back, first_gain, first_shift = first_pull(hidden_back)
    attention_back = first_back.astype(jnp.bfloat16)
    output_part = over_rows(mixed_low, attention_back)
    output_bias = jnp.sum(attention_back.astype(jnp.float32), axis=0)
    mixed_back = against(attention_back, output_weight).astype(jnp.bfloat16)
    joint_back = attend_backward(joint_low, labels, log_totals, mixed_back).astype(jnp.bfloat16)
    joint_part = over_rows(inputs, joint_back)
    joint_bias = jnp.sum(joint_back.astype(jnp.float32), axis=0)
    passed = first_back + against(joint_back, joint_weight)
    width_part = jnp.stack([joint_bias[:width], joint_bias[2 * width :], output_bias, down_bias])
    gain_part = jnp.stack([first_gain, second_gain])
    shift_part = jnp.stack([first_shift, second_shift])
    return (
        passed,
        (joint_part, output_part, up_part, down_part, width_part, up_bias, gain_part, shift_part),
    )


def on_device_general(
    frames,
    cotangent,
    segments,
    layer_keep,
    joint_weight,
    output_weight,
    up_weight,
    down_weight,
    width_bias,
    hidden_bias,
    norm_gain,
    norm_shift,
):
    params = tuple(
        (
            array[0]
            for array in (
                joint_weight,
                output_weight,
                up_weight,
                down_weight,
                width_bias,
                hidden_bias,
                norm_gain,
                norm_shift,
            )
        )
    )
    section = lax.axis_index(SECTION_AXIS)
    rows = BATCH_ROWS
    number = BATCHES
    width = frames.shape[1]
    hidden_width = up_weight.shape[2]
    layer_out = jnp.zeros(frames.shape, jnp.bfloat16)
    stored = []
    previous = jnp.zeros((rows, width), jnp.bfloat16)
    for step in range(number + 1):
        arrived = shifted(previous, SECTION_AXIS, 1) if step > 0 else previous
        batch = step - section
        within = (batch >= 0) & (batch < number)
        place = jnp.clip(batch, 0, number - 1)
        start = place * rows
        inputs = jnp.where(section == 0, lax.dynamic_slice_in_dim(frames, start, rows, 0), arrived)
        labels = lax.dynamic_slice_in_dim(segments, start, rows, 0)
        valid = (labels >= 0).astype(jnp.float32)[:, None]
        flag = lax.dynamic_slice_in_dim(layer_keep[0], place, 1, 0)[0]
        running = within & (flag == 1)
        result, kept = lax.cond(
            running,
            lambda: layer_forward(inputs, labels, params),
            lambda: (inputs.astype(jnp.float32), empty_kept(rows, width, hidden_width)),
        )
        output = (valid * result).astype(jnp.bfloat16)
        earlier = lax.dynamic_slice_in_dim(layer_out, start, rows, 0)
        layer_out = lax.dynamic_update_slice_in_dim(
            layer_out, jnp.where(within, output, earlier), start, 0
        )
        previous = output
        stored.append((inputs, labels, running, start, within, kept))
    input_back = jnp.zeros(frames.shape, jnp.float32)
    totals = None
    sending = jnp.zeros((rows, width), jnp.float32)
    for step in range(number + 1):
        arrived = (
            shifted(sending.astype(jnp.bfloat16), SECTION_AXIS, -1).astype(sending.dtype)
            if step > 0
            else sending
        )
        entry = stored[number - step]
        inputs, labels, running, start, within = (entry[0], entry[1], entry[2], entry[3], entry[4])
        valid = (labels >= 0).astype(jnp.float32)[:, None]
        given = lax.dynamic_slice_in_dim(cotangent, start, rows, 0).astype(jnp.float32)
        upstream = valid * jnp.where(section == 1, given, arrived)

        def run_back():
            kept = entry[5]
            return layer_backward(inputs, labels, params, kept, upstream)

        def skip_back():
            return (upstream, tuple((jnp.zeros(item.shape, jnp.float32) for item in params)))

        passed, pieces = lax.cond(running, run_back, skip_back)
        earlier = lax.dynamic_slice_in_dim(input_back, start, rows, 0)
        input_back = lax.dynamic_update_slice_in_dim(
            input_back, jnp.where(within, passed, earlier), start, 0
        )
        sending = passed
        shares = pieces
        totals = (
            tuple(shares)
            if totals is None
            else tuple((left + right for left, right in zip(totals, shares)))
        )
    shares = (
        lax.psum_scatter(
            totals[0][None].astype(jnp.bfloat16), SHARD_AXIS, scatter_dimension=1, tiled=True
        ).astype(jnp.float32),
        lax.psum_scatter(
            totals[1][None].astype(jnp.bfloat16), SHARD_AXIS, scatter_dimension=1, tiled=True
        ).astype(jnp.float32),
        lax.psum_scatter(
            totals[2][None].astype(jnp.bfloat16), SHARD_AXIS, scatter_dimension=1, tiled=True
        ).astype(jnp.float32),
        lax.psum_scatter(
            totals[3][None].astype(jnp.bfloat16), SHARD_AXIS, scatter_dimension=2, tiled=True
        ).astype(jnp.float32),
        lax.psum_scatter(
            totals[4][None].astype(jnp.bfloat16), SHARD_AXIS, scatter_dimension=2, tiled=True
        ).astype(jnp.float32),
        lax.psum_scatter(
            totals[5][None].astype(jnp.bfloat16), SHARD_AXIS, scatter_dimension=1, tiled=True
        ).astype(jnp.float32),
        lax.psum_scatter(
            totals[6][None].astype(jnp.bfloat16), SHARD_AXIS, scatter_dimension=2, tiled=True
        ).astype(jnp.float32),
        lax.psum_scatter(
            totals[7][None].astype(jnp.bfloat16), SHARD_AXIS, scatter_dimension=2, tiled=True
        ).astype(jnp.float32),
    )
    reduced = (
        lax.psum(shares[0].astype(jnp.bfloat16), REPLICA_AXIS).astype(jnp.float32),
        lax.psum(shares[1].astype(jnp.bfloat16), REPLICA_AXIS).astype(jnp.float32),
        lax.psum(shares[2].astype(jnp.bfloat16), REPLICA_AXIS).astype(jnp.float32),
        lax.psum(shares[3].astype(jnp.bfloat16), REPLICA_AXIS).astype(jnp.float32),
        lax.psum(shares[4].astype(jnp.bfloat16), REPLICA_AXIS).astype(jnp.float32),
        lax.psum(shares[5].astype(jnp.bfloat16), REPLICA_AXIS).astype(jnp.float32),
        lax.psum(shares[6].astype(jnp.bfloat16), REPLICA_AXIS).astype(jnp.float32),
        lax.psum(shares[7].astype(jnp.bfloat16), REPLICA_AXIS).astype(jnp.float32),
    )
    return (
        layer_out[None],
        input_back[None],
        reduced[0],
        reduced[1],
        reduced[2],
        reduced[3],
        reduced[4],
        reduced[5],
        reduced[6],
        reduced[7],
    )


F32, BF16 = jnp.float32, jnp.bfloat16
MESH = pl.DeviceIdType.MESH
D, FF, ROWS, PAIRS = 768, 3072, 512, 6
SHARE = D // 4
TILE = 256
FIRST_TILE = {DOWN: 0, "up": 12, "o": 24, QKV: 27}
TILES = {DOWN: 12, "up": 12, "o": 3, QKV: 9}
LAYER_TILES = 36
LAYER_CHUNKS = LAYER_TILES // 2
CHUNKS = 2 * LAYER_CHUNKS
LAST_STAGE = 9
WEIGHTS = (QKV, "o", "up", DOWN)
WEIGHT_SHAPE = {QKV: (D, 3 * D), "o": (D, D), "up": (D, FF), DOWN: (FF, D)}
SAVED = {
    QKV: ((ROWS, 3 * D), BF16),
    "mixed": ((ROWS, D), BF16),
    "aug": ((PAIRS, ROWS, 128), BF16),
    "n1": ((ROWS, D), F32),
    "scales": ((2, ROWS, 128), F32),
    "hid": ((ROWS, D), BF16),
    "act": ((ROWS, FF), BF16),
    "slope": ((ROWS, FF), BF16),
    "n2": ((ROWS, D), F32),
}
TEMPORARY = {
    "big": ((ROWS, D), F32),
    "low": ((ROWS, D), BF16),
    "left": ((D, ROWS), BF16),
    "mb": ((ROWS, D), BF16),
    "qb": ((ROWS, 3 * D), BF16),
}


def nn(a, b):
    return lax.dot_general(a, b, (((1,), (0,)), ((), ())), preferred_element_type=F32)


def nt(a, b):
    return lax.dot_general(a, b, (((1,), (1,)), ((), ())), preferred_element_type=F32)


def tn(a, b):
    return lax.dot_general(a, b, (((0,), (0,)), ((), ())), preferred_element_type=F32)


def half_lanes():
    return lax.broadcasted_iota(jnp.int32, (ROWS, 128), 1) < 64


def lane_place():
    return lax.broadcasted_iota(jnp.int32, (ROWS, 128), 1) % 64


def label_columns(row):
    return jnp.transpose(jnp.broadcast_to(row, (128, ROWS)))


def mask_columns(label):
    place = lane_place()
    mine = place.astype(F32) == label + 1.0
    within = place < 17
    query = jnp.where(mine & within, 1.0, 0.0)
    keys = jnp.where(within & jnp.logical_not(mine), -1e30, 0.0)
    ones = jnp.where((place >= 20) & (place < 23), 1.0, 0.0)
    return query, keys + ones, ones


def three_parts(column, base):
    place = lane_place()
    first = column.astype(BF16).astype(F32)
    rest = column - first
    second = rest.astype(BF16).astype(F32)
    third = rest - second
    out = jnp.where(place == 20, first, base)
    out = jnp.where(place == 21, second, out)
    return jnp.where(place == 22, third, out)


def norm(total):
    mean = jnp.mean(total, axis=1, keepdims=True)
    centre = total - mean
    spread = jnp.mean(centre * centre, axis=1, keepdims=True)
    scale = lax.rsqrt(spread + 1e-05)
    return centre * scale, scale


def norm_back(upstream, normed, scale, gain):
    e = upstream * gain
    first = jnp.mean(e, axis=1, keepdims=True)
    second = jnp.mean(e * normed, axis=1, keepdims=True)
    return scale * (e - first - normed * second)


def gelu_both(v):
    cdf = 0.5 * (1.0 + lax.erf(v * 0.7071067811865476))
    return v * cdf, cdf + v * (jnp.exp(-0.5 * v * v) * 0.3989422804014327)


def column_sum(value):
    return jnp.sum(value, axis=0, keepdims=True)


def times(start, stop, body):
    lax.fori_loop(start, stop, lambda i, _: (body(i), 0)[1], 0)


def forward(x, label, w, sm, out, hook):
    hook("start")
    for part in range(3):

        def tile(j, part=part):
            at = pl.multiple_of(j * TILE, TILE)
            cols = pl.ds(pl.multiple_of(part * D + j * TILE, TILE), TILE)
            acc = nn(x[...], w[QKV][:, cols])
            if part == 0:
                acc = (acc + sm[0:1, pl.ds(at, TILE)]).astype(BF16) * jnp.bfloat16(0.125)
            elif part == 2:
                acc = (acc + sm[1:2, pl.ds(at, TILE)]).astype(BF16)
            else:
                acc = acc.astype(BF16)
            out[QKV][:, cols] = acc

        times(0, 3, tile)
    hook(QKV)
    aq, ak, _ = mask_columns(label)
    aq16, ak16 = aq.astype(BF16), ak.astype(BF16)
    low = half_lanes()

    def pair(p):
        at = pl.multiple_of(p * 128, 128)
        qp = out[QKV][:, pl.ds(at, 128)]
        kp = out[QKV][:, pl.ds(D + at, 128)]
        vp = out[QKV][:, pl.ds(2 * D + at, 128)]
        res, lse = [], []
        for e in range(2):
            mask = low if e == 0 else jnp.logical_not(low)
            scores = nt(jnp.where(mask, qp, aq16), jnp.where(mask, kp, ak16))
            top = jnp.max(scores, axis=1, keepdims=True)
            raised = jnp.exp(scores - top).astype(BF16)
            o = nn(raised, jnp.where(mask, vp, jnp.bfloat16(1.0)))
            total = o[:, 64:65] if e == 0 else o[:, 0:1]
            res.append(o * (1.0 / total))
            lse.append(-(top + jnp.log(total)))
        out["mixed"][:, pl.ds(at, 128)] = jnp.where(low, res[0], res[1]).astype(BF16)
        out["aug"][p] = three_parts(jnp.where(low, lse[1], lse[0]), aq).astype(BF16)

    times(0, PAIRS, pair)
    hook("attention")
    first = x[...].astype(F32) + nn(out["mixed"][...], w["o"][...]) + sm[2:3, :]
    n1, r1 = norm(first)
    out["n1"][...] = n1
    out["scales"][0] = jnp.broadcast_to(r1, (ROWS, 128))
    out["hid"][...] = (n1 * sm[8:9, :] + sm[10:11, :]).astype(BF16)
    hook("first")

    def up_tile(j):
        cols = pl.ds(pl.multiple_of(j * D, TILE), D)
        v = nn(out["hid"][...], w["up"][:, cols]) + sm[pl.ds(4 + j, 1), :]
        act, slope = gelu_both(v)
        out["act"][:, cols] = act.astype(BF16)
        out["slope"][:, cols] = slope.astype(BF16)

    times(0, 4, up_tile)
    hook("up")
    hidden = out["n1"][...] * sm[8:9, :] + sm[10:11, :]
    second = hidden + nn(out["act"][...], w[DOWN][...]) + sm[3:4, :]
    n2, r2 = norm(second)
    out["n2"][...] = n2
    out["scales"][1] = jnp.broadcast_to(r2, (ROWS, 128))
    hook("second")
    return n2 * sm[9:10, :] + sm[11:12, :]


def backward(upstream, label, w, sm, s, x, t, sums, grad, tick, wait, done, last):
    wait("n2")
    wait("scales")
    u = upstream()
    n2 = s["n2"][...]
    back = norm_back(u, n2, s["scales"][1][:, 0:1], sm[9:10, :])
    sums[9:10, :] = column_sum(u * n2)
    sums[11:12, :] = column_sum(u)
    t["big"][...] = back
    low16 = back.astype(BF16)
    t["low"][...] = low16
    sums[3:4, :] = column_sum(low16.astype(F32))
    t["left"][...] = jnp.transpose(low16)
    done("n2")
    wait("act")
    grad(DOWN, t["left"], s["act"])
    done("act")
    tick("down_end")
    wait(DOWN)
    wait("slope")

    def up_tile(j):
        cols = pl.ds(pl.multiple_of(j * D, TILE), D)
        ub = (nt(t["low"][...], w[DOWN][cols, :]) * s["slope"][:, cols].astype(F32)).astype(BF16)
        s["slope"][:, cols] = ub
        sums[pl.ds(4 + j, 1), :] = column_sum(ub.astype(F32))
        tick("up_tile", j)

    times(0, 4, up_tile)
    done(DOWN)
    wait("hid")
    t["left"][...] = jnp.transpose(s["hid"][...])
    done("hid")
    grad("up", t["left"], s["slope"])
    wait("up")
    hb = t["big"][...] + nt(s["slope"][...], w["up"][...])
    done("up")
    done("slope")
    wait("n1")
    n1 = s["n1"][...]
    sums[8:9, :] = column_sum(hb * n1)
    sums[10:11, :] = column_sum(hb)
    fb = norm_back(hb, n1, s["scales"][0][:, 0:1], sm[8:9, :])
    t["big"][...] = fb
    low16 = fb.astype(BF16)
    t["low"][...] = low16
    sums[2:3, :] = column_sum(low16.astype(F32))
    done("n1")
    done("scales")
    tick("hidden")
    wait("mixed")
    t["left"][...] = jnp.transpose(s["mixed"][...])
    grad("o", t["left"], t["low"])
    wait("o")
    t["mb"][...] = nt(t["low"][...], w["o"][...]).astype(BF16)
    done("o")
    tick("mixed")
    _, ak, av = mask_columns(label)
    ak16, av16 = ak.astype(BF16), av.astype(BF16)
    low = half_lanes()
    wait("saved_qkv")
    wait("aug")

    def pair(p):
        at = pl.multiple_of(p * 128, 128)
        qp = s[QKV][:, pl.ds(at, 128)]
        kp = s[QKV][:, pl.ds(D + at, 128)]
        vp = s[QKV][:, pl.ds(2 * D + at, 128)]
        dp = t["mb"][:, pl.ds(at, 128)]
        aq16 = s["aug"][p]
        product = dp.astype(F32) * s["mixed"][:, pl.ds(at, 128)].astype(F32)
        even = -jnp.sum(jnp.where(low, product, 0.0), axis=1, keepdims=True)
        odd = -jnp.sum(jnp.where(low, 0.0, product), axis=1, keepdims=True)
        ad16 = three_parts(jnp.where(low, odd, even), jnp.zeros((ROWS, 128), F32)).astype(BF16)
        parts = []
        for e in range(2):
            mask = low if e == 0 else jnp.logical_not(low)
            probs = jnp.exp(nt(jnp.where(mask, kp, ak16), jnp.where(mask, qp, aq16)))
            pb = nt(jnp.where(mask, vp, av16), jnp.where(mask, dp, ad16))
            sb = (probs * pb).astype(BF16)
            parts.append((tn(sb, kp) * 0.125, nn(sb, qp), nn(probs.astype(BF16), dp)))
        for k in range(3):
            t["qb"][:, pl.ds(k * D + at, 128)] = jnp.where(low, parts[0][k], parts[1][k]).astype(BF16)
        tick("pair", p)

    times(0, PAIRS, pair)
    done("saved_qkv")
    done("aug")
    done("mixed")
    sums[0:1, :] = column_sum(t["qb"][:, 0:D].astype(F32))
    sums[1:2, :] = column_sum(t["qb"][:, 2 * D :].astype(F32))
    t["left"][...] = jnp.transpose(x[...])
    grad(QKV, t["left"], t["qb"])
    tick("joint")
    wait(QKV)
    last(t["big"][...] + nt(t["qb"][...], w[QKV][...]))
    done(QKV)
    tick("end")


def whole_step(*refs):
    it = iter(refs)
    take = lambda n: [next(it) for _ in range(n)]
    frames, cotangent, segments, small_in = take(4)
    weight_in = dict(zip(WEIGHTS, take(4)))
    layer_out, input_back, shares, small_out = take(4)
    weight_far = dict(zip(WEIGHTS, take(4)))
    made, given = take(2)
    spill = dict(zip(SAVED, take(len(SAVED))))
    w = dict(zip(WEIGHTS, take(4)))
    s = dict(zip(SAVED, take(len(SAVED))))
    t = dict(zip(TEMPORARY, take(len(TEMPORARY))))
    x0, x1, x2, cot, dx1, small, sums, stage = take(8)
    ra, rb, sbuf, kbuf, r1, zbuf, zr1, part, zs2, zr2, ybuf, r3, fbuf, sb, sr = take(15)
    (
        load_sem, spill_sem, in_sem, out_sem, out_recv, w_send, w_recv, small_sem,
        made_sem, give_send, give_recv, ra_sem, rb_sem, s1_send, s1_recv, z1_send, z1_recv,
        z2_send, z2_recv, s3_send, s3_recv, push_send, push_recv, sum_send, sum_recv, back_sem, back_recv,
    ) = take(27)

    me = lax.axis_index(SECTION_AXIS)
    z = lax.axis_index(SHARD_AXIS)
    r = lax.axis_index(REPLICA_AXIS)
    other = 1 - me
    x_at, y_at = lax.rem(r, 2), lax.div(r, 2)
    x_near, y_near = r + 1 - 2 * x_at, r + 2 - 4 * y_at
    half = (1 - me) * x_at + me * y_at
    first_near = (1 - me) * x_near + me * y_near
    second_near = (1 - me) * y_near + me * x_near
    is_end = lax.rem(z, 3) == 0
    is_middle = jnp.logical_not(is_end)
    partner = (other, z, r)

    def local(src, dst, sem):
        return pltpu.make_async_copy(src, dst, sem)

    def remote(src, dst, send, recv, device):
        return pltpu.make_async_remote_copy(
            src_ref=src, dst_ref=dst, send_sem=send, recv_sem=recv, device_id=device, device_id_type=MESH
        )

    own_rows = pl.ds(pl.multiple_of(me * ROWS, ROWS), ROWS)
    load_frames = local(frames.at[own_rows], x0, in_sem.at[0])
    load_cot = local(cotangent.at[own_rows], cot, in_sem.at[1])

    def weight_near(k):
        return local(weight_in[k].at[0], w[k], load_sem.at[WEIGHTS.index(k)])

    def weight_got(k):
        return local(weight_far[k], w[k], load_sem.at[WEIGHTS.index(k)])

    weight_send = {
        k: remote(weight_in[k].at[0], weight_far[k], w_send.at[i], w_recv.at[i], partner)
        for i, k in enumerate(WEIGHTS)
    }
    small_send = remote(small_in, small.at[me], small_sem.at[0], small_sem.at[1], partner)

    load_frames.start()
    load_cot.start()

    @pl.when(me == 0)
    def _():
        for k in WEIGHTS:
            weight_near(k).start()

    barrier = pltpu.get_barrier_semaphore()
    greeted = [partner, (me, z, x_near), (me, z, y_near), (other, z, x_near), (other, z, y_near)]
    for device in greeted:
        pl.semaphore_signal(barrier, inc=1, device_id=device, device_id_type=MESH)
    for step in (1, 2):

        @pl.when(z + step < 4)
        def _(step=step):
            pl.semaphore_signal(barrier, inc=1, device_id=(me, z + step, r), device_id_type=MESH)

        @pl.when(z >= step)
        def _(step=step):
            pl.semaphore_signal(barrier, inc=1, device_id=(me, z - step, r), device_id_type=MESH)

    pl.semaphore_wait(barrier, len(greeted) + 2 + lax.rem(lax.div(z + 1, 2), 2))

    small_send.start()
    for k in WEIGHTS:
        weight_send[k].start()
    small[me] = small_in[...]
    sums[...] = jnp.zeros_like(sums)

    label = label_columns(segments[pl.ds(me, 1), :].astype(F32))
    valid = jnp.where(label[:, 0:1] >= 0.0, 1.0, 0.0)

    def spilled(k):
        return local(s[k], spill[k], spill_sem.at[list(SAVED).index(k)])

    def saved_load(k):
        return local(spill[k], s[k], spill_sem.at[list(SAVED).index(k)])

    def got(k):
        @pl.when(me == 1)
        def _():
            weight_send[k].wait_recv()
            weight_got(k).start()

    def next_weight(k, arrived):
        @pl.when(me == 0)
        def _():
            if arrived:
                weight_send[k].wait_recv()
            weight_got(k).start()

        @pl.when(me == 1)
        def _():
            weight_near(k).start()

    def first_weight(k):
        @pl.when(me == 0)
        def _():
            weight_near(k).start()

        @pl.when(me == 1)
        def _():
            weight_got(k).start()

    def weight_wait(k):
        weight_near(k).wait()

    def hook0(point):
        if point == "start":
            got(QKV)
            load_frames.wait()
            small_send.wait()
            weight_wait(QKV)
        elif point == QKV:
            spilled(QKV).start()
            got("o")
        elif point == "attention":
            spilled("mixed").start()
            spilled("aug").start()
            got("up")
            next_weight(QKV, True)
            weight_wait("o")
        elif point == "first":
            spilled("n1").start()
            spilled("hid").start()
            next_weight("o", True)
            weight_wait("up")
        elif point == "up":
            spilled("act").start()
            spilled("slope").start()
            got(DOWN)
            weight_wait(DOWN)
        elif point == "second":
            spilled("n2").start()
            spilled("scales").start()

    def hook1(point):
        if point == "start":
            spilled(QKV).wait()
            weight_wait(QKV)
        elif point == QKV:
            spilled("mixed").wait()
            spilled("aug").wait()
            next_weight("up", True)
        elif point == "attention":
            spilled("n1").wait()
            spilled("hid").wait()
            spilled("scales").wait()
            next_weight(DOWN, True)
            weight_wait("o")
        elif point == "first":
            spilled("act").wait()
            spilled("slope").wait()
            weight_wait("up")
        elif point == "up":
            spilled("n2").wait()
            weight_wait(DOWN)

    def keep_of(layer):
        return jnp.where(me == 0, small[layer, 12:13, 0:1], small[layer, 13:14, 0:1])

    def out_copy(src, layer, buffer, send, recv, start):
        here = local(src, buffer.at[own_rows], send.at[layer])
        there = remote(src, buffer.at[own_rows], send.at[layer], recv, partner)

        @pl.when(me == layer)
        def _():
            here.start() if start else here.wait()

        @pl.when(me != layer)
        def _():
            there.start() if start else there.wait_send()

    def layer_result(result, x, layer):
        kept = jnp.where(keep_of(layer) > 0.5, result, x[...].astype(F32))
        return (valid * kept).astype(BF16)

    x1[...] = layer_result(forward(x0, label, w, small.at[0], s, hook0), x0, 0)
    out_copy(x1, 0, layer_out, out_sem, out_recv.at[0], True)
    x2[...] = layer_result(forward(x1, label, w, small.at[1], s, hook1), x1, 1)
    out_copy(x2, 1, layer_out, out_sem, out_recv.at[0], True)

    def send_tile(q, slot, start):
        chunk = lax.div(q, 2)
        mine = lax.rem(q, 2) == me
        keep_copy = local(stage.at[slot], made.at[chunk], made_sem.at[slot])
        give_copy = remote(stage.at[slot], given.at[chunk], give_send.at[slot], give_recv.at[chunk], partner)

        @pl.when(mine)
        def _():
            keep_copy.start() if start else keep_copy.wait()

        @pl.when(jnp.logical_not(mine))
        def _():
            give_copy.start() if start else give_copy.wait_send()

    def load_own(c):
        return local(made.at[c], ra.at[lax.rem(c, 2)], ra_sem.at[lax.rem(c, 2)])

    def load_given(c):
        return local(given.at[c], rb.at[lax.rem(c, 2)], rb_sem.at[lax.rem(c, 2)])

    def copy_first(c):
        a, b = lax.rem(c, 4), lax.rem(c, 6)
        return remote(sbuf.at[a], r1.at[b], s1_send.at[a], s1_recv.at[b], (me, z, first_near))

    def copy_end(c):
        a, b = lax.rem(c, 4), lax.rem(c, 6)
        rows = pl.ds(pl.multiple_of(SHARE - SHARE * lax.div(z, 3), SHARE), 3 * SHARE)
        return remote(zbuf.at[a, rows], zr1.at[b], z1_send.at[a], z1_recv.at[b], (me, 1 + lax.div(z, 3), r))

    def copy_middle(c):
        a, b = lax.rem(c, 4), lax.rem(c, 6)
        rows = pl.ds(pl.multiple_of(3 * SHARE * lax.div(z, 2), SHARE), SHARE)
        return remote(
            zbuf.at[a, rows], zr1.at[b, pl.ds(0, SHARE)], z1_send.at[a], z1_recv.at[b], (me, 3 * lax.div(z, 2), r)
        )

    def copy_across(c, which):
        a, b = lax.rem(c, 4), lax.rem(c, 8)
        far = 3 - z if which == 0 else 3 - 3 * lax.div(z, 2)
        return remote(zs2.at[a, which], zr2.at[b], z2_send.at[a, which], z2_recv.at[b], (me, far, r))

    def copy_second(c):
        a, b = lax.rem(c, 4), lax.rem(c, 6)
        return remote(ybuf.at[a], r3.at[b], s3_send.at[a], s3_recv.at[b], (me, z, second_near))

    def push(c, start):
        a = lax.rem(c, 4)
        layer = 1 - lax.div(c, LAYER_CHUNKS)
        place = lax.rem(c, LAYER_CHUNKS)
        cols = pl.ds(pl.multiple_of((2 * (2 * place + me) + half) * 128, 128), 128)
        here = local(fbuf.at[a], shares.at[:, cols], push_send.at[a, 0])
        beside = remote(fbuf.at[a], shares.at[:, cols], push_send.at[a, 0], push_recv.at[0, place], partner)
        near_same = remote(
            fbuf.at[a], shares.at[:, cols], push_send.at[a, 1], push_recv.at[1, place], (me, z, first_near)
        )
        near_other = remote(
            fbuf.at[a], shares.at[:, cols], push_send.at[a, 1], push_recv.at[2, place], (other, z, first_near)
        )

        @pl.when(layer == me)
        def _():
            here.start() if start else here.wait()
            near_same.start() if start else near_same.wait_send()

        @pl.when(layer != me)
        def _():
            beside.start() if start else beside.wait_send()
            near_other.start() if start else near_other.wait_send()

    def at_stage(c):
        return (c >= 0) & (c < CHUNKS)

    def comm(now):
        @pl.when(at_stage(now - 9))
        def _():
            c = now - 9
            a, b = lax.rem(c, 4), lax.rem(c, 6)
            copy_second(c).wait()

            @pl.when(c >= 4)
            def _():
                push(c - 4, False)

            fbuf[a] = (ybuf[a].astype(F32) + r3[b].astype(F32)).astype(BF16)
            push(c, True)

        @pl.when(at_stage(now - 7))
        def _():
            c = now - 7
            a, b = lax.rem(c, 4), lax.rem(c, 8)

            @pl.when(is_middle)
            def _():
                copy_across(c, 0).wait_send()
                copy_across(c, 1).wait_send()

            copy_across(c, 0).wait_recv()
            ybuf[a] = (part[a] + zr2[b].astype(F32)).astype(BF16)
            copy_second(c).start()

        @pl.when(at_stage(now - 5))
        def _():
            c = now - 5
            a, b = lax.rem(c, 4), lax.rem(c, 6)

            @pl.when(is_end)
            def _():
                copy_end(c).wait_send()
                copy_middle(c).wait_recv()
                own = pl.ds(pl.multiple_of(z * SHARE, SHARE), SHARE)
                part[a] = kbuf[b, own] + zr1[b, 0:SHARE].astype(F32)

            @pl.when(is_middle)
            def _():
                copy_middle(c).wait_send()
                copy_end(c).wait_recv()
                low_row = SHARE * (2 - z)

                def sum_of(row):
                    row = pl.multiple_of(row, SHARE)
                    return (
                        kbuf[b, pl.ds(pl.multiple_of(low_row + row, SHARE), SHARE)]
                        + zr1[b, pl.ds(row, SHARE)].astype(F32)
                    )

                zs2[a, 0] = sum_of(jnp.int32(SHARE)).astype(BF16)
                zs2[a, 1] = sum_of(2 * SHARE * (2 - z)).astype(BF16)
                copy_across(c, 0).start()
                copy_across(c, 1).start()
                part[a] = sum_of(2 * SHARE * (z - 1))

        @pl.when(at_stage(now - 3))
        def _():
            c = now - 3
            a, b = lax.rem(c, 4), lax.rem(c, 6)
            copy_first(c).wait()
            total = kbuf[b] + r1[b].astype(F32)
            kbuf[b] = total
            zbuf[a] = total.astype(BF16)

            @pl.when(is_end)
            def _():
                copy_end(c).start()

            @pl.when(is_middle)
            def _():
                copy_middle(c).start()

        @pl.when(at_stage(now - 1))
        def _():
            c = now - 1
            a, b, d = lax.rem(c, 4), lax.rem(c, 6), lax.rem(c, 2)
            load_own(c).wait()
            load_given(c).wait()
            sbuf[a] = (ra[d, 1 - half].astype(F32) + rb[d, 1 - half].astype(F32)).astype(BF16)
            copy_first(c).start()
            kbuf[b] = ra[d, half].astype(F32) + rb[d, half].astype(F32)

        @pl.when(at_stage(now))
        def _():
            remote(stage.at[0], given.at[now], give_send.at[0], give_recv.at[now], partner).wait_recv()
            load_own(now).start()
            load_given(now).start()

    def run_layer(layer, upstream, passed, x, base, ticks, wait, done):
        first_tile = 0 if layer == 1 else LAYER_TILES

        def grad(k, left, right):
            n = TILES[k]
            begin = first_tile + FIRST_TILE[k]
            marks = ticks.get(k, {})

            def tile(j):
                q = begin + j
                slot = lax.rem(q, 4)

                @pl.when(j >= 4)
                def _():
                    send_tile(q - 4, slot, False)

                cols = pl.ds(pl.multiple_of(j * TILE, TILE), TILE)
                g = nn(left[...], right[:, cols]).astype(BF16)
                stage[slot, 0] = g[:, :128]
                stage[slot, 1] = g[:, 128:]
                send_tile(q, slot, True)
                for at, number in marks.items():

                    @pl.when(j == at)
                    def _(number=number):
                        comm(jnp.int32(number))

            times(0, n, tile)
            times(max(n - 4, 0), n, lambda j: send_tile(begin + j, lax.rem(begin + j, 4), False))

        def tick(point, index=None):
            marks = ticks.get(point)
            if marks is None:
                return
            if index is None:
                comm(jnp.int32(marks))
            else:
                number, every = marks

                @pl.when(lax.rem(index, every) == every - 1)
                def _():
                    comm(number + lax.div(index, every))

        sm = small.at[layer]
        keep = keep_of(layer)

        def masked():
            return upstream[...].astype(F32) * (valid * keep)

        def last(value):
            passed[...] = value + upstream[...].astype(F32) * (valid * (1.0 - keep))

        backward(masked, label, w, sm, s, x, t, sums.at[layer], grad, tick, wait, done, last)

    def wait1(k):
        pass

    def done1(k):
        if k in WEIGHTS:
            first_weight(k)
        elif k == "saved_qkv":
            saved_load(QKV).start()
        else:
            saved_load(k).start()

    def wait0(k):
        if k in WEIGHTS:
            weight_wait(k)
        elif k == "saved_qkv":
            saved_load(QKV).wait()
        else:
            saved_load(k).wait()

    load_cot.wait()
    run_layer(1, cot, dx1, x1, 0, TICKS[0], wait1, done1)
    out_copy(dx1, 1, input_back, back_sem, back_recv.at[0], True)
    run_layer(0, dx1, s["n1"], x0, 0, TICKS[1], wait0, lambda k: None)
    out_copy(s["n1"], 0, input_back, back_sem, back_recv.at[0], True)

    def sum_copy(step):
        if step == 0:
            return remote(sums.at[other], sr.at[0], sum_send.at[0], sum_recv.at[0], partner)
        z_one = z + 1 - 2 * lax.rem(z, 2)
        z_two = lax.rem(z + 2, 4)
        device = [(me, z, x_near), (me, z, y_near), (me, z_one, r), (me, z_two, r)][step - 1]
        return remote(sb.at[step - 1], sr.at[step], sum_send.at[step], sum_recv.at[step], device)

    sum_copy(0).start()

    def final(now):
        for step in range(5):

            @pl.when(now == SUM_TICK + 2 * step)
            def _(step=step):
                sum_copy(step).wait()
                if step == 0:
                    sb[0] = sums[me] + sr[0]
                else:
                    sb[step] = sb[step - 1] + sr[step]
                if step < 4:
                    sum_copy(step + 1).start()

        comm(now)

    times(SUM_TICK, CHUNKS + LAST_STAGE, final)
    small_out[...] = sb[4]

    times(CHUNKS - 4, CHUNKS, lambda c: push(c, False))
    for stream in range(3):

        def arrived(place, stream=stream):
            remote(
                fbuf.at[0], shares.at[:, pl.ds(0, 128)], push_send.at[0, 0], push_recv.at[stream, place], partner
            ).wait_recv()

        times(0, LAYER_CHUNKS, arrived)
    for k in WEIGHTS:
        weight_send[k].wait_send()
    out_copy(x1, 0, layer_out, out_sem, out_recv.at[0], False)
    out_copy(x2, 1, layer_out, out_sem, out_recv.at[0], False)
    out_copy(dx1, 1, input_back, back_sem, back_recv.at[0], False)
    out_copy(s["n1"], 0, input_back, back_sem, back_recv.at[0], False)
    remote(x1, layer_out.at[own_rows], out_sem.at[0], out_recv.at[0], partner).wait_recv()
    remote(dx1, input_back.at[own_rows], back_sem.at[0], back_recv.at[0], partner).wait_recv()


TICKS = (
    {"down_end": 0, "up_tile": (1, 2), "up": {5: 3, 11: 4}, "hidden": 5, "mixed": 6, "pair": (7, 1), "joint": 13, "end": 14},
    {DOWN: {5: 15, 11: 16}, "up_tile": (17, 2), "up": {5: 19, 11: 20}, "hidden": 21, "mixed": 22, "pair": (23, 1)},
)
SUM_TICK = 29


def any_space():
    return pl.BlockSpec(memory_space=pl.ANY)


def in_vmem():
    return pl.BlockSpec(memory_space=pltpu.VMEM)


def run_whole(frames, cotangent, segments, small, weights):
    shape = jax.ShapeDtypeStruct
    outs = [
        shape((2 * ROWS, D), BF16),
        shape((2 * ROWS, D), F32),
        shape((SHARE, LAYER_TILES * TILE), BF16),
        shape((16, D), F32),
    ]
    outs += [shape(WEIGHT_SHAPE[k], BF16) for k in WEIGHTS]
    outs += [shape((CHUNKS, 2, D, 128), BF16)] * 2
    outs += [shape(*SAVED[k]) for k in SAVED]
    out_specs = [any_space()] * 3 + [in_vmem()] + [any_space()] * (len(outs) - 4)
    dma = pltpu.SemaphoreType.DMA
    scratch = [pltpu.VMEM(WEIGHT_SHAPE[k], BF16) for k in WEIGHTS]
    scratch += [pltpu.VMEM(*SAVED[k]) for k in SAVED]
    scratch += [pltpu.VMEM(*TEMPORARY[k]) for k in TEMPORARY]
    scratch += [pltpu.VMEM((ROWS, D), BF16)] * 4
    scratch += [
        pltpu.VMEM((ROWS, D), F32),
        pltpu.VMEM((2, 16, D), F32),
        pltpu.VMEM((2, 16, D), F32),
        pltpu.VMEM((4, 2, D, 128), BF16),
        pltpu.VMEM((2, 2, D, 128), BF16),
        pltpu.VMEM((2, 2, D, 128), BF16),
        pltpu.VMEM((4, D, 128), BF16),
        pltpu.VMEM((6, D, 128), F32),
        pltpu.VMEM((6, D, 128), BF16),
        pltpu.VMEM((4, D, 128), BF16),
        pltpu.VMEM((6, 3 * SHARE, 128), BF16),
        pltpu.VMEM((4, SHARE, 128), F32),
        pltpu.VMEM((4, 2, SHARE, 128), BF16),
        pltpu.VMEM((8, SHARE, 128), BF16),
        pltpu.VMEM((4, SHARE, 128), BF16),
        pltpu.VMEM((6, SHARE, 128), BF16),
        pltpu.VMEM((4, SHARE, 128), BF16),
        pltpu.VMEM((5, 16, D), F32),
        pltpu.VMEM((5, 16, D), F32),
    ]
    sems = [
        (4,), (len(SAVED),), (2,), (2,), (1,), (4,), (4,), (2,),
        (4,), (4,), (CHUNKS,), (2,), (2,), (4,), (6,), (4,), (6,),
        (4, 2), (8,), (4,), (6,), (4, 2), (3, LAYER_CHUNKS), (5,), (5,), (2,), (1,),
    ]
    scratch += [dma(n) for n in sems]
    got = pl.pallas_call(
        whole_step,
        out_shape=outs,
        in_specs=[any_space(), any_space(), in_vmem(), in_vmem()] + [any_space()] * 4,
        out_specs=out_specs,
        scratch_shapes=scratch,
        compiler_params=pltpu.CompilerParams(
            collective_id=0, has_side_effects=True, vmem_limit_bytes=64 * 2**20 - 2**17
        ),
        name="whole_step",
    )(frames, cotangent, segments, small, *weights)
    return got[:4]


def on_device_block(
    frames, cotangent, segments, layer_keep, joint_weight, output_weight, up_weight, down_weight,
    width_bias, hidden_bias, norm_gain, norm_shift,
):
    keep = jnp.broadcast_to(layer_keep.reshape(2, 1).astype(F32), (2, D))
    small = jnp.concatenate(
        [width_bias[0], hidden_bias.reshape(4, D), norm_gain[0], norm_shift[0], keep, jnp.zeros((2, D), F32)], axis=0
    )
    layer_out, input_back, shares, sums = run_whole(
        frames,
        cotangent,
        segments.reshape(2, ROWS),
        small,
        [joint_weight, output_weight, up_weight, down_weight],
    )
    shares = shares.astype(F32)
    at = {k: FIRST_TILE[k] * TILE for k in WEIGHTS}
    size = {k: TILES[k] * TILE for k in WEIGHTS}
    part = {k: shares[:, at[k] : at[k] + size[k]] for k in WEIGHTS}
    z = lax.axis_index(SHARD_AXIS)
    mine = lax.dynamic_slice_in_dim(sums, z * SHARE, SHARE, 1)
    hidden = lax.dynamic_slice_in_dim(sums, 4 + z, 1, 0)
    return (
        layer_out[None],
        input_back[None],
        part[QKV][None],
        part["o"][None],
        part["up"][None],
        part[DOWN].T[None],
        mine[None, 0:4],
        hidden,
        mine[None, 8:10],
        mine[None, 10:12],
    )


def solution(mesh):
    sizes = dict(mesh.shape)
    fits = sizes == {SECTION_AXIS: 2, SHARD_AXIS: 4, REPLICA_AXIS: 4}
    placed = (
        P((SHARD_AXIS, REPLICA_AXIS), None),
        P((SHARD_AXIS, REPLICA_AXIS), None),
        P((SHARD_AXIS, REPLICA_AXIS)),
        P(SECTION_AXIS, (SHARD_AXIS, REPLICA_AXIS)),
        P(SECTION_AXIS, None, None),
        P(SECTION_AXIS, None, None),
        P(SECTION_AXIS, None, None),
        P(SECTION_AXIS, None, None),
        P(SECTION_AXIS, None, None),
        P(SECTION_AXIS, None),
        P(SECTION_AXIS, None, None),
        P(SECTION_AXIS, None, None),
    )
    return jax.shard_map(
        on_device_block if fits else on_device_general,
        mesh=mesh,
        in_specs=placed,
        out_specs=(
            P(SECTION_AXIS, (SHARD_AXIS, REPLICA_AXIS), None),
            P(SECTION_AXIS, (SHARD_AXIS, REPLICA_AXIS), None),
            P(SECTION_AXIS, SHARD_AXIS, None),
            P(SECTION_AXIS, SHARD_AXIS, None),
            P(SECTION_AXIS, SHARD_AXIS, None),
            P(SECTION_AXIS, None, SHARD_AXIS),
            P(SECTION_AXIS, None, SHARD_AXIS),
            P(SECTION_AXIS, SHARD_AXIS),
            P(SECTION_AXIS, None, SHARD_AXIS),
            P(SECTION_AXIS, None, SHARD_AXIS),
        ),
        check_vma=False,
    )
```

```python
import functools

import jax
import jax.numpy as jnp
from jax import lax
from jax.experimental import pallas as pl
from jax.experimental.pallas import tpu as pltpu
from jax.sharding import PartitionSpec as P

SECTION_AXIS, SHARD_AXIS, REPLICA_AXIS = "section", "shard", "replica"
QKV, DOWN = "qkv", "down"

HEADS = 12
HEAD_SIZE = 64
BATCH_ROWS = 512
BATCHES = 2


epsilon = 1e-05
masked_score = -1e30


def shifted(block, axis, distance):
    devices = range(lax.axis_size(axis))
    route = [(i - distance, i) for i in devices if i - distance in devices]
    return lax.ppermute(block, axis, route)


def layer_norm(value, gain, shift):
    centre = value - jnp.mean(value, axis=-1, keepdims=True)
    spread = jnp.mean(centre * centre, axis=-1, keepdims=True)
    return centre * lax.rsqrt(spread + epsilon) * gain + shift


def exact_gelu(value):
    return jax.nn.gelu(value, approximate=False)


def over_rows(left, right):
    return lax.dot_general(
        left, right, (((0,), (0,)), ((), ())), preferred_element_type=jnp.float32
    )


def against(left, right):
    return lax.dot_general(
        left, right, (((1,), (1,)), ((), ())), preferred_element_type=jnp.float32
    )


def split_heads(joint_low):
    rows = joint_low.shape[0]
    width = joint_low.shape[1] // 3
    query = joint_low[:, :width].reshape(rows, HEADS, HEAD_SIZE)
    keys = joint_low[:, width : 2 * width].reshape(rows, HEADS, HEAD_SIZE)
    values = joint_low[:, 2 * width :].reshape(rows, HEADS, HEAD_SIZE)
    return (query, keys, values)


def block_scores(query_part, keys, label_part, labels):
    scores = jnp.einsum(
        "qhd,khd->hqk", query_part, keys, preferred_element_type=jnp.float32
    ) * HEAD_SIZE ** (-0.5)
    allowed = label_part[:, None] == labels[None, :]
    return jnp.where(allowed[None], scores, masked_score)


def attend_forward(joint_low, labels):
    query, keys, values = split_heads(joint_low)
    rows = query.shape[0]
    block = min(512, rows)

    def one_block(start):
        scores = block_scores(query, keys, labels, labels)
        peak = jnp.max(scores, axis=-1, keepdims=True)
        raised = jnp.exp(scores - peak)
        total = jnp.sum(raised, axis=-1, keepdims=True)
        probs_low = (raised / total).astype(jnp.bfloat16)
        mixed = jnp.einsum("hqk,khd->qhd", probs_low, values, preferred_element_type=jnp.float32)
        return (mixed.reshape(block, HEADS * HEAD_SIZE), (peak + jnp.log(total))[..., 0])

    starts = jnp.arange(rows // block, dtype=jnp.int32) * block
    mixed, log_totals = lax.map(one_block, starts)
    return (mixed.reshape(rows, HEADS * HEAD_SIZE), log_totals)


def attend_backward(joint_low, labels, log_totals, mixed_back):
    query, keys, values = split_heads(joint_low)
    rows = query.shape[0]
    block = min(512, rows)
    back_heads = mixed_back.reshape(rows, HEADS, HEAD_SIZE)
    factor = HEAD_SIZE ** (-0.5)

    def one_block(carry, items):
        key_sum, value_sum = carry
        start, log_part = items
        scores = block_scores(query, keys, labels, labels)
        probs = jnp.exp(scores - log_part[..., None])
        probs_low = probs.astype(jnp.bfloat16)
        prob_back = jnp.einsum(
            "qhd,khd->hqk", back_heads, values, preferred_element_type=jnp.float32
        )
        inner = jnp.sum(prob_back * probs, axis=-1, keepdims=True)
        score_back = (probs * (prob_back - inner)).astype(jnp.bfloat16)
        query_back = (
            jnp.einsum("hqk,khd->qhd", score_back, keys, preferred_element_type=jnp.float32)
            * factor
        )
        key_sum = (
            key_sum
            + jnp.einsum("hqk,qhd->khd", score_back, query, preferred_element_type=jnp.float32)
            * factor
        )
        value_sum = value_sum + jnp.einsum(
            "hqk,qhd->khd", probs_low, back_heads, preferred_element_type=jnp.float32
        )
        return ((key_sum, value_sum), query_back.reshape(block, HEADS * HEAD_SIZE))

    starts = jnp.arange(rows // block, dtype=jnp.int32) * block
    empty = jnp.zeros((rows, HEADS, HEAD_SIZE), jnp.float32)
    (key_sum, value_sum), query_back = lax.scan(one_block, (empty, empty), (starts, log_totals))
    width = HEADS * HEAD_SIZE
    return jnp.concatenate(
        [
            query_back.reshape(rows, width),
            key_sum.reshape(rows, width),
            value_sum.reshape(rows, width),
        ],
        axis=1,
    )


def layer_forward(inputs, labels, params):
    (
        joint_weight,
        output_weight,
        up_weight,
        down_weight,
        width_bias,
        hidden_bias,
        norm_gain,
        norm_shift,
    ) = params
    width = inputs.shape[1]
    joint_bias = jnp.concatenate([width_bias[0], jnp.zeros((width,), jnp.float32), width_bias[1]])
    joint_low = (
        jnp.dot(inputs, joint_weight, preferred_element_type=jnp.float32) + joint_bias
    ).astype(jnp.bfloat16)
    mixed, log_totals = attend_forward(joint_low, labels)
    mixed_low = mixed.astype(jnp.bfloat16)
    first_sum = inputs.astype(jnp.float32) + (
        jnp.dot(mixed_low, output_weight, preferred_element_type=jnp.float32) + width_bias[2]
    )
    hidden = layer_norm(first_sum, norm_gain[0], norm_shift[0])
    hidden_low = hidden.astype(jnp.bfloat16)
    up_value = jnp.dot(hidden_low, up_weight, preferred_element_type=jnp.float32) + hidden_bias
    active_low = exact_gelu(up_value).astype(jnp.bfloat16)
    second_sum = hidden + (
        jnp.dot(active_low, down_weight, preferred_element_type=jnp.float32) + width_bias[3]
    )
    result = layer_norm(second_sum, norm_gain[1], norm_shift[1])
    return (
        result,
        (joint_low, log_totals, mixed_low, first_sum, hidden_low, up_value, active_low, second_sum),
    )


def empty_kept(rows, width, hidden_width):
    block = min(512, rows)
    return (
        jnp.zeros((rows, 3 * width), jnp.bfloat16),
        jnp.zeros((rows // block, HEADS, block), jnp.float32),
        jnp.zeros((rows, width), jnp.bfloat16),
        jnp.zeros((rows, width), jnp.float32),
        jnp.zeros((rows, width), jnp.bfloat16),
        jnp.zeros((rows, hidden_width), jnp.float32),
        jnp.zeros((rows, hidden_width), jnp.bfloat16),
        jnp.zeros((rows, width), jnp.float32),
    )


def layer_backward(inputs, labels, params, kept, upstream):
    (
        joint_weight,
        output_weight,
        up_weight,
        down_weight,
        width_bias,
        hidden_bias,
        norm_gain,
        norm_shift,
    ) = params
    joint_low, log_totals, mixed_low, first_sum, hidden_low, up_value, active_low, second_sum = kept
    width = inputs.shape[1]
    second_norm, second_pull = jax.vjp(layer_norm, second_sum, norm_gain[1], norm_shift[1])
    second_back, second_gain, second_shift = second_pull(upstream)
    branch_back = second_back.astype(jnp.bfloat16)
    down_part = over_rows(active_low, branch_back)
    down_bias = jnp.sum(branch_back.astype(jnp.float32), axis=0)
    active_back = against(branch_back, down_weight)
    gelu_value, gelu_pull = jax.vjp(exact_gelu, up_value)
    up_back = gelu_pull(active_back)[0].astype(jnp.bfloat16)
    up_part = over_rows(hidden_low, up_back)
    up_bias = jnp.sum(up_back.astype(jnp.float32), axis=0)
    hidden_back = second_back + against(up_back, up_weight)
    first_norm, first_pull = jax.vjp(layer_norm, first_sum, norm_gain[0], norm_shift[0])
    first_back, first_gain, first_shift = first_pull(hidden_back)
    attention_back = first_back.astype(jnp.bfloat16)
    output_part = over_rows(mixed_low, attention_back)
    output_bias = jnp.sum(attention_back.astype(jnp.float32), axis=0)
    mixed_back = against(attention_back, output_weight).astype(jnp.bfloat16)
    joint_back = attend_backward(joint_low, labels, log_totals, mixed_back).astype(jnp.bfloat16)
    joint_part = over_rows(inputs, joint_back)
    joint_bias = jnp.sum(joint_back.astype(jnp.float32), axis=0)
    passed = first_back + against(joint_back, joint_weight)
    width_part = jnp.stack([joint_bias[:width], joint_bias[2 * width :], output_bias, down_bias])
    gain_part = jnp.stack([first_gain, second_gain])
    shift_part = jnp.stack([first_shift, second_shift])
    return (
        passed,
        (joint_part, output_part, up_part, down_part, width_part, up_bias, gain_part, shift_part),
    )


def on_device_general(
    frames,
    cotangent,
    segments,
    layer_keep,
    joint_weight,
    output_weight,
    up_weight,
    down_weight,
    width_bias,
    hidden_bias,
    norm_gain,
    norm_shift,
):
    params = tuple(
        (
            array[0]
            for array in (
                joint_weight,
                output_weight,
                up_weight,
                down_weight,
                width_bias,
                hidden_bias,
                norm_gain,
                norm_shift,
            )
        )
    )
    section = lax.axis_index(SECTION_AXIS)
    rows = BATCH_ROWS
    number = BATCHES
    width = frames.shape[1]
    hidden_width = up_weight.shape[2]
    layer_out = jnp.zeros(frames.shape, jnp.bfloat16)
    stored = []
    previous = jnp.zeros((rows, width), jnp.bfloat16)
    for step in range(number + 1):
        arrived = shifted(previous, SECTION_AXIS, 1) if step > 0 else previous
        batch = step - section
        within = (batch >= 0) & (batch < number)
        place = jnp.clip(batch, 0, number - 1)
        start = place * rows
        inputs = jnp.where(section == 0, lax.dynamic_slice_in_dim(frames, start, rows, 0), arrived)
        labels = lax.dynamic_slice_in_dim(segments, start, rows, 0)
        valid = (labels >= 0).astype(jnp.float32)[:, None]
        flag = lax.dynamic_slice_in_dim(layer_keep[0], place, 1, 0)[0]
        running = within & (flag == 1)
        result, kept = lax.cond(
            running,
            lambda: layer_forward(inputs, labels, params),
            lambda: (inputs.astype(jnp.float32), empty_kept(rows, width, hidden_width)),
        )
        output = (valid * result).astype(jnp.bfloat16)
        earlier = lax.dynamic_slice_in_dim(layer_out, start, rows, 0)
        layer_out = lax.dynamic_update_slice_in_dim(
            layer_out, jnp.where(within, output, earlier), start, 0
        )
        previous = output
        stored.append((inputs, labels, running, start, within, kept))
    input_back = jnp.zeros(frames.shape, jnp.float32)
    totals = None
    sending = jnp.zeros((rows, width), jnp.float32)
    for step in range(number + 1):
        arrived = (
            shifted(sending.astype(jnp.bfloat16), SECTION_AXIS, -1).astype(sending.dtype)
            if step > 0
            else sending
        )
        entry = stored[number - step]
        inputs, labels, running, start, within = (entry[0], entry[1], entry[2], entry[3], entry[4])
        valid = (labels >= 0).astype(jnp.float32)[:, None]
        given = lax.dynamic_slice_in_dim(cotangent, start, rows, 0).astype(jnp.float32)
        upstream = valid * jnp.where(section == 1, given, arrived)

        def run_back():
            kept = entry[5]
            return layer_backward(inputs, labels, params, kept, upstream)

        def skip_back():
            return (upstream, tuple((jnp.zeros(item.shape, jnp.float32) for item in params)))

        passed, pieces = lax.cond(running, run_back, skip_back)
        earlier = lax.dynamic_slice_in_dim(input_back, start, rows, 0)
        input_back = lax.dynamic_update_slice_in_dim(
            input_back, jnp.where(within, passed, earlier), start, 0
        )
        sending = passed
        shares = pieces
        totals = (
            tuple(shares)
            if totals is None
            else tuple((left + right for left, right in zip(totals, shares)))
        )
    shares = (
        lax.psum_scatter(
            totals[0][None].astype(jnp.bfloat16), SHARD_AXIS, scatter_dimension=1, tiled=True
        ).astype(jnp.float32),
        lax.psum_scatter(
            totals[1][None].astype(jnp.bfloat16), SHARD_AXIS, scatter_dimension=1, tiled=True
        ).astype(jnp.float32),
        lax.psum_scatter(
            totals[2][None].astype(jnp.bfloat16), SHARD_AXIS, scatter_dimension=1, tiled=True
        ).astype(jnp.float32),
        lax.psum_scatter(
            totals[3][None].astype(jnp.bfloat16), SHARD_AXIS, scatter_dimension=2, tiled=True
        ).astype(jnp.float32),
        lax.psum_scatter(
            totals[4][None].astype(jnp.bfloat16), SHARD_AXIS, scatter_dimension=2, tiled=True
        ).astype(jnp.float32),
        lax.psum_scatter(
            totals[5][None].astype(jnp.bfloat16), SHARD_AXIS, scatter_dimension=1, tiled=True
        ).astype(jnp.float32),
        lax.psum_scatter(
            totals[6][None].astype(jnp.bfloat16), SHARD_AXIS, scatter_dimension=2, tiled=True
        ).astype(jnp.float32),
        lax.psum_scatter(
            totals[7][None].astype(jnp.bfloat16), SHARD_AXIS, scatter_dimension=2, tiled=True
        ).astype(jnp.float32),
    )
    reduced = (
        lax.psum(shares[0].astype(jnp.bfloat16), REPLICA_AXIS).astype(jnp.float32),
        lax.psum(shares[1].astype(jnp.bfloat16), REPLICA_AXIS).astype(jnp.float32),
        lax.psum(shares[2].astype(jnp.bfloat16), REPLICA_AXIS).astype(jnp.float32),
        lax.psum(shares[3].astype(jnp.bfloat16), REPLICA_AXIS).astype(jnp.float32),
        lax.psum(shares[4].astype(jnp.bfloat16), REPLICA_AXIS).astype(jnp.float32),
        lax.psum(shares[5].astype(jnp.bfloat16), REPLICA_AXIS).astype(jnp.float32),
        lax.psum(shares[6].astype(jnp.bfloat16), REPLICA_AXIS).astype(jnp.float32),
        lax.psum(shares[7].astype(jnp.bfloat16), REPLICA_AXIS).astype(jnp.float32),
    )
    return (
        layer_out[None],
        input_back[None],
        reduced[0],
        reduced[1],
        reduced[2],
        reduced[3],
        reduced[4],
        reduced[5],
        reduced[6],
        reduced[7],
    )


F32, BF16 = jnp.float32, jnp.bfloat16
MESH = pl.DeviceIdType.MESH
D, FF, ROWS, PAIRS = 768, 3072, 512, 6
SHARE = D // 4
TILE = 256
FIRST_TILE = {DOWN: 0, "up": 12, "o": 24, QKV: 27}
TILES = {DOWN: 12, "up": 12, "o": 3, QKV: 9}
LAYER_TILES = 36
LAYER_CHUNKS = LAYER_TILES // 2
CHUNKS = 2 * LAYER_CHUNKS
GAP = 3
STEP = [1 + GAP * i for i in range(5)]
SLOTS = 2 * GAP + 1
FAR_SLOTS = 3 * GAP + 1
WEIGHTS = (QKV, "o", "up", DOWN)
WEIGHT_SHAPE = {QKV: (D, 3 * D), "o": (D, D), "up": (D, FF), DOWN: (FF, D)}
SAVED = {
    QKV: ((ROWS, 3 * D), BF16),
    "mixed": ((ROWS, D), BF16),
    "aug": ((PAIRS, ROWS, 128), BF16),
    "n1": ((ROWS, D), F32),
    "scales": ((2, ROWS, 128), F32),
    "hid": ((ROWS, D), BF16),
    "act": ((ROWS, FF), BF16),
    "slope": ((ROWS, FF), BF16),
    "n2": ((ROWS, D), F32),
}
TEMPORARY = {
    "big": ((ROWS, D), F32),
    "low": ((ROWS, D), BF16),
    "left": ((D, ROWS), BF16),
    "mb": ((ROWS, D), BF16),
    "qb": ((ROWS, 3 * D), BF16),
}


def nn(a, b):
    return lax.dot_general(a, b, (((1,), (0,)), ((), ())), preferred_element_type=F32)


def nt(a, b):
    return lax.dot_general(a, b, (((1,), (1,)), ((), ())), preferred_element_type=F32)


def tn(a, b):
    return lax.dot_general(a, b, (((0,), (0,)), ((), ())), preferred_element_type=F32)


def half_lanes():
    return lax.broadcasted_iota(jnp.int32, (ROWS, 128), 1) < 64


def lane_place():
    return lax.broadcasted_iota(jnp.int32, (ROWS, 128), 1) % 64


def label_columns(rows):
    return jnp.concatenate([jnp.transpose(jnp.broadcast_to(row, (128, 128))) for row in rows], axis=0)


def mask_columns(label):
    place = lane_place()
    mine = place.astype(F32) == label + 1.0
    within = place < 17
    query = jnp.where(mine & within, 1.0, 0.0)
    keys = jnp.where(within & jnp.logical_not(mine), -1e30, 0.0)
    ones = jnp.where((place >= 20) & (place < 23), 1.0, 0.0)
    return query, keys + ones, ones


def three_parts(column, base):
    place = lane_place()
    first = column.astype(BF16).astype(F32)
    rest = column - first
    second = rest.astype(BF16).astype(F32)
    third = rest - second
    out = jnp.where(place == 20, first, base)
    out = jnp.where(place == 21, second, out)
    return jnp.where(place == 22, third, out)


def norm(total):
    mean = jnp.mean(total, axis=1, keepdims=True)
    centre = total - mean
    spread = jnp.mean(centre * centre, axis=1, keepdims=True)
    scale = lax.rsqrt(spread + 1e-05)
    return centre * scale, scale


def norm_back(upstream, normed, scale, gain):
    e = upstream * gain
    first = jnp.mean(e, axis=1, keepdims=True)
    second = jnp.mean(e * normed, axis=1, keepdims=True)
    return scale * (e - first - normed * second)


def gelu_both(v):
    cdf = 0.5 * (1.0 + lax.erf(v * 0.7071067811865476))
    return v * cdf, cdf + v * (jnp.exp(-0.5 * v * v) * 0.3989422804014327)


def column_sum(value):
    return jnp.sum(value, axis=0, keepdims=True)


def times(start, stop, body):
    lax.fori_loop(start, stop, lambda i, _: (body(i), 0)[1], 0)


def forward(x, label, w, sm, out, hook):
    for part in range(3):
        hook("part", part)
        acc = nn(x[...], w[QKV][:, part * D : part * D + D])
        if part == 0:
            acc = (acc + sm[0:1, :]).astype(BF16) * jnp.bfloat16(0.125)
        elif part == 2:
            acc = (acc + sm[1:2, :]).astype(BF16)
        else:
            acc = acc.astype(BF16)
        out[QKV][:, part * D : part * D + D] = acc
    hook(QKV)
    aq, ak, _ = mask_columns(label)
    aq16, ak16 = aq.astype(BF16), ak.astype(BF16)
    low = half_lanes()

    masks = [low, jnp.logical_not(low)]

    def pair(p):
        at = pl.multiple_of(p * 128, 128)
        qp = out[QKV][:, pl.ds(at, 128)]
        kp = out[QKV][:, pl.ds(D + at, 128)]
        vp = out[QKV][:, pl.ds(2 * D + at, 128)]
        scores = [nt(jnp.where(m, qp, aq16), jnp.where(m, kp, ak16)) for m in masks]
        res, lse = [], []
        for e in range(2):
            top = jnp.max(scores[e], axis=1, keepdims=True)
            raised = jnp.exp(scores[e] - top).astype(BF16)
            o = nn(raised, jnp.where(masks[e], vp, jnp.bfloat16(1.0)))
            total = o[:, 64:65] if e == 0 else o[:, 0:1]
            res.append(o * (1.0 / total))
            lse.append(-(top + jnp.log(total)))
        out["mixed"][:, pl.ds(at, 128)] = jnp.where(low, res[0], res[1]).astype(BF16)
        out["aug"][p] = three_parts(jnp.where(low, lse[1], lse[0]), aq).astype(BF16)

    def two_pairs(i):
        pair(2 * i)
        pair(2 * i + 1)

    times(0, PAIRS // 2, two_pairs)
    hook("attention")
    first = x[...].astype(F32) + nn(out["mixed"][...], w["o"][...]) + sm[2:3, :]
    n1, r1 = norm(first)
    out["n1"][...] = n1
    out["scales"][0] = jnp.broadcast_to(r1, (ROWS, 128))
    out["hid"][...] = (n1 * sm[8:9, :] + sm[10:11, :]).astype(BF16)
    hook("first")

    for j in range(4):
        hook("up_part", j)
        cols = slice(j * D, j * D + D)
        act, slope = gelu_both(nn(out["hid"][...], w["up"][:, cols]) + sm[4 + j : 5 + j, :])
        out["act"][:, cols] = act.astype(BF16)
        out["slope"][:, cols] = slope.astype(BF16)
    hook("up")
    hidden = out["n1"][...] * sm[8:9, :] + sm[10:11, :]
    hook("down_part", 0)
    second = hidden + nn(out["act"][:, : FF // 2], w[DOWN][: FF // 2, :]) + sm[3:4, :]
    hook("down_part", 1)
    second = second + nn(out["act"][:, FF // 2 :], w[DOWN][FF // 2 :, :])
    n2, r2 = norm(second)
    out["n2"][...] = n2
    out["scales"][1] = jnp.broadcast_to(r2, (ROWS, 128))
    hook("second")
    return n2 * sm[9:10, :] + sm[11:12, :]


def backward(upstream, label, w, sm, s, x, t, sums, grad, tick, wait, done, last):
    wait("n2")
    wait("scales")
    u = upstream()
    n2 = s["n2"][...]
    back = norm_back(u, n2, s["scales"][1][:, 0:1], sm[9:10, :])
    sums[9:10, :] = column_sum(u * n2)
    sums[11:12, :] = column_sum(u)
    t["big"][...] = back
    low16 = back.astype(BF16)
    t["low"][...] = low16
    sums[3:4, :] = column_sum(low16.astype(F32))
    t["left"][...] = jnp.transpose(low16)
    done("n2")
    wait("act")
    grad(DOWN, t["left"], s["act"])
    done("act")
    wait(DOWN)
    wait("slope")

    for j in range(4):
        cols = slice(j * D, j * D + D)
        ub = (nt(t["low"][...], w[DOWN][cols, :]) * s["slope"][:, cols].astype(F32)).astype(BF16)
        s["slope"][:, cols] = ub
        sums[4 + j : 5 + j, :] = column_sum(ub.astype(F32))
        tick("up_back", j)
    done(DOWN)
    wait("hid")
    t["left"][...] = jnp.transpose(s["hid"][...])
    done("hid")
    grad("up", t["left"], s["slope"])
    wait("up")
    hb = t["big"][...] + nt(s["slope"][...], w["up"][...])
    done("up")
    done("slope")
    wait("n1")
    n1 = s["n1"][...]
    sums[8:9, :] = column_sum(hb * n1)
    sums[10:11, :] = column_sum(hb)
    fb = norm_back(hb, n1, s["scales"][0][:, 0:1], sm[8:9, :])
    t["big"][...] = fb
    low16 = fb.astype(BF16)
    t["low"][...] = low16
    sums[2:3, :] = column_sum(low16.astype(F32))
    done("n1")
    done("scales")
    tick("hidden")
    wait("mixed")
    t["left"][...] = jnp.transpose(s["mixed"][...])
    grad("o", t["left"], t["low"])
    wait("o")
    t["mb"][...] = nt(t["low"][...], w["o"][...]).astype(BF16)
    done("o")
    tick("mixed")
    _, ak, av = mask_columns(label)
    ak16, av16 = ak.astype(BF16), av.astype(BF16)
    low = half_lanes()
    masks = [low, jnp.logical_not(low)]
    wait("saved_qkv")
    wait("aug")

    def pair(p):
        at = pl.multiple_of(p * 128, 128)
        qp = s[QKV][:, pl.ds(at, 128)]
        kp = s[QKV][:, pl.ds(D + at, 128)]
        vp = s[QKV][:, pl.ds(2 * D + at, 128)]
        dp = t["mb"][:, pl.ds(at, 128)]
        aq16 = s["aug"][p]
        product = dp.astype(F32) * s["mixed"][:, pl.ds(at, 128)].astype(F32)
        even = -jnp.sum(jnp.where(low, product, 0.0), axis=1, keepdims=True)
        odd = -jnp.sum(jnp.where(low, 0.0, product), axis=1, keepdims=True)
        ad16 = three_parts(jnp.where(low, odd, even), jnp.zeros((ROWS, 128), F32)).astype(BF16)
        scores = [nt(jnp.where(m, kp, ak16), jnp.where(m, qp, aq16)) for m in masks]
        prob_back = [nt(jnp.where(m, vp, av16), jnp.where(m, dp, ad16)) for m in masks]
        probs = [jnp.exp(score) for score in scores]
        score_back = [(probs[e] * prob_back[e]).astype(BF16) for e in range(2)]
        value_part = [nn(probs[e].astype(BF16), dp) for e in range(2)]
        key_part = [nn(score_back[e], qp) for e in range(2)]
        query_part = [tn(score_back[e], kp) * 0.125 for e in range(2)]
        for k, (even, odd) in enumerate((query_part, key_part, value_part)):
            t["qb"][:, pl.ds(k * D + at, 128)] = jnp.where(low, even, odd).astype(BF16)

    def two_pairs(i):
        pair(2 * i)
        pair(2 * i + 1)
        tick("pairs", i)

    times(0, PAIRS // 2, two_pairs)
    done("saved_qkv")
    done("aug")
    done("mixed")
    sums[0:1, :] = column_sum(t["qb"][:, 0:D].astype(F32))
    sums[1:2, :] = column_sum(t["qb"][:, 2 * D :].astype(F32))
    t["left"][...] = jnp.transpose(x[...])
    grad(QKV, t["left"], t["qb"])
    wait(QKV)
    last(t["big"][...] + nt(t["qb"][...], w[QKV][...]))
    done(QKV)
    tick("end")


def whole_step(*refs):
    it = iter(refs)
    take = lambda n: [next(it) for _ in range(n)]
    frames, cotangent, segments, keep_in, width_in, hidden_in, gain_in, shift_in = take(8)
    weight_in = dict(zip(WEIGHTS, take(4)))
    layer_out, input_back, shares, small_out = take(4)
    weight_far = dict(zip(WEIGHTS, take(4)))
    made, given = take(2)
    spill = dict(zip(SAVED, take(len(SAVED))))
    w = dict(zip(WEIGHTS, take(4)))
    s = dict(zip(SAVED, take(len(SAVED))))
    t = dict(zip(TEMPORARY, take(len(TEMPORARY))))
    x0, x1, x2, cot, dx1, small, sums, keep_tile, give_tile = take(9)
    ra, rb, sbuf, kbuf, r1, zbuf, zr1, part, zs2, zr2, ybuf, r3, fbuf, sb, sr = take(15)
    (
        load_sem, piece_sem, store_sem, spill_sem, in_sem, out_sem, out_recv, w_send, w_recv, small_sem,
        made_sem, give_send, give_recv, ra_sem, rb_sem, s1_send, s1_recv, z1_send, z1_recv,
        z2_send, z2_recv, s3_send, s3_recv, push_send, push_recv, sum_send, sum_recv, back_sem, back_recv,
    ) = take(29)

    me = lax.axis_index(SECTION_AXIS)
    z = lax.axis_index(SHARD_AXIS)
    r = lax.axis_index(REPLICA_AXIS)
    other = 1 - me
    x_at, y_at = lax.rem(r, 2), lax.div(r, 2)
    x_near, y_near = r + 1 - 2 * x_at, r + 2 - 4 * y_at
    half = (1 - me) * x_at + me * y_at
    first_near = (1 - me) * x_near + me * y_near
    second_near = (1 - me) * y_near + me * x_near
    is_end = lax.rem(z, 3) == 0
    is_middle = jnp.logical_not(is_end)
    partner = (other, z, r)

    def local(src, dst, sem):
        return pltpu.make_async_copy(src, dst, sem)

    def remote(src, dst, send, recv, device):
        return pltpu.make_async_remote_copy(
            src_ref=src, dst_ref=dst, send_sem=send, recv_sem=recv, device_id=device, device_id_type=MESH
        )

    own_rows = pl.ds(pl.multiple_of(me * ROWS, ROWS), ROWS)
    load_frames = local(frames.at[own_rows], x0, in_sem.at[0])
    load_cot = local(cotangent.at[own_rows], cot, in_sem.at[1])

    def weight_near(k):
        return local(weight_in[k].at[0], w[k], load_sem.at[WEIGHTS.index(k)])

    def weight_got(k):
        return local(weight_far[k], w[k], load_sem.at[WEIGHTS.index(k)])

    def piece(ref, k, i):
        if k == "o":
            return ref
        if k == DOWN:
            return ref.at[i * FF // 2 : (i + 1) * FF // 2]
        return ref.at[:, i * D : (i + 1) * D]

    near_piece, far_piece, far_store = {}, {}, {}
    for number, (k, i) in enumerate(PIECES):
        source = piece(weight_in[k].at[0], k, i)
        near_piece[k, i] = local(source, piece(w[k], k, i), piece_sem.at[number])
        far_piece[k, i] = remote(source, piece(w[k], k, i), w_send.at[number], w_recv.at[number], partner)
        far_store[k, i] = remote(source, piece(weight_far[k], k, i), w_send.at[number], w_recv.at[number], partner)
    small_send = remote(small.at[me], small.at[me], small_sem.at[0], small_sem.at[1], partner)

    load_frames.start()

    @pl.when(me == 0)
    def _():
        for key in PIECES:
            near_piece[key].start()

    small[me, 0:4] = width_in[0]
    for i in range(4):
        small[me, 4 + i : 5 + i] = hidden_in[0:1, i * D : (i + 1) * D]
    small[me, 8:10] = gain_in[0]
    small[me, 10:12] = shift_in[0]
    for i in range(2):
        small[me, 12 + i : 13 + i] = jnp.broadcast_to(keep_in[0:1, i : i + 1].astype(F32), (1, D))
    small[me, 14:16] = jnp.zeros((2, D), F32)

    barrier = pltpu.get_barrier_semaphore()
    greeted = [partner, (me, z, x_near), (me, z, y_near), (other, z, x_near), (other, z, y_near)]
    for device in greeted:
        pl.semaphore_signal(barrier, inc=1, device_id=device, device_id_type=MESH)
    for step in (1, 2):

        @pl.when(z + step < 4)
        def _(step=step):
            pl.semaphore_signal(barrier, inc=1, device_id=(me, z + step, r), device_id_type=MESH)

        @pl.when(z >= step)
        def _(step=step):
            pl.semaphore_signal(barrier, inc=1, device_id=(me, z - step, r), device_id_type=MESH)

    pl.semaphore_wait(barrier, len(greeted) + 2 + lax.rem(lax.div(z + 1, 2), 2))

    small_send.start()

    @pl.when(me == 0)
    def _():
        for key in PIECES:
            far_piece[key].start()

    @pl.when(me == 1)
    def _():
        for key in PIECES:
            far_store[key].start()

    load_cot.start()
    sums[...] = jnp.zeros_like(sums)
    label = label_columns([segments[pl.ds(4 * me + i, 1), :].astype(F32) for i in range(4)])
    valid = jnp.where(label[:, 0:1] >= 0.0, 1.0, 0.0)

    def spilled(k):
        return local(s[k], spill[k], spill_sem.at[list(SAVED).index(k)])

    def saved_load(k):
        return local(spill[k], s[k], spill_sem.at[list(SAVED).index(k)])

    def store_weight(k):
        return local(w[k], weight_far[k], store_sem.at[WEIGHTS.index(k)])

    def store_start(k):
        @pl.when(me == 1)
        def _():
            store_weight(k).start()

    def next_weight(k):
        @pl.when(me == 0)
        def _():
            for key in PIECES:
                if key[0] == k:
                    far_store[key].wait_recv()
            weight_got(k).start()

        @pl.when(me == 1)
        def _():
            store_weight(k).wait()
            weight_near(k).start()

    def first_weight(k):
        @pl.when(me == 0)
        def _():
            weight_near(k).start()

        @pl.when(me == 1)
        def _():
            weight_got(k).start()

    def weight_wait(k):
        weight_near(k).wait()

    def piece_wait(k, i):
        @pl.when(me == 0)
        def _():
            near_piece[k, i].wait()

        @pl.when(me == 1)
        def _():
            far_piece[k, i].wait_recv()

    def hook0(point, i=None):
        if point == "part":
            if i == 0:
                load_frames.wait()
                small_send.wait()
            piece_wait(QKV, i)
        elif point == QKV:
            store_start(QKV)
            spilled(QKV).start()
        elif point == "attention":
            next_weight(QKV)
            spilled("mixed").start()
            spilled("aug").start()
            piece_wait("o", 0)
        elif point == "first":
            store_start("o")
            spilled("n1").start()
            spilled("hid").start()
        elif point == "up_part":
            piece_wait("up", i)
        elif point == "up":
            next_weight("o")
            store_start("up")
            spilled("act").start()
            spilled("slope").start()
        elif point == "down_part":
            piece_wait(DOWN, i)
        elif point == "second":
            store_start(DOWN)
            spilled("n2").start()
            spilled("scales").start()

    def hook1(point, i=None):
        if point == "part":
            if i == 0:
                spilled(QKV).wait()
                weight_wait(QKV)
        elif point == QKV:
            next_weight("up")
            spilled("mixed").wait()
            spilled("aug").wait()
        elif point == "attention":
            next_weight(DOWN)
            spilled("n1").wait()
            spilled("hid").wait()
            spilled("scales").wait()
            weight_wait("o")
        elif point == "first":
            spilled("act").wait()
            spilled("slope").wait()
            weight_wait("up")
        elif point == "up":
            spilled("n2").wait()
            weight_wait(DOWN)

    def keep_of(layer):
        return jnp.where(me == 0, small[layer, 12:13, 0:1], small[layer, 13:14, 0:1])

    def out_copy(src, layer, buffer, send, recv, start):
        here = local(src, buffer.at[own_rows], send.at[layer])
        there = remote(src, buffer.at[own_rows], send.at[layer], recv, partner)

        @pl.when(me == layer)
        def _():
            here.start() if start else here.wait()

        @pl.when(me != layer)
        def _():
            there.start() if start else there.wait_send()

    def layer_result(result, x, layer):
        kept = jnp.where(keep_of(layer) > 0.5, result, x[...].astype(F32))
        return (valid * kept).astype(BF16)

    x1[...] = layer_result(forward(x0, label, w, small.at[0], s, hook0), x0, 0)
    out_copy(x1, 0, layer_out, out_sem, out_recv.at[0], True)
    x2[...] = layer_result(forward(x1, label, w, small.at[1], s, hook1), x1, 1)
    out_copy(x2, 1, layer_out, out_sem, out_recv.at[0], True)

    def keep_copy(c):
        return local(keep_tile.at[lax.rem(c, 2)], made.at[c], made_sem.at[lax.rem(c, 2)])

    def give_copy(c):
        slot = lax.rem(c, 4)
        return remote(give_tile.at[slot], given.at[c], give_send.at[slot], give_recv.at[c], partner)

    def load_own(c):
        return local(made.at[c], ra.at[lax.rem(c, 2)], ra_sem.at[lax.rem(c, 2)])

    def load_given(c):
        return local(given.at[c], rb.at[lax.rem(c, 2)], rb_sem.at[lax.rem(c, 2)])

    def copy_first(c):
        a, b = lax.rem(c, 4), lax.rem(c, SLOTS)
        return remote(sbuf.at[a], r1.at[b], s1_send.at[a], s1_recv.at[b], (me, z, first_near))

    def copy_end(c):
        a, b = lax.rem(c, 4), lax.rem(c, SLOTS)
        rows = pl.ds(pl.multiple_of(SHARE - SHARE * lax.div(z, 3), SHARE), 3 * SHARE)
        return remote(zbuf.at[a, rows], zr1.at[b], z1_send.at[a], z1_recv.at[b], (me, 1 + lax.div(z, 3), r))

    def copy_middle(c):
        a, b = lax.rem(c, 4), lax.rem(c, SLOTS)
        rows = pl.ds(pl.multiple_of(3 * SHARE * lax.div(z, 2), SHARE), SHARE)
        return remote(
            zbuf.at[a, rows], zr1.at[b, pl.ds(0, SHARE)], z1_send.at[a], z1_recv.at[b], (me, 3 * lax.div(z, 2), r)
        )

    def copy_across(c, which):
        a, b = lax.rem(c, 4), lax.rem(c, FAR_SLOTS)
        far = 3 - z if which == 0 else 3 - 3 * lax.div(z, 2)
        return remote(zs2.at[a, which], zr2.at[b], z2_send.at[a, which], z2_recv.at[b], (me, far, r))

    def copy_second(c):
        a, b = lax.rem(c, 4), lax.rem(c, SLOTS)
        return remote(ybuf.at[a], r3.at[b], s3_send.at[a], s3_recv.at[b], (me, z, second_near))

    def push(c, start):
        a = lax.rem(c, 4)
        layer = 1 - lax.div(c, LAYER_CHUNKS)
        place = lax.rem(c, LAYER_CHUNKS)
        cols = pl.ds(pl.multiple_of((2 * (2 * place + me) + half) * 128, 128), 128)
        here = local(fbuf.at[a], shares.at[:, cols], push_send.at[a, 0])
        beside = remote(fbuf.at[a], shares.at[:, cols], push_send.at[a, 0], push_recv.at[0, place], partner)
        near_same = remote(
            fbuf.at[a], shares.at[:, cols], push_send.at[a, 1], push_recv.at[1, place], (me, z, first_near)
        )
        near_other = remote(
            fbuf.at[a], shares.at[:, cols], push_send.at[a, 1], push_recv.at[2, place], (other, z, first_near)
        )

        @pl.when(layer == me)
        def _():
            here.start() if start else here.wait()
            near_same.start() if start else near_same.wait_send()

        @pl.when(layer != me)
        def _():
            beside.start() if start else beside.wait_send()
            near_other.start() if start else near_other.wait_send()

    def at_stage(c):
        return (c >= 0) & (c < CHUNKS)

    def comm(now):
        @pl.when(at_stage(now - STEP[4]))
        def _():
            c = now - STEP[4]
            a, b = lax.rem(c, 4), lax.rem(c, SLOTS)
            copy_second(c).wait()

            @pl.when(c >= 4)
            def _():
                push(c - 4, False)

            fbuf[a] = (ybuf[a].astype(F32) + r3[b].astype(F32)).astype(BF16)
            push(c, True)

        @pl.when(at_stage(now - STEP[3]))
        def _():
            c = now - STEP[3]
            a, b = lax.rem(c, 4), lax.rem(c, FAR_SLOTS)

            @pl.when(is_middle)
            def _():
                copy_across(c, 0).wait_send()
                copy_across(c, 1).wait_send()

            copy_across(c, 0).wait_recv()
            ybuf[a] = (part[a] + zr2[b].astype(F32)).astype(BF16)
            copy_second(c).start()

        @pl.when(at_stage(now - STEP[2]))
        def _():
            c = now - STEP[2]
            a, b = lax.rem(c, 4), lax.rem(c, SLOTS)

            @pl.when(is_end)
            def _():
                copy_end(c).wait_send()
                copy_middle(c).wait_recv()
                own = pl.ds(pl.multiple_of(z * SHARE, SHARE), SHARE)
                part[a] = kbuf[b, own] + zr1[b, 0:SHARE].astype(F32)

            @pl.when(is_middle)
            def _():
                copy_middle(c).wait_send()
                copy_end(c).wait_recv()
                low_row = SHARE * (2 - z)

                def sum_of(row):
                    row = pl.multiple_of(row, SHARE)
                    return (
                        kbuf[b, pl.ds(pl.multiple_of(low_row + row, SHARE), SHARE)]
                        + zr1[b, pl.ds(row, SHARE)].astype(F32)
                    )

                zs2[a, 0] = sum_of(jnp.int32(SHARE)).astype(BF16)
                zs2[a, 1] = sum_of(2 * SHARE * (2 - z)).astype(BF16)
                copy_across(c, 0).start()
                copy_across(c, 1).start()
                part[a] = sum_of(2 * SHARE * (z - 1))

        @pl.when(at_stage(now - STEP[1]))
        def _():
            c = now - STEP[1]
            a, b = lax.rem(c, 4), lax.rem(c, SLOTS)
            copy_first(c).wait()
            total = kbuf[b] + r1[b].astype(F32)
            kbuf[b] = total
            zbuf[a] = total.astype(BF16)

            @pl.when(is_end)
            def _():
                copy_end(c).start()

            @pl.when(is_middle)
            def _():
                copy_middle(c).start()

        @pl.when(at_stage(now - STEP[0]))
        def _():
            c = now - STEP[0]
            a, b, d = lax.rem(c, 4), lax.rem(c, SLOTS), lax.rem(c, 2)
            load_own(c).wait()
            load_given(c).wait()
            sbuf[a] = (ra[d, 1 - half].astype(F32) + rb[d, 1 - half].astype(F32)).astype(BF16)
            copy_first(c).start()
            kbuf[b] = ra[d, half].astype(F32) + rb[d, half].astype(F32)

        @pl.when(at_stage(now))
        def _():
            give_copy(now).wait_recv()
            load_own(now).start()
            load_given(now).start()

    def run_layer(layer, upstream, passed, x, ticks, wait, done):
        first_tile = 0 if layer == 1 else LAYER_TILES

        def put(c, tile, value):
            @pl.when(me == tile)
            def _():
                for i in range(2):
                    keep_tile[lax.rem(c, 2), i] = value[:, i * 128 : (i + 1) * 128]
                keep_copy(c).start()

            @pl.when(me != tile)
            def _():
                @pl.when(c >= 4)
                def _():
                    give_copy(c - 4).wait_send()

                for i in range(2):
                    give_tile[lax.rem(c, 4), i] = value[:, i * 128 : (i + 1) * 128]
                give_copy(c).start()

        def single(k, left, right, j):
            q = first_tile + FIRST_TILE[k] + j
            put(q // 2, q % 2, nn(left[...], right[:, j * TILE : (j + 1) * TILE]).astype(BF16))

        def grad(k, left, right):
            marks = ticks.get(k, {})
            first = FIRST_TILE[k] % 2
            begin = (first_tile + FIRST_TILE[k] + first) // 2
            n = (TILES[k] - first) // 2
            if first:
                single(k, left, right, 0)
                keep_copy(jnp.int32(begin - 1)).wait()

            def chunk(j):
                c = begin + j
                cols = pl.ds(pl.multiple_of((2 * j + first) * TILE, TILE), 2 * TILE)
                g = nn(left[...], right[:, cols]).astype(BF16)

                @pl.when(j >= 1)
                def _():
                    keep_copy(c - 1).wait()

                put(c, 0, g[:, :TILE])
                put(c, 1, g[:, TILE:])
                for at, number in marks.items():

                    @pl.when(j == at)
                    def _(number=number):
                        comm(jnp.int32(number))

            times(0, n, chunk)
            keep_copy(jnp.int32(begin + n - 1)).wait()
            if (TILES[k] - first) % 2:
                single(k, left, right, TILES[k] - 1)

        def tick(point, index=None):
            marks = ticks.get(point)
            if marks is None:
                return
            if index is None:
                comm(jnp.int32(marks))
            elif isinstance(marks, dict):
                if index in marks:
                    comm(jnp.int32(marks[index]))
            else:
                comm(marks + index)

        sm = small.at[layer]
        keep = keep_of(layer)

        def masked():
            return upstream[...].astype(F32) * (valid * keep)

        def last(value):
            passed[...] = value + upstream[...].astype(F32) * (valid * (1.0 - keep))

        backward(masked, label, w, sm, s, x, t, sums.at[layer], grad, tick, wait, done, last)

    def wait1(k):
        pass

    def done1(k):
        if k in WEIGHTS:
            first_weight(k)
        elif k == "saved_qkv":
            saved_load(QKV).start()
        else:
            saved_load(k).start()

    def wait0(k):
        if k in WEIGHTS:
            weight_wait(k)
        elif k == "saved_qkv":
            saved_load(QKV).wait()
        else:
            saved_load(k).wait()

    load_cot.wait()
    run_layer(1, cot, dx1, x1, TICKS[0], wait1, done1)
    out_copy(dx1, 1, input_back, back_sem, back_recv.at[0], True)
    run_layer(0, dx1, s["n1"], x0, TICKS[1], wait0, lambda k: None)
    out_copy(s["n1"], 0, input_back, back_sem, back_recv.at[0], True)

    def sum_copy(step):
        if step == 0:
            return remote(sums.at[other], sr.at[0], sum_send.at[0], sum_recv.at[0], partner)
        z_one = z + 1 - 2 * lax.rem(z, 2)
        z_two = lax.rem(z + 2, 4)
        device = [(me, z, x_near), (me, z, y_near), (me, z_one, r), (me, z_two, r)][step - 1]
        return remote(sb.at[step - 1], sr.at[step], sum_send.at[step], sum_recv.at[step], device)

    sum_copy(0).start()

    def final(now):
        for step in range(5):

            @pl.when(now == SUM_TICK + 2 * step)
            def _(step=step):
                sum_copy(step).wait()
                if step == 0:
                    sb[0] = sums[me] + sr[0]
                else:
                    sb[step] = sb[step - 1] + sr[step]
                if step < 4:
                    sum_copy(step + 1).start()

        comm(now)

    times(SUM_TICK, CHUNKS + STEP[-1], final)
    small_out[...] = sb[4]

    times(CHUNKS - 4, CHUNKS, lambda c: push(c, False))
    for stream in range(3):

        def arrived(place, stream=stream):
            remote(
                fbuf.at[0], shares.at[:, pl.ds(0, 128)], push_send.at[0, 0], push_recv.at[stream, place], partner
            ).wait_recv()

        times(0, LAYER_CHUNKS, arrived)
    times(CHUNKS - 4, CHUNKS, lambda c: give_copy(c).wait_send())
    for key in PIECES:
        far_piece[key].wait_send()
    out_copy(x1, 0, layer_out, out_sem, out_recv.at[0], False)
    out_copy(x2, 1, layer_out, out_sem, out_recv.at[0], False)
    out_copy(dx1, 1, input_back, back_sem, back_recv.at[0], False)
    out_copy(s["n1"], 0, input_back, back_sem, back_recv.at[0], False)
    remote(x1, layer_out.at[own_rows], out_sem.at[0], out_recv.at[0], partner).wait_recv()
    remote(dx1, input_back.at[own_rows], back_sem.at[0], back_recv.at[0], partner).wait_recv()


TICKS = (
    {DOWN: {1: 0, 3: 1, 5: 2}, "up_back": {1: 3, 3: 4}, "up": {1: 5, 3: 6, 5: 7}, "hidden": 8, "mixed": 9,
     "pairs": 10, QKV: {1: 13, 3: 14}, "end": 15},
    {DOWN: {1: 16, 3: 17, 5: 18}, "up_back": {1: 19, 3: 20}, "up": {1: 21, 3: 22, 5: 23}, "hidden": 24, "mixed": 25,
     "pairs": 26, QKV: {1: 29, 3: 30}, "end": 31},
)
SUM_TICK = 32
PIECES = [(QKV, 0), (QKV, 1), (QKV, 2), ("o", 0)] + [("up", i) for i in range(4)] + [(DOWN, i) for i in range(2)]


def any_space():
    return pl.BlockSpec(memory_space=pl.ANY)


def in_vmem():
    return pl.BlockSpec(memory_space=pltpu.VMEM)


def run_whole(*arguments):
    shape = jax.ShapeDtypeStruct
    outs = [
        shape((2 * ROWS, D), BF16),
        shape((2 * ROWS, D), F32),
        shape((SHARE, LAYER_TILES * TILE), BF16),
        shape((16, D), F32),
    ]
    outs += [shape(WEIGHT_SHAPE[k], BF16) for k in WEIGHTS]
    outs += [shape((CHUNKS, 2, D, 128), BF16)] * 2
    outs += [shape(*SAVED[k]) for k in SAVED]
    out_specs = [any_space()] * 3 + [in_vmem()] + [any_space()] * (len(outs) - 4)
    dma = pltpu.SemaphoreType.DMA
    scratch = [pltpu.VMEM(WEIGHT_SHAPE[k], BF16) for k in WEIGHTS]
    scratch += [pltpu.VMEM(*SAVED[k]) for k in SAVED]
    scratch += [pltpu.VMEM(*TEMPORARY[k]) for k in TEMPORARY]
    scratch += [pltpu.VMEM((ROWS, D), BF16)] * 4
    scratch += [
        pltpu.VMEM((ROWS, D), F32),
        pltpu.VMEM((2, 16, D), F32),
        pltpu.VMEM((2, 16, D), F32),
        pltpu.VMEM((2, 2, D, 128), BF16),
        pltpu.VMEM((4, 2, D, 128), BF16),
        pltpu.VMEM((2, 2, D, 128), BF16),
        pltpu.VMEM((2, 2, D, 128), BF16),
        pltpu.VMEM((4, D, 128), BF16),
        pltpu.VMEM((SLOTS, D, 128), F32),
        pltpu.VMEM((SLOTS, D, 128), BF16),
        pltpu.VMEM((4, D, 128), BF16),
        pltpu.VMEM((SLOTS, 3 * SHARE, 128), BF16),
        pltpu.VMEM((4, SHARE, 128), F32),
        pltpu.VMEM((4, 2, SHARE, 128), BF16),
        pltpu.VMEM((FAR_SLOTS, SHARE, 128), BF16),
        pltpu.VMEM((4, SHARE, 128), BF16),
        pltpu.VMEM((SLOTS, SHARE, 128), BF16),
        pltpu.VMEM((4, SHARE, 128), BF16),
        pltpu.VMEM((5, 16, D), F32),
        pltpu.VMEM((5, 16, D), F32),
    ]
    n = len(PIECES)
    sems = [
        (4,), (n,), (4,), (len(SAVED),), (2,), (2,), (1,), (n,), (n,), (2,),
        (2,), (4,), (CHUNKS,), (2,), (2,), (4,), (SLOTS,), (4,), (SLOTS,),
        (4, 2), (FAR_SLOTS,), (4,), (SLOTS,), (4, 2), (3, LAYER_CHUNKS), (5,), (5,), (2,), (1,),
    ]
    scratch += [dma(n) for n in sems]
    got = pl.pallas_call(
        whole_step,
        out_shape=outs,
        in_specs=[any_space()] * 2 + [in_vmem()] * 6 + [any_space()] * 4,
        out_specs=out_specs,
        scratch_shapes=scratch,
        compiler_params=pltpu.CompilerParams(
            collective_id=0, has_side_effects=True, vmem_limit_bytes=64 * 2**20 - 2**17
        ),
        name="whole_step",
    )(*arguments)
    return got[:4]


def finish_step(layer_out, input_back, shares, sums, *refs):
    out_layer, out_back, out_qkv, out_o, out_up, out_down, width, hidden, gain, shift = refs[:10]
    held, big_qkv, big_o, big_up, big_down, rows_low, rows_wide, sem = refs[10:]
    big = {QKV: big_qkv, "o": big_o, "up": big_up, DOWN: big_down}
    out = {QKV: out_qkv, "o": out_o, "up": out_up, DOWN: out_down}
    order = (DOWN, "up", QKV, "o")
    cols = {k: slice(FIRST_TILE[k] * TILE, (FIRST_TILE[k] + TILES[k]) * TILE) for k in order}
    load = {k: pltpu.make_async_copy(shares.at[:, cols[k]], held.at[:, cols[k]], sem.at[i]) for i, k in enumerate(order)}
    store = {k: pltpu.make_async_copy(big[k], out[k].at[0], sem.at[4 + i]) for i, k in enumerate(order)}
    through = [(layer_out, rows_low, out_layer), (input_back, rows_wide, out_back)]
    into = [pltpu.make_async_copy(a, b, sem.at[8 + i]) for i, (a, b, _) in enumerate(through)]
    onward = [pltpu.make_async_copy(b, c.at[0], sem.at[10 + i]) for i, (_, b, c) in enumerate(through)]
    for k in order:
        load[k].start()
    for copy in into:
        copy.start()
    for k in order:
        load[k].wait()
        big[k][...] = held[:, cols[k]].astype(F32)
        store[k].start()
    for one, two in zip(into, onward):
        one.wait()
        two.start()
    z = lax.axis_index(SHARD_AXIS)
    for i in range(4):

        @pl.when(z == i)
        def _(i=i):
            mine = slice(i * SHARE, (i + 1) * SHARE)
            width[0] = sums[0:4, mine]
            hidden[...] = sums[4 + i : 5 + i, :]
            gain[0] = sums[8:10, mine]
            shift[0] = sums[10:12, mine]

    for k in order:
        store[k].wait()
    for copy in onward:
        copy.wait()


def run_finish(layer_out, input_back, shares, sums):
    shape = jax.ShapeDtypeStruct
    outs = [shape((1, 2 * ROWS, D), BF16), shape((1, 2 * ROWS, D), F32), shape((1, SHARE, 3 * D), F32)]
    outs += [shape((1, SHARE, D), F32), shape((1, SHARE, FF), F32), shape((1, SHARE, FF), F32)]
    outs += [shape((1, 4, SHARE), F32), shape((1, D), F32), shape((1, 2, SHARE), F32), shape((1, 2, SHARE), F32)]
    return pl.pallas_call(
        finish_step,
        out_shape=outs,
        in_specs=[any_space()] * 3 + [in_vmem()],
        out_specs=[any_space()] * 6 + [in_vmem()] * 4,
        scratch_shapes=[
            pltpu.VMEM((SHARE, LAYER_TILES * TILE), BF16),
            pltpu.VMEM((SHARE, 3 * D), F32),
            pltpu.VMEM((SHARE, D), F32),
            pltpu.VMEM((SHARE, FF), F32),
            pltpu.VMEM((SHARE, FF), F32),
            pltpu.VMEM((2 * ROWS, D), BF16),
            pltpu.VMEM((2 * ROWS, D), F32),
            pltpu.SemaphoreType.DMA((12,)),
        ],
        compiler_params=pltpu.CompilerParams(vmem_limit_bytes=64 * 2**20 - 2**17),
        name="finish_step",
    )(layer_out, input_back, shares, sums)


def on_device_block(
    frames, cotangent, segments, layer_keep, joint_weight, output_weight, up_weight, down_weight,
    width_bias, hidden_bias, norm_gain, norm_shift,
):
    got = run_whole(
        frames, cotangent, segments.reshape(8, 128), layer_keep, width_bias, hidden_bias, norm_gain, norm_shift,
        joint_weight, output_weight, up_weight, down_weight,
    )
    outs = list(run_finish(*got))
    outs[5] = jnp.transpose(outs[5], (0, 2, 1))
    return tuple(outs)


def solution(mesh):
    sizes = dict(mesh.shape)
    fits = sizes == {SECTION_AXIS: 2, SHARD_AXIS: 4, REPLICA_AXIS: 4}
    placed = (
        P((SHARD_AXIS, REPLICA_AXIS), None),
        P((SHARD_AXIS, REPLICA_AXIS), None),
        P((SHARD_AXIS, REPLICA_AXIS)),
        P(SECTION_AXIS, (SHARD_AXIS, REPLICA_AXIS)),
        P(SECTION_AXIS, None, None),
        P(SECTION_AXIS, None, None),
        P(SECTION_AXIS, None, None),
        P(SECTION_AXIS, None, None),
        P(SECTION_AXIS, None, None),
        P(SECTION_AXIS, None),
        P(SECTION_AXIS, None, None),
        P(SECTION_AXIS, None, None),
    )
    return jax.shard_map(
        on_device_block if fits else on_device_general,
        mesh=mesh,
        in_specs=placed,
        out_specs=(
            P(SECTION_AXIS, (SHARD_AXIS, REPLICA_AXIS), None),
            P(SECTION_AXIS, (SHARD_AXIS, REPLICA_AXIS), None),
            P(SECTION_AXIS, SHARD_AXIS, None),
            P(SECTION_AXIS, SHARD_AXIS, None),
            P(SECTION_AXIS, SHARD_AXIS, None),
            P(SECTION_AXIS, None, SHARD_AXIS),
            P(SECTION_AXIS, None, SHARD_AXIS),
            P(SECTION_AXIS, SHARD_AXIS),
            P(SECTION_AXIS, None, SHARD_AXIS),
            P(SECTION_AXIS, None, SHARD_AXIS),
        ),
        check_vma=False,
    )
```

```python
import functools

import jax
import jax.numpy as jnp
from jax import lax
from jax.experimental import pallas as pl
from jax.experimental.pallas import tpu as pltpu
from jax.sharding import PartitionSpec as P

SECTION_AXIS, SHARD_AXIS, REPLICA_AXIS = "section", "shard", "replica"
QKV, DOWN = "qkv", "down"

HEADS = 12
HEAD_SIZE = 64
BATCH_ROWS = 512
BATCHES = 2


epsilon = 1e-05
masked_score = -1e30


def shifted(block, axis, distance):
    devices = range(lax.axis_size(axis))
    route = [(i - distance, i) for i in devices if i - distance in devices]
    return lax.ppermute(block, axis, route)


def layer_norm(value, gain, shift):
    centre = value - jnp.mean(value, axis=-1, keepdims=True)
    spread = jnp.mean(centre * centre, axis=-1, keepdims=True)
    return centre * lax.rsqrt(spread + epsilon) * gain + shift


def exact_gelu(value):
    return jax.nn.gelu(value, approximate=False)


def over_rows(left, right):
    return lax.dot_general(
        left, right, (((0,), (0,)), ((), ())), preferred_element_type=jnp.float32
    )


def against(left, right):
    return lax.dot_general(
        left, right, (((1,), (1,)), ((), ())), preferred_element_type=jnp.float32
    )


def split_heads(joint_low):
    rows = joint_low.shape[0]
    width = joint_low.shape[1] // 3
    query = joint_low[:, :width].reshape(rows, HEADS, HEAD_SIZE)
    keys = joint_low[:, width : 2 * width].reshape(rows, HEADS, HEAD_SIZE)
    values = joint_low[:, 2 * width :].reshape(rows, HEADS, HEAD_SIZE)
    return (query, keys, values)


def block_scores(query_part, keys, label_part, labels):
    scores = jnp.einsum(
        "qhd,khd->hqk", query_part, keys, preferred_element_type=jnp.float32
    ) * HEAD_SIZE ** (-0.5)
    allowed = label_part[:, None] == labels[None, :]
    return jnp.where(allowed[None], scores, masked_score)


def attend_forward(joint_low, labels):
    query, keys, values = split_heads(joint_low)
    rows = query.shape[0]
    block = min(512, rows)

    def one_block(start):
        scores = block_scores(query, keys, labels, labels)
        peak = jnp.max(scores, axis=-1, keepdims=True)
        raised = jnp.exp(scores - peak)
        total = jnp.sum(raised, axis=-1, keepdims=True)
        probs_low = (raised / total).astype(jnp.bfloat16)
        mixed = jnp.einsum("hqk,khd->qhd", probs_low, values, preferred_element_type=jnp.float32)
        return (mixed.reshape(block, HEADS * HEAD_SIZE), (peak + jnp.log(total))[..., 0])

    starts = jnp.arange(rows // block, dtype=jnp.int32) * block
    mixed, log_totals = lax.map(one_block, starts)
    return (mixed.reshape(rows, HEADS * HEAD_SIZE), log_totals)


def attend_backward(joint_low, labels, log_totals, mixed_back):
    query, keys, values = split_heads(joint_low)
    rows = query.shape[0]
    block = min(512, rows)
    back_heads = mixed_back.reshape(rows, HEADS, HEAD_SIZE)
    factor = HEAD_SIZE ** (-0.5)

    def one_block(carry, items):
        key_sum, value_sum = carry
        start, log_part = items
        scores = block_scores(query, keys, labels, labels)
        probs = jnp.exp(scores - log_part[..., None])
        probs_low = probs.astype(jnp.bfloat16)
        prob_back = jnp.einsum(
            "qhd,khd->hqk", back_heads, values, preferred_element_type=jnp.float32
        )
        inner = jnp.sum(prob_back * probs, axis=-1, keepdims=True)
        score_back = (probs * (prob_back - inner)).astype(jnp.bfloat16)
        query_back = (
            jnp.einsum("hqk,khd->qhd", score_back, keys, preferred_element_type=jnp.float32)
            * factor
        )
        key_sum = (
            key_sum
            + jnp.einsum("hqk,qhd->khd", score_back, query, preferred_element_type=jnp.float32)
            * factor
        )
        value_sum = value_sum + jnp.einsum(
            "hqk,qhd->khd", probs_low, back_heads, preferred_element_type=jnp.float32
        )
        return ((key_sum, value_sum), query_back.reshape(block, HEADS * HEAD_SIZE))

    starts = jnp.arange(rows // block, dtype=jnp.int32) * block
    empty = jnp.zeros((rows, HEADS, HEAD_SIZE), jnp.float32)
    (key_sum, value_sum), query_back = lax.scan(one_block, (empty, empty), (starts, log_totals))
    width = HEADS * HEAD_SIZE
    return jnp.concatenate(
        [
            query_back.reshape(rows, width),
            key_sum.reshape(rows, width),
            value_sum.reshape(rows, width),
        ],
        axis=1,
    )


def layer_forward(inputs, labels, params):
    (
        joint_weight,
        output_weight,
        up_weight,
        down_weight,
        width_bias,
        hidden_bias,
        norm_gain,
        norm_shift,
    ) = params
    width = inputs.shape[1]
    joint_bias = jnp.concatenate([width_bias[0], jnp.zeros((width,), jnp.float32), width_bias[1]])
    joint_low = (
        jnp.dot(inputs, joint_weight, preferred_element_type=jnp.float32) + joint_bias
    ).astype(jnp.bfloat16)
    mixed, log_totals = attend_forward(joint_low, labels)
    mixed_low = mixed.astype(jnp.bfloat16)
    first_sum = inputs.astype(jnp.float32) + (
        jnp.dot(mixed_low, output_weight, preferred_element_type=jnp.float32) + width_bias[2]
    )
    hidden = layer_norm(first_sum, norm_gain[0], norm_shift[0])
    hidden_low = hidden.astype(jnp.bfloat16)
    up_value = jnp.dot(hidden_low, up_weight, preferred_element_type=jnp.float32) + hidden_bias
    active_low = exact_gelu(up_value).astype(jnp.bfloat16)
    second_sum = hidden + (
        jnp.dot(active_low, down_weight, preferred_element_type=jnp.float32) + width_bias[3]
    )
    result = layer_norm(second_sum, norm_gain[1], norm_shift[1])
    return (
        result,
        (joint_low, log_totals, mixed_low, first_sum, hidden_low, up_value, active_low, second_sum),
    )


def empty_kept(rows, width, hidden_width):
    block = min(512, rows)
    return (
        jnp.zeros((rows, 3 * width), jnp.bfloat16),
        jnp.zeros((rows // block, HEADS, block), jnp.float32),
        jnp.zeros((rows, width), jnp.bfloat16),
        jnp.zeros((rows, width), jnp.float32),
        jnp.zeros((rows, width), jnp.bfloat16),
        jnp.zeros((rows, hidden_width), jnp.float32),
        jnp.zeros((rows, hidden_width), jnp.bfloat16),
        jnp.zeros((rows, width), jnp.float32),
    )


def layer_backward(inputs, labels, params, kept, upstream):
    (
        joint_weight,
        output_weight,
        up_weight,
        down_weight,
        width_bias,
        hidden_bias,
        norm_gain,
        norm_shift,
    ) = params
    joint_low, log_totals, mixed_low, first_sum, hidden_low, up_value, active_low, second_sum = kept
    width = inputs.shape[1]
    second_norm, second_pull = jax.vjp(layer_norm, second_sum, norm_gain[1], norm_shift[1])
    second_back, second_gain, second_shift = second_pull(upstream)
    branch_back = second_back.astype(jnp.bfloat16)
    down_part = over_rows(active_low, branch_back)
    down_bias = jnp.sum(branch_back.astype(jnp.float32), axis=0)
    active_back = against(branch_back, down_weight)
    gelu_value, gelu_pull = jax.vjp(exact_gelu, up_value)
    up_back = gelu_pull(active_back)[0].astype(jnp.bfloat16)
    up_part = over_rows(hidden_low, up_back)
    up_bias = jnp.sum(up_back.astype(jnp.float32), axis=0)
    hidden_back = second_back + against(up_back, up_weight)
    first_norm, first_pull = jax.vjp(layer_norm, first_sum, norm_gain[0], norm_shift[0])
    first_back, first_gain, first_shift = first_pull(hidden_back)
    attention_back = first_back.astype(jnp.bfloat16)
    output_part = over_rows(mixed_low, attention_back)
    output_bias = jnp.sum(attention_back.astype(jnp.float32), axis=0)
    mixed_back = against(attention_back, output_weight).astype(jnp.bfloat16)
    joint_back = attend_backward(joint_low, labels, log_totals, mixed_back).astype(jnp.bfloat16)
    joint_part = over_rows(inputs, joint_back)
    joint_bias = jnp.sum(joint_back.astype(jnp.float32), axis=0)
    passed = first_back + against(joint_back, joint_weight)
    width_part = jnp.stack([joint_bias[:width], joint_bias[2 * width :], output_bias, down_bias])
    gain_part = jnp.stack([first_gain, second_gain])
    shift_part = jnp.stack([first_shift, second_shift])
    return (
        passed,
        (joint_part, output_part, up_part, down_part, width_part, up_bias, gain_part, shift_part),
    )


def on_device_general(
    frames,
    cotangent,
    segments,
    layer_keep,
    joint_weight,
    output_weight,
    up_weight,
    down_weight,
    width_bias,
    hidden_bias,
    norm_gain,
    norm_shift,
):
    params = tuple(
        (
            array[0]
            for array in (
                joint_weight,
                output_weight,
                up_weight,
                down_weight,
                width_bias,
                hidden_bias,
                norm_gain,
                norm_shift,
            )
        )
    )
    section = lax.axis_index(SECTION_AXIS)
    rows = BATCH_ROWS
    number = BATCHES
    width = frames.shape[1]
    hidden_width = up_weight.shape[2]
    layer_out = jnp.zeros(frames.shape, jnp.bfloat16)
    stored = []
    previous = jnp.zeros((rows, width), jnp.bfloat16)
    for step in range(number + 1):
        arrived = shifted(previous, SECTION_AXIS, 1) if step > 0 else previous
        batch = step - section
        within = (batch >= 0) & (batch < number)
        place = jnp.clip(batch, 0, number - 1)
        start = place * rows
        inputs = jnp.where(section == 0, lax.dynamic_slice_in_dim(frames, start, rows, 0), arrived)
        labels = lax.dynamic_slice_in_dim(segments, start, rows, 0)
        valid = (labels >= 0).astype(jnp.float32)[:, None]
        flag = lax.dynamic_slice_in_dim(layer_keep[0], place, 1, 0)[0]
        running = within & (flag == 1)
        result, kept = lax.cond(
            running,
            lambda: layer_forward(inputs, labels, params),
            lambda: (inputs.astype(jnp.float32), empty_kept(rows, width, hidden_width)),
        )
        output = (valid * result).astype(jnp.bfloat16)
        earlier = lax.dynamic_slice_in_dim(layer_out, start, rows, 0)
        layer_out = lax.dynamic_update_slice_in_dim(
            layer_out, jnp.where(within, output, earlier), start, 0
        )
        previous = output
        stored.append((inputs, labels, running, start, within, kept))
    input_back = jnp.zeros(frames.shape, jnp.float32)
    totals = None
    sending = jnp.zeros((rows, width), jnp.float32)
    for step in range(number + 1):
        arrived = (
            shifted(sending.astype(jnp.bfloat16), SECTION_AXIS, -1).astype(sending.dtype)
            if step > 0
            else sending
        )
        entry = stored[number - step]
        inputs, labels, running, start, within = (entry[0], entry[1], entry[2], entry[3], entry[4])
        valid = (labels >= 0).astype(jnp.float32)[:, None]
        given = lax.dynamic_slice_in_dim(cotangent, start, rows, 0).astype(jnp.float32)
        upstream = valid * jnp.where(section == 1, given, arrived)

        def run_back():
            kept = entry[5]
            return layer_backward(inputs, labels, params, kept, upstream)

        def skip_back():
            return (upstream, tuple((jnp.zeros(item.shape, jnp.float32) for item in params)))

        passed, pieces = lax.cond(running, run_back, skip_back)
        earlier = lax.dynamic_slice_in_dim(input_back, start, rows, 0)
        input_back = lax.dynamic_update_slice_in_dim(
            input_back, jnp.where(within, passed, earlier), start, 0
        )
        sending = passed
        shares = pieces
        totals = (
            tuple(shares)
            if totals is None
            else tuple((left + right for left, right in zip(totals, shares)))
        )
    shares = (
        lax.psum_scatter(
            totals[0][None].astype(jnp.bfloat16), SHARD_AXIS, scatter_dimension=1, tiled=True
        ).astype(jnp.float32),
        lax.psum_scatter(
            totals[1][None].astype(jnp.bfloat16), SHARD_AXIS, scatter_dimension=1, tiled=True
        ).astype(jnp.float32),
        lax.psum_scatter(
            totals[2][None].astype(jnp.bfloat16), SHARD_AXIS, scatter_dimension=1, tiled=True
        ).astype(jnp.float32),
        lax.psum_scatter(
            totals[3][None].astype(jnp.bfloat16), SHARD_AXIS, scatter_dimension=2, tiled=True
        ).astype(jnp.float32),
        lax.psum_scatter(
            totals[4][None].astype(jnp.bfloat16), SHARD_AXIS, scatter_dimension=2, tiled=True
        ).astype(jnp.float32),
        lax.psum_scatter(
            totals[5][None].astype(jnp.bfloat16), SHARD_AXIS, scatter_dimension=1, tiled=True
        ).astype(jnp.float32),
        lax.psum_scatter(
            totals[6][None].astype(jnp.bfloat16), SHARD_AXIS, scatter_dimension=2, tiled=True
        ).astype(jnp.float32),
        lax.psum_scatter(
            totals[7][None].astype(jnp.bfloat16), SHARD_AXIS, scatter_dimension=2, tiled=True
        ).astype(jnp.float32),
    )
    reduced = (
        lax.psum(shares[0].astype(jnp.bfloat16), REPLICA_AXIS).astype(jnp.float32),
        lax.psum(shares[1].astype(jnp.bfloat16), REPLICA_AXIS).astype(jnp.float32),
        lax.psum(shares[2].astype(jnp.bfloat16), REPLICA_AXIS).astype(jnp.float32),
        lax.psum(shares[3].astype(jnp.bfloat16), REPLICA_AXIS).astype(jnp.float32),
        lax.psum(shares[4].astype(jnp.bfloat16), REPLICA_AXIS).astype(jnp.float32),
        lax.psum(shares[5].astype(jnp.bfloat16), REPLICA_AXIS).astype(jnp.float32),
        lax.psum(shares[6].astype(jnp.bfloat16), REPLICA_AXIS).astype(jnp.float32),
        lax.psum(shares[7].astype(jnp.bfloat16), REPLICA_AXIS).astype(jnp.float32),
    )
    return (
        layer_out[None],
        input_back[None],
        reduced[0],
        reduced[1],
        reduced[2],
        reduced[3],
        reduced[4],
        reduced[5],
        reduced[6],
        reduced[7],
    )


F32, BF16 = jnp.float32, jnp.bfloat16
MESH = pl.DeviceIdType.MESH
D, FF, ROWS, PAIRS = 768, 3072, 512, 6
SHARE = D // 4
TILE = 256
FIRST_TILE = {DOWN: 0, "up": 12, "o": 24, QKV: 27}
TILES = {DOWN: 12, "up": 12, "o": 3, QKV: 9}
LAYER_TILES = 36
LAYER_CHUNKS = LAYER_TILES // 2
CHUNKS = 2 * LAYER_CHUNKS
GAP = 4
STEP = [1 + GAP * i for i in range(5)]
SLOTS = 2 * GAP + 1
FAR_SLOTS = 3 * GAP + 1
WIDE_GAP = 6
LAST_STEP = STEP[2] + WIDE_GAP
WIDE_SLOTS = 2 * WIDE_GAP + 1
RESULTS = 10
KEPT = 9
AHEAD = 10
LOOK = 9
TAKE, USE = 3, 2
LATE = 4
FIRST_LATE = CHUNKS - LATE
HALF_SHARE = SHARE // 2
FAR_SLOTS = 3 * GAP + 1
WEIGHTS = (QKV, "o", "up", DOWN)
WEIGHT_SHAPE = {QKV: (D, 3 * D), "o": (D, D), "up": (D, FF), DOWN: (FF, D)}
SAVED = {
    QKV: ((ROWS, 3 * D), BF16),
    "mixed": ((ROWS, D), BF16),
    "aug": ((PAIRS, ROWS, 128), BF16),
    "n1": ((ROWS, D), F32),
    "scales": ((2, ROWS, 128), F32),
    "hid": ((ROWS, D), BF16),
    "act": ((ROWS, FF), BF16),
    "slope": ((ROWS, FF), BF16),
    "n2": ((ROWS, D), F32),
}
TEMPORARY = {
    "big": ((ROWS, D), F32),
    "low": ((ROWS, D), BF16),
    "left": ((D, ROWS), BF16),
    "mb": ((ROWS, D), BF16),
    "qb": ((ROWS, 3 * D), BF16),
}


def nn(a, b):
    return lax.dot_general(a, b, (((1,), (0,)), ((), ())), preferred_element_type=F32)


def nt(a, b):
    return lax.dot_general(a, b, (((1,), (1,)), ((), ())), preferred_element_type=F32)


def tn(a, b):
    return lax.dot_general(a, b, (((0,), (0,)), ((), ())), preferred_element_type=F32)


def half_lanes():
    return lax.broadcasted_iota(jnp.int32, (ROWS, 128), 1) < 64


def lane_place():
    return lax.broadcasted_iota(jnp.int32, (ROWS, 128), 1) % 64


def label_columns(rows):
    return jnp.concatenate([jnp.transpose(jnp.broadcast_to(row, (128, 128))) for row in rows], axis=0)


def mask_columns(label):
    place = lane_place()
    mine = place.astype(F32) == label + 1.0
    within = place < 17
    query = jnp.where(mine & within, 1.0, 0.0)
    keys = jnp.where(within & jnp.logical_not(mine), -1e30, 0.0)
    ones = jnp.where((place >= 20) & (place < 23), 1.0, 0.0)
    return query, keys + ones, ones


def three_parts(column, base):
    place = lane_place()
    first = column.astype(BF16).astype(F32)
    rest = column - first
    second = rest.astype(BF16).astype(F32)
    third = rest - second
    out = jnp.where(place == 20, first, base)
    out = jnp.where(place == 21, second, out)
    return jnp.where(place == 22, third, out)


def norm(total):
    mean = jnp.mean(total, axis=1, keepdims=True)
    centre = total - mean
    spread = jnp.mean(centre * centre, axis=1, keepdims=True)
    scale = lax.rsqrt(spread + 1e-05)
    return centre * scale, scale


def norm_back(upstream, normed, scale, gain):
    e = upstream * gain
    first = jnp.mean(e, axis=1, keepdims=True)
    second = jnp.mean(e * normed, axis=1, keepdims=True)
    return scale * (e - first - normed * second)


def gelu_both(v):
    cdf = 0.5 * (1.0 + lax.erf(v * 0.7071067811865476))
    return v * cdf, cdf + v * (jnp.exp(-0.5 * v * v) * 0.3989422804014327)


def column_sum(value):
    return jnp.sum(value, axis=0, keepdims=True)


def times(start, stop, body):
    lax.fori_loop(start, stop, lambda i, _: (body(i), 0)[1], 0)


def forward(x, label, w, sm, out, hook, groups):
    aq, ak, _ = mask_columns(label)
    aq16, ak16 = aq.astype(BF16), ak.astype(BF16)
    low = half_lanes()
    masks = [low, jnp.logical_not(low)]

    def pair(p):
        at = p * 128
        qp = out[QKV][:, at : at + 128]
        kp = out[QKV][:, D + at : D + at + 128]
        vp = out[QKV][:, 2 * D + at : 2 * D + at + 128]
        scores = [nt(jnp.where(m, qp, aq16), jnp.where(m, kp, ak16)) for m in masks]
        res, lse = [], []
        for e in range(2):
            top = jnp.max(scores[e], axis=1, keepdims=True)
            raised = jnp.exp(scores[e] - top).astype(BF16)
            o = nn(raised, jnp.where(masks[e], vp, jnp.bfloat16(1.0)))
            total = o[:, 64:65] if e == 0 else o[:, 0:1]
            res.append(o * (1.0 / total))
            lse.append(-(top + jnp.log(total)))
        out["mixed"][:, at : at + 128] = jnp.where(low, res[0], res[1]).astype(BF16)
        out["aug"][p] = three_parts(jnp.where(low, lse[1], lse[0]), aq).astype(BF16)

    wide = D // groups
    for group in range(groups):
        hook("part", group)
        here = slice(group * wide, group * wide + wide)
        for part in range(3):
            cols = slice(part * D + group * wide, part * D + group * wide + wide)
            acc = nn(x[...], w[QKV][:, cols])
            if part == 0:
                acc = (acc + sm[0:1, here]).astype(BF16) * jnp.bfloat16(0.125)
            elif part == 2:
                acc = (acc + sm[1:2, here]).astype(BF16)
            else:
                acc = acc.astype(BF16)
            out[QKV][:, cols] = acc
        if group == groups - 1:
            hook(QKV)
        for p in range(PAIRS // groups):
            pair(group * (PAIRS // groups) + p)
    hook("attention")
    first = x[...].astype(F32) + nn(out["mixed"][...], w["o"][...]) + sm[2:3, :]
    n1, r1 = norm(first)
    out["n1"][...] = n1
    out["scales"][0] = jnp.broadcast_to(r1, (ROWS, 128))
    out["hid"][...] = (n1 * sm[8:9, :] + sm[10:11, :]).astype(BF16)
    hook("first")
    for j in range(4):
        cols = slice(j * D, j * D + D)
        act, slope = gelu_both(nn(out["hid"][...], w["up"][:, cols]) + sm[4 + j : 5 + j, :])
        out["act"][:, cols] = act.astype(BF16)
        out["slope"][:, cols] = slope.astype(BF16)
    hook("up")
    hidden = out["n1"][...] * sm[8:9, :] + sm[10:11, :]
    second = hidden + nn(out["act"][...], w[DOWN][...]) + sm[3:4, :]
    n2, r2 = norm(second)
    out["n2"][...] = n2
    out["scales"][1] = jnp.broadcast_to(r2, (ROWS, 128))
    hook("second")


def backward(upstream, label, w, sm, s, x, t, sums, grad, tick, wait, done, last, extra):
    wait("n2")
    wait("scales")
    u = upstream()
    n2 = s["n2"][...]
    back = norm_back(u, n2, s["scales"][1][:, 0:1], sm[9:10, :])
    t["big"][...] = back
    low16 = back.astype(BF16)
    t["low"][...] = low16
    t["left"][...] = jnp.transpose(low16)
    tick("start")
    wait("act")
    grad(DOWN, t["left"], s["act"])
    done("act")
    u = upstream()
    sums[9:10, :] = column_sum(u * s["n2"][...])
    sums[11:12, :] = column_sum(u)
    sums[3:4, :] = column_sum(t["low"][...].astype(F32))
    extra()
    done("n2")
    wait(DOWN)
    wait("slope")

    for j in range(4):
        cols = slice(j * D, j * D + D)
        ub = (nt(t["low"][...], w[DOWN][cols, :]) * s["slope"][:, cols].astype(F32)).astype(BF16)
        s["slope"][:, cols] = ub
        sums[4 + j : 5 + j, :] = column_sum(ub.astype(F32))
        tick("up_back", j)
    done(DOWN)
    wait("hid")
    t["left"][...] = jnp.transpose(s["hid"][...])
    done("hid")
    grad("up", t["left"], s["slope"])
    wait("up")
    hb = t["big"][...] + nt(s["slope"][...], w["up"][...])
    done("up")
    done("slope")
    wait("n1")
    n1 = s["n1"][...]
    sums[8:9, :] = column_sum(hb * n1)
    sums[10:11, :] = column_sum(hb)
    fb = norm_back(hb, n1, s["scales"][0][:, 0:1], sm[8:9, :])
    t["big"][...] = fb
    low16 = fb.astype(BF16)
    t["low"][...] = low16
    sums[2:3, :] = column_sum(low16.astype(F32))
    done("n1")
    done("scales")
    tick("hidden")
    wait("mixed")
    t["left"][...] = jnp.transpose(s["mixed"][...])
    grad("o", t["left"], t["low"])
    wait("o")
    t["mb"][...] = nt(t["low"][...], w["o"][...]).astype(BF16)
    done("o")
    tick("mixed")
    _, ak, av = mask_columns(label)
    ak16, av16 = ak.astype(BF16), av.astype(BF16)
    low = half_lanes()
    masks = [low, jnp.logical_not(low)]
    tick("before")
    wait("saved_qkv")
    wait("aug")

    def pair(p):
        at = pl.multiple_of(p * 128, 128)
        qp = s[QKV][:, pl.ds(at, 128)]
        kp = s[QKV][:, pl.ds(D + at, 128)]
        vp = s[QKV][:, pl.ds(2 * D + at, 128)]
        dp = t["mb"][:, pl.ds(at, 128)]
        aq16 = s["aug"][p]
        product = dp.astype(F32) * s["mixed"][:, pl.ds(at, 128)].astype(F32)
        even = -jnp.sum(jnp.where(low, product, 0.0), axis=1, keepdims=True)
        odd = -jnp.sum(jnp.where(low, 0.0, product), axis=1, keepdims=True)
        ad16 = three_parts(jnp.where(low, odd, even), jnp.zeros((ROWS, 128), F32)).astype(BF16)
        scores = [nt(jnp.where(m, kp, ak16), jnp.where(m, qp, aq16)) for m in masks]
        prob_back = [nt(jnp.where(m, vp, av16), jnp.where(m, dp, ad16)) for m in masks]
        probs = [jnp.exp(score) for score in scores]
        score_back = [(probs[e] * prob_back[e]).astype(BF16) for e in range(2)]
        value_part = [nn(probs[e].astype(BF16), dp) for e in range(2)]
        key_part = [nn(score_back[e], qp) for e in range(2)]
        query_part = [tn(score_back[e], kp) * 0.125 for e in range(2)]
        for k, (even, odd) in enumerate((query_part, key_part, value_part)):
            t["qb"][:, pl.ds(k * D + at, 128)] = jnp.where(low, even, odd).astype(BF16)

    def two_pairs(i):
        pair(2 * i)
        pair(2 * i + 1)
        tick("pairs", i)

    times(0, PAIRS // 2, two_pairs)
    done("saved_qkv")
    done("aug")
    done("mixed")
    sums[0:1, :] = column_sum(t["qb"][:, 0:D].astype(F32))
    sums[1:2, :] = column_sum(t["qb"][:, 2 * D :].astype(F32))
    t["left"][...] = jnp.transpose(x[...])
    grad(QKV, t["left"], t["qb"])
    wait(QKV)
    last(t["big"][...] + nt(t["qb"][...], w[QKV][...]))
    done(QKV)
    tick("end")


def whole_step(*refs):
    it = iter(refs)
    take = lambda n: [next(it) for _ in range(n)]
    frames, cotangent, segments, keep_in, width_in, hidden_in, gain_in, shift_in = take(8)
    weight_in = dict(zip(WEIGHTS, take(4)))
    layer_out, input_back, shares, small_out = take(4)
    weight_far = dict(zip(WEIGHTS, take(4)))
    given, firsts = take(2)
    spill = dict(zip(SAVED, take(len(SAVED))))
    w = dict(zip(WEIGHTS, take(4)))
    s = dict(zip(SAVED, take(len(SAVED))))
    t = dict(zip(TEMPORARY, take(len(TEMPORARY))))
    x0, x1, x2, cot, dx1, small, sums, keep_tile, give_tile = take(9)
    rb, sbuf, kbuf, rv, zbuf, zr1, part, zs2, zr2, ybuf, r3, fbuf, sb, sr, late_got = take(15)
    (
        load_sem, piece_sem, store_sem, spill_sem, in_sem, out_sem, out_recv, w_send, w_recv, small_sem,
        give_send, give_recv, rb_sem, rv_sem, s1_send, s1_recv, z1_send, z1_recv,
        z2_send, z2_recv, s3_send, s3_recv, push_send, push_recv, sum_send, sum_recv, back_sem, back_recv, late_sems,
    ) = take(29)

    me = lax.axis_index(SECTION_AXIS)
    z = lax.axis_index(SHARD_AXIS)
    r = lax.axis_index(REPLICA_AXIS)
    other = 1 - me
    x_at, y_at = lax.rem(r, 2), lax.div(r, 2)
    x_near, y_near = r + 1 - 2 * x_at, r + 2 - 4 * y_at
    half = (1 - me) * x_at + me * y_at
    half_two = (1 - me) * y_at + me * x_at
    first_near = (1 - me) * x_near + me * y_near
    second_near = (1 - me) * y_near + me * x_near
    is_end = lax.rem(z, 3) == 0
    is_middle = jnp.logical_not(is_end)
    partner = (other, z, r)
    z_near = z + 1 - 2 * lax.rem(z, 2)

    def local(src, dst, sem):
        return pltpu.make_async_copy(src, dst, sem)

    def remote(src, dst, send, recv, device):
        return pltpu.make_async_remote_copy(
            src_ref=src, dst_ref=dst, send_sem=send, recv_sem=recv, device_id=device, device_id_type=MESH
        )

    own_rows = pl.ds(pl.multiple_of(me * ROWS, ROWS), ROWS)
    load_frames = local(frames.at[own_rows], x0, in_sem.at[0])
    load_cot = local(cotangent.at[own_rows], cot, in_sem.at[1])

    def weight_near(k):
        return local(weight_in[k].at[0], w[k], load_sem.at[WEIGHTS.index(k)])

    def weight_got(k):
        return local(weight_far[k], w[k], load_sem.at[WEIGHTS.index(k)])

    def piece(ref, k, i):
        if k == "o":
            return ref
        if k == DOWN:
            return ref.at[i * D : (i + 1) * D]
        if k == "up":
            return ref.at[:, i * D : (i + 1) * D]
        start = (i % 3) * D + (i // 3) * TILE
        return ref.at[:, start : start + TILE]

    near_piece, far_piece, far_store = {}, {}, {}
    for number, (k, i) in enumerate(PIECES):
        source = piece(weight_in[k].at[0], k, i)
        near_piece[k, i] = local(source, piece(w[k], k, i), piece_sem.at[number])
        device = partner if k != DOWN else [partner, (other, z, x_near), (other, z, y_near), (other, z_near, r)][i]
        far_piece[k, i] = remote(source, piece(w[k], k, i), w_send.at[number], w_recv.at[number], device)
        far_store[k, i] = remote(source, piece(weight_far[k], k, i), w_send.at[number], w_recv.at[number], partner)
    small_send = remote(small.at[me], small.at[me], small_sem.at[0], small_sem.at[1], partner)

    load_frames.start()

    @pl.when(me == 0)
    def _():
        for key in PIECES:
            near_piece[key].start()

    small[me, 0:4] = width_in[0]
    for i in range(4):
        small[me, 4 + i : 5 + i] = hidden_in[0:1, i * D : (i + 1) * D]
    small[me, 8:10] = gain_in[0]
    small[me, 10:12] = shift_in[0]
    for i in range(2):
        small[me, 12 + i : 13 + i] = jnp.broadcast_to(keep_in[0:1, i : i + 1].astype(F32), (1, D))
    small[me, 14:16] = jnp.zeros((2, D), F32)

    barrier = pltpu.get_barrier_semaphore()
    greeted = [partner, (me, z, x_near), (me, z, y_near), (other, z, x_near), (other, z, y_near), (other, z_near, r)]
    for device in greeted:
        pl.semaphore_signal(barrier, inc=1, device_id=device, device_id_type=MESH)
    for step in (1, 2):

        @pl.when(z + step < 4)
        def _(step=step):
            pl.semaphore_signal(barrier, inc=1, device_id=(me, z + step, r), device_id_type=MESH)

        @pl.when(z >= step)
        def _(step=step):
            pl.semaphore_signal(barrier, inc=1, device_id=(me, z - step, r), device_id_type=MESH)

    pl.semaphore_wait(barrier, len(greeted) + 2 + lax.rem(lax.div(z + 1, 2), 2))

    small_send.start()

    @pl.when(me == 0)
    def _():
        for key in PIECES:
            far_piece[key].start()

    @pl.when(me == 1)
    def _():
        for key in PIECES:
            far_store[key].start()

    load_cot.start()
    sums[...] = jnp.zeros_like(sums)
    label = label_columns([segments[pl.ds(4 * me + i, 1), :].astype(F32) for i in range(4)])
    valid = jnp.where(label[:, 0:1] >= 0.0, 1.0, 0.0)

    def spilled(k):
        return local(s[k], spill[k], spill_sem.at[list(SAVED).index(k)])

    def saved_load(k):
        return local(spill[k], s[k], spill_sem.at[list(SAVED).index(k)])

    def store_weight(k):
        return local(w[k], weight_far[k], store_sem.at[WEIGHTS.index(k)])

    def store_start(k):
        @pl.when(me == 1)
        def _():
            store_weight(k).start()

    def next_weight(k):
        @pl.when(me == 0)
        def _():
            for key in PIECES:
                if key[0] == k:
                    far_store[key].wait_recv()
            weight_got(k).start()

        @pl.when(me == 1)
        def _():
            store_weight(k).wait()
            weight_near(k).start()

    def first_weight(k):
        @pl.when(me == 0)
        def _():
            weight_near(k).start()

        @pl.when(me == 1)
        def _():
            weight_got(k).start()

    def weight_wait(k):
        weight_near(k).wait()

    def piece_wait(k, i):
        @pl.when(me == 0)
        def _():
            near_piece[k, i].wait()

        @pl.when(me == 1)
        def _():
            far_piece[k, i].wait_recv()

    def hook0(point, i=None):
        if point == "part":
            if i == 0:
                load_frames.wait()
                small_send.wait()
            for j in range(3):
                piece_wait(QKV, 3 * i + j)
        elif point == QKV:
            store_start(QKV)
            spilled(QKV).start()
        elif point == "attention":
            next_weight(QKV)
            spilled("mixed").start()
            spilled("aug").start()
            piece_wait("o", 0)
        elif point == "first":
            store_start("o")
            spilled("n1").start()
            spilled("hid").start()
            for i in range(4):
                piece_wait("up", i)
        elif point == "up":
            next_weight("o")
            store_start("up")
            spilled("act").start()
            spilled("slope").start()
            for i in range(4):
                piece_wait(DOWN, i)
        elif point == "second":
            store_start(DOWN)
            spilled("n2").start()
            spilled("scales").start()

    def hook1(point, i=None):
        if point == "part":
            if i == 0:
                spilled(QKV).wait()
                weight_wait(QKV)
        elif point == QKV:
            next_weight("up")
            spilled("mixed").wait()
            spilled("aug").wait()
        elif point == "attention":
            next_weight(DOWN)
            spilled("n1").wait()
            spilled("hid").wait()
            spilled("scales").wait()
            weight_wait("o")
        elif point == "first":
            spilled("act").wait()
            spilled("slope").wait()
            weight_wait("up")
        elif point == "up":
            spilled("n2").wait()
            weight_wait(DOWN)

    def keep_of(layer):
        return jnp.where(me == 0, small[layer, 12:13, 0:1], small[layer, 13:14, 0:1])

    def out_copy(src, layer, buffer, send, recv, start):
        here = local(src, buffer.at[own_rows], send.at[layer])
        there = remote(src, buffer.at[own_rows], send.at[layer], recv, partner)

        @pl.when(me == layer)
        def _():
            here.start() if start else here.wait()

        @pl.when(me != layer)
        def _():
            there.start() if start else there.wait_send()

    def layer_result(x, layer):
        result = s["n2"][...] * small[layer, 9:10, :] + small[layer, 11:12, :]
        kept = jnp.where(keep_of(layer) > 0.5, result, x[...].astype(F32))
        return (valid * kept).astype(BF16)

    forward(x0, label, w, small.at[0], s, hook0, 3)
    x1[...] = layer_result(x0, 0)
    out_copy(x1, 0, layer_out, out_sem, out_recv.at[0], True)
    forward(x1, label, w, small.at[1], s, hook1, 1)

    def give_copy(c):
        slot = lax.rem(c, 4)
        return remote(give_tile.at[slot], given.at[c], give_send.at[slot], give_recv.at[c], partner)

    def load_given(c):
        return local(given.at[c], rb.at[lax.rem(c, 4)], rb_sem.at[lax.rem(c, 4)])

    def copy_first(c):
        a = lax.rem(c, AHEAD)
        return remote(sbuf.at[a], firsts.at[c], s1_send.at[a], s1_recv.at[c], (me, z, first_near))

    def load_first(c):
        return local(firsts.at[c], rv.at[lax.rem(c, 2)], rv_sem.at[lax.rem(c, 2)])

    def copy_end(c, high=SHARE):
        a, b = lax.rem(c, 4), lax.rem(c, SLOTS)
        rows = pl.ds(pl.multiple_of(high - high * lax.div(z, 3), high), 3 * high)
        return remote(
            zbuf.at[a, rows], zr1.at[b, pl.ds(0, 3 * high)], z1_send.at[a], z1_recv.at[b], (me, 1 + lax.div(z, 3), r)
        )

    def copy_middle(c, high=SHARE):
        a, b = lax.rem(c, 4), lax.rem(c, SLOTS)
        rows = pl.ds(pl.multiple_of(3 * high * lax.div(z, 2), high), high)
        return remote(
            zbuf.at[a, rows], zr1.at[b, pl.ds(0, high)], z1_send.at[a], z1_recv.at[b], (me, 3 * lax.div(z, 2), r)
        )

    def copy_across(c, which, high=SHARE):
        a, b = lax.rem(c, 4), lax.rem(c, FAR_SLOTS)
        far = 3 - z if which == 0 else 3 - 3 * lax.div(z, 2)
        rows = pl.ds(0, high)
        return remote(zs2.at[a, which, rows], zr2.at[b, rows], z2_send.at[a, which], z2_recv.at[b], (me, far, r))

    def copy_second(c, high=SHARE):
        a, b = lax.rem(c, RESULTS), lax.rem(c, WIDE_SLOTS)
        rows = pl.ds(0, high)
        return remote(ybuf.at[a, rows], r3.at[b, rows], s3_send.at[a], s3_recv.at[b], (me, z, second_near))

    def copy_halved(c):
        i = c - FIRST_LATE
        source = sbuf.at[lax.rem(c, AHEAD), pl.ds(0, 4 * HALF_SHARE)]
        return remote(source, late_got.at[i], late_sems.at[0, i], late_sems.at[1, i], (me, z, second_near))

    def push(c, start):
        a = lax.rem(c, RESULTS)
        layer = 1 - lax.div(c, LAYER_CHUNKS)
        place = lax.rem(c, LAYER_CHUNKS)
        cols = pl.ds(pl.multiple_of((2 * (2 * place + me) + half) * 128, 128), 128)
        here = local(fbuf.at[a], shares.at[:, cols], push_send.at[a, 0])
        beside = remote(fbuf.at[a], shares.at[:, cols], push_send.at[a, 0], push_recv.at[0, place], partner)
        near_same = remote(
            fbuf.at[a], shares.at[:, cols], push_send.at[a, 1], push_recv.at[1, place], (me, z, first_near)
        )
        near_other = remote(
            fbuf.at[a], shares.at[:, cols], push_send.at[a, 1], push_recv.at[2, place], (other, z, first_near)
        )

        @pl.when(layer == me)
        def _():
            here.start() if start else here.wait()
            near_same.start() if start else near_same.wait_send()

        @pl.when(layer != me)
        def _():
            beside.start() if start else beside.wait_send()
            near_other.start() if start else near_other.wait_send()

    def within(c, first, after):
        return (c >= first) & (c < after)

    def across_stage(c, high):
        a, b = lax.rem(c, 4), lax.rem(c, SLOTS)
        rows = pl.ds(0, high)

        @pl.when(is_end)
        def _():
            copy_end(c, high).wait_send()
            copy_middle(c, high).wait_recv()
            own = pl.ds(pl.multiple_of(z * high, high), high)
            part[a, rows] = zbuf[a, own].astype(F32) + zr1[b, rows].astype(F32)

        @pl.when(is_middle)
        def _():
            copy_middle(c, high).wait_send()
            copy_end(c, high).wait_recv()
            low_row = high * (2 - z)

            def sum_of(row):
                row = pl.multiple_of(row, high)
                mine = zbuf[a, pl.ds(pl.multiple_of(low_row + row, high), high)]
                return mine.astype(F32) + zr1[b, pl.ds(row, high)].astype(F32)

            zs2[a, 0, rows] = sum_of(jnp.int32(high)).astype(BF16)
            zs2[a, 1, rows] = sum_of(2 * high * (2 - z)).astype(BF16)
            copy_across(c, 0, high).start()
            copy_across(c, 1, high).start()
            part[a, rows] = sum_of(2 * high * (z - 1))

    def along_stage(c, high):
        @pl.when(is_end)
        def _():
            copy_end(c, high).start()

        @pl.when(is_middle)
        def _():
            copy_middle(c, high).start()

    def second_stage(c, high):
        a, b = lax.rem(c, 4), lax.rem(c, FAR_SLOTS)
        rows = pl.ds(0, high)

        @pl.when(is_middle)
        def _():
            copy_across(c, 0, high).wait_send()
            copy_across(c, 1, high).wait_send()

        copy_across(c, 0, high).wait_recv()
        ybuf[lax.rem(c, RESULTS), rows] = (part[a, rows] + zr2[b, rows].astype(F32)).astype(BF16)
        copy_second(c, high).start()

    def late(now):
        @pl.when(within(now - STEP[4], FIRST_LATE, CHUNKS))
        def _():
            c = now - STEP[4]
            a, b = lax.rem(c, RESULTS), lax.rem(c, WIDE_SLOTS)
            copy_second(c, HALF_SHARE).wait()
            push(c - RESULTS, False)
            fbuf[a, pl.ds(pl.multiple_of(HALF_SHARE * half_two, 32), HALF_SHARE)] = ybuf[a, :HALF_SHARE]
            fbuf[a, pl.ds(pl.multiple_of(HALF_SHARE * (1 - half_two), 32), HALF_SHARE)] = r3[b, :HALF_SHARE]
            push(c, True)

        @pl.when(within(now - STEP[3], FIRST_LATE, CHUNKS))
        def _():
            second_stage(now - STEP[3], HALF_SHARE)

        @pl.when(within(now - STEP[2], FIRST_LATE, CHUNKS))
        def _():
            across_stage(now - STEP[2], HALF_SHARE)

        @pl.when(within(now - STEP[1], FIRST_LATE, CHUNKS))
        def _():
            c = now - STEP[1]
            kept = kbuf[lax.rem(c, AHEAD), : 4 * HALF_SHARE].astype(F32)
            copy_halved(c).wait()
            zbuf[lax.rem(c, 4), : 4 * HALF_SHARE] = (kept + late_got[c - FIRST_LATE].astype(F32)).astype(BF16)
            along_stage(c, HALF_SHARE)

        @pl.when(within(now - STEP[0], FIRST_LATE, CHUNKS))
        def _():
            c = now - STEP[0]
            k, d = lax.rem(c, AHEAD), lax.rem(c, 2)
            load_first(c).wait()
            for j in range(4):
                to = slice(j * HALF_SHARE, (j + 1) * HALF_SHARE)
                given_rows = pl.ds(pl.multiple_of(j * SHARE + HALF_SHARE * (1 - half_two), 32), HALF_SHARE)
                kept_rows = pl.ds(pl.multiple_of(j * SHARE + HALF_SHARE * half_two, 32), HALF_SHARE)
                sbuf[k, to] = (kbuf[k, given_rows].astype(F32) + rv[d, given_rows].astype(F32)).astype(BF16)
                kbuf[k, to] = (kbuf[k, kept_rows].astype(F32) + rv[d, kept_rows].astype(F32)).astype(BF16)
            copy_halved(c).start()

    def comm(now):
        @pl.when(within(now - LAST_STEP, 0, FIRST_LATE))
        def _():
            c = now - LAST_STEP
            a, b = lax.rem(c, RESULTS), lax.rem(c, WIDE_SLOTS)
            copy_second(c).wait()

            @pl.when(c >= RESULTS)
            def _():
                push(c - RESULTS, False)

            fbuf[a] = ybuf[a] + r3[b]
            push(c, True)

        @pl.when(within(now - STEP[2], 0, FIRST_LATE))
        def _():
            second_stage(now - STEP[2], SHARE)

        @pl.when(within(now - STEP[1], 0, FIRST_LATE))
        def _():
            across_stage(now - STEP[1], SHARE)

        @pl.when(within(now - STEP[0], 0, FIRST_LATE))
        def _():
            c = now - STEP[0]
            a, d, k = lax.rem(c, 4), lax.rem(c, 2), lax.rem(c, AHEAD)
            load_first(c).wait()
            zbuf[a] = kbuf[k] + rv[d]
            along_stage(c, SHARE)

        @pl.when(within(now, 0, CHUNKS))
        def _():
            copy_first(now).wait()
            load_first(now).start()

    def take_given(c):
        give_copy(c).wait_recv()
        load_given(c).start()

    def halve(c):
        k, d, e = lax.rem(c, AHEAD), lax.rem(c, 4), lax.rem(c, KEPT)
        load_given(c).wait()
        sbuf[k] = keep_tile[e, 1 - half] + rb[d, 1 - half]
        copy_first(c).start()
        kbuf[k] = keep_tile[e, half] + rb[d, half]

    place, steps = [0], [0]
    made_at, taken_at, halved = [], [], [0]

    def feed(rush=False):
        place[0] += 1
        soon = halved[0] < steps[0] + (AHEAD - 1 if rush else LOOK)
        if soon and halved[0] < len(taken_at) and (rush or place[0] - taken_at[halved[0]] >= (USE if halved[0] > 1 else 1)):
            halve(jnp.int32(halved[0]))
            halved[0] += 1
        free = len(taken_at) < halved[0] + 4
        wait = TAKE if len(taken_at) > 1 else 2
        if free and len(taken_at) < len(made_at) and (rush or place[0] - made_at[len(taken_at)] >= wait):
            take_given(jnp.int32(len(taken_at)))
            taken_at.append(place[0])

    def run_layer(layer, upstream, passed, x, ticks, wait, done):
        first_tile = 0 if layer == 1 else LAYER_TILES

        def put(c, tile, value):
            @pl.when(me == tile)
            def _():
                for i in range(2):
                    keep_tile[lax.rem(c, KEPT), i] = value[:, i * 128 : (i + 1) * 128]

            @pl.when(me != tile)
            def _():
                @pl.when(c >= 4)
                def _():
                    give_copy(c - 4).wait_send()

                for i in range(2):
                    give_tile[lax.rem(c, 4), i] = value[:, i * 128 : (i + 1) * 128]
                give_copy(c).start()

        def single(k, left, right, j):
            q = first_tile + FIRST_TILE[k] + j
            put(q // 2, q % 2, nn(left[...], right[:, j * TILE : (j + 1) * TILE]).astype(BF16))

        def grad(k, left, right):
            marks = ticks.get(k, {})
            first = FIRST_TILE[k] % 2
            begin = (first_tile + FIRST_TILE[k] + first) // 2
            n = (TILES[k] - first) // 2
            if first:
                single(k, left, right, 0)
                made_at.append(place[0])


            for j in range(n):
                c = jnp.int32(begin + j)
                assert begin + j - KEPT < halved[0]
                cols = slice((2 * j + first) * TILE, (2 * j + first + 2) * TILE)
                g = nn(left[...], right[:, cols]).astype(BF16)
                put(c, 0, g[:, :TILE])
                put(c, 1, g[:, TILE:])
                made_at.append(place[0])
                feed()
                if j in marks:
                    comm(jnp.int32(marks[j]))
                    steps[0] = marks[j] + 1
            if (TILES[k] - first) % 2:
                single(k, left, right, TILES[k] - 1)

        def tick(point, index=None):
            if point != "pairs":
                feed()
            if point in ("hidden", "mixed", "end"):
                feed()
            marks = ticks.get(point)
            if isinstance(marks, dict):
                marks = marks.get(index)
            if point == "pairs":
                comm(marks + index)
                steps[0] = marks + 3
            elif marks is not None:
                for number in marks if isinstance(marks, tuple) else (marks,):
                    comm(jnp.int32(number))
                    steps[0] = number + 1

        sm = small.at[layer]
        keep = keep_of(layer)

        def extra():
            if layer == 1:
                x2[...] = layer_result(x1, 1)
                out_copy(x2, 1, layer_out, out_sem, out_recv.at[0], True)

        def masked():
            return upstream[...].astype(F32) * (valid * keep)

        def last(value):
            passed[...] = value + upstream[...].astype(F32) * (valid * (1.0 - keep))

        backward(masked, label, w, sm, s, x, t, sums.at[layer], grad, tick, wait, done, last, extra)

    def wait1(k):
        pass

    def done1(k):
        if k in WEIGHTS:
            first_weight(k)
        elif k == "saved_qkv":
            saved_load(QKV).start()
        else:
            saved_load(k).start()

    def wait0(k):
        if k in WEIGHTS:
            weight_wait(k)
        elif k == "saved_qkv":
            saved_load(QKV).wait()
        else:
            saved_load(k).wait()

    load_cot.wait()
    run_layer(1, cot, dx1, x1, TICKS[0], wait1, done1)
    out_copy(dx1, 1, input_back, back_sem, back_recv.at[0], True)
    run_layer(0, dx1, s["n1"], x0, TICKS[1], wait0, lambda k: None)
    out_copy(s["n1"], 0, input_back, back_sem, back_recv.at[0], True)

    while halved[0] < min(CHUNKS, steps[0] + AHEAD - 1):
        feed(True)
    while len(taken_at) < CHUNKS:
        feed(True)
    rest = halved[0]

    def sum_copy(step):
        if step == 0:
            return remote(sums.at[other], sr.at[0], sum_send.at[0], sum_recv.at[0], partner)
        z_two = lax.rem(z + 2, 4)
        device = [(me, z, x_near), (me, z, y_near), (me, z_near, r), (me, z_two, r)][step - 1]
        return remote(sb.at[step - 1], sr.at[step], sum_send.at[step], sum_recv.at[step], device)

    sum_copy(0).start()

    def final(now):
        for step in range(5):

            @pl.when(now == SUM_TICKS[step])
            def _(step=step):
                sum_copy(step).wait()
                if step == 0:
                    sb[0] = sums[me] + sr[0]
                else:
                    sb[step] = sb[step - 1] + sr[step]
                if step < 4:
                    sum_copy(step + 1).start()

        late(now)
        comm(now)

        @pl.when(within(now + AHEAD - 1, rest, CHUNKS))
        def _():
            halve(now + AHEAD - 1)

    times(SUM_TICKS[0], max(CHUNKS + STEP[4], FIRST_LATE + LAST_STEP), final)
    small_out[...] = sb[4]

    times(CHUNKS - RESULTS, CHUNKS, lambda c: push(c, False))
    for stream in range(3):

        def arrived(place, stream=stream):
            remote(
                fbuf.at[0], shares.at[:, pl.ds(0, 128)], push_send.at[0, 0], push_recv.at[stream, place], partner
            ).wait_recv()

        times(0, LAYER_CHUNKS, arrived)
    times(CHUNKS - 4, CHUNKS, lambda c: give_copy(c).wait_send())
    for key in PIECES:
        far_piece[key].wait_send()
    out_copy(x1, 0, layer_out, out_sem, out_recv.at[0], False)
    out_copy(x2, 1, layer_out, out_sem, out_recv.at[0], False)
    out_copy(dx1, 1, input_back, back_sem, back_recv.at[0], False)
    out_copy(s["n1"], 0, input_back, back_sem, back_recv.at[0], False)
    remote(x1, layer_out.at[own_rows], out_sem.at[0], out_recv.at[0], partner).wait_recv()
    remote(dx1, input_back.at[own_rows], back_sem.at[0], back_recv.at[0], partner).wait_recv()


TICKS = (
    {"up_back": {1: 0, 2: 1}, "up": {0: 2, 3: 3}, "hidden": 4, "mixed": 5, "pairs": 6, QKV: {3: 9}, "end": 10},
    {DOWN: {2: 11, 5: 12}, "up_back": {1: 13, 3: 14}, "up": {2: 15, 5: 16}, "hidden": 17, "mixed": 18, "pairs": 19, QKV: {3: 22}, "end": 23},
)
SUM_TICKS = (24, 36, 40, 44, 48)
PIECES = [(QKV, i) for i in range(9)] + [("o", 0)] + [("up", i) for i in range(4)] + [(DOWN, i) for i in range(4)]


def any_space():
    return pl.BlockSpec(memory_space=pl.ANY)


def in_vmem():
    return pl.BlockSpec(memory_space=pltpu.VMEM)


def run_whole(*arguments):
    shape = jax.ShapeDtypeStruct
    outs = [
        shape((2 * ROWS, D), BF16),
        shape((2 * ROWS, D), F32),
        shape((SHARE, LAYER_TILES * TILE), BF16),
        shape((16, D), F32),
    ]
    outs += [shape(WEIGHT_SHAPE[k], BF16) for k in WEIGHTS]
    outs += [shape((CHUNKS, 2, D, 128), BF16), shape((CHUNKS, D, 128), BF16)]
    outs += [shape(*SAVED[k]) for k in SAVED]
    out_specs = [any_space()] * 3 + [in_vmem()] + [any_space()] * (len(outs) - 4)
    dma = pltpu.SemaphoreType.DMA
    scratch = [pltpu.VMEM(WEIGHT_SHAPE[k], BF16) for k in WEIGHTS]
    scratch += [pltpu.VMEM(*SAVED[k]) for k in SAVED]
    scratch += [pltpu.VMEM(*TEMPORARY[k]) for k in TEMPORARY]
    scratch += [pltpu.VMEM((ROWS, D), BF16)] * 4
    scratch += [
        pltpu.VMEM((ROWS, D), F32),
        pltpu.VMEM((2, 16, D), F32),
        pltpu.VMEM((2, 16, D), F32),
        pltpu.VMEM((KEPT, 2, D, 128), BF16),
        pltpu.VMEM((4, 2, D, 128), BF16),
        pltpu.VMEM((4, 2, D, 128), BF16),
        pltpu.VMEM((AHEAD, D, 128), BF16),
        pltpu.VMEM((AHEAD, D, 128), BF16),
        pltpu.VMEM((2, D, 128), BF16),
        pltpu.VMEM((4, D, 128), BF16),
        pltpu.VMEM((SLOTS, 3 * SHARE, 128), BF16),
        pltpu.VMEM((4, SHARE, 128), F32),
        pltpu.VMEM((4, 2, SHARE, 128), BF16),
        pltpu.VMEM((FAR_SLOTS, SHARE, 128), BF16),
        pltpu.VMEM((RESULTS, SHARE, 128), BF16),
        pltpu.VMEM((WIDE_SLOTS, SHARE, 128), BF16),
        pltpu.VMEM((RESULTS, SHARE, 128), BF16),
        pltpu.VMEM((5, 16, D), F32),
        pltpu.VMEM((5, 16, D), F32),
        pltpu.VMEM((LATE, 4 * HALF_SHARE, 128), BF16),
    ]
    n = len(PIECES)
    sems = [
        (4,), (n,), (4,), (len(SAVED),), (2,), (2,), (1,), (n,), (n,), (2,),
        (4,), (CHUNKS,), (4,), (2,), (AHEAD,), (CHUNKS,), (4,), (SLOTS,),
        (4, 2), (FAR_SLOTS,), (RESULTS,), (WIDE_SLOTS,), (RESULTS, 2), (3, LAYER_CHUNKS), (5,), (5,), (2,), (1,), (2, LATE),
    ]
    scratch += [dma(n) for n in sems]
    got = pl.pallas_call(
        whole_step,
        out_shape=outs,
        in_specs=[any_space()] * 2 + [in_vmem()] * 6 + [any_space()] * 4,
        out_specs=out_specs,
        scratch_shapes=scratch,
        compiler_params=pltpu.CompilerParams(
            collective_id=0, has_side_effects=True, vmem_limit_bytes=64 * 2**20 - 2**17
        ),
        name="whole_step",
    )(*arguments)
    return got[:4]


def finish_step(layer_out, input_back, shares, sums, *refs):
    out_layer, out_back, out_qkv, out_o, out_up, out_down, width, hidden, gain, shift = refs[:10]
    held, big_qkv, big_o, big_up, big_down, rows_low, rows_wide, sem = refs[10:]
    big = {QKV: big_qkv, "o": big_o, "up": big_up, DOWN: big_down}
    out = {QKV: out_qkv, "o": out_o, "up": out_up, DOWN: out_down}
    order = (DOWN, "up", QKV, "o")
    cols = {k: slice(FIRST_TILE[k] * TILE, (FIRST_TILE[k] + TILES[k]) * TILE) for k in order}
    load = {k: pltpu.make_async_copy(shares.at[:, cols[k]], held.at[:, cols[k]], sem.at[i]) for i, k in enumerate(order)}
    store = {k: pltpu.make_async_copy(big[k], out[k].at[0], sem.at[4 + i]) for i, k in enumerate(order)}
    through = [(layer_out, rows_low, out_layer), (input_back, rows_wide, out_back)]
    into = [pltpu.make_async_copy(a, b, sem.at[8 + i]) for i, (a, b, _) in enumerate(through)]
    onward = [pltpu.make_async_copy(b, c.at[0], sem.at[10 + i]) for i, (_, b, c) in enumerate(through)]
    for k in order:
        load[k].start()
    for copy in into:
        copy.start()
    for k in order:
        load[k].wait()
        big[k][...] = held[:, cols[k]].astype(F32)
        store[k].start()
    for one, two in zip(into, onward):
        one.wait()
        two.start()
    z = lax.axis_index(SHARD_AXIS)
    for i in range(4):

        @pl.when(z == i)
        def _(i=i):
            mine = slice(i * SHARE, (i + 1) * SHARE)
            width[0] = sums[0:4, mine]
            hidden[...] = sums[4 + i : 5 + i, :]
            gain[0] = sums[8:10, mine]
            shift[0] = sums[10:12, mine]

    for k in order:
        store[k].wait()
    for copy in onward:
        copy.wait()


def run_finish(layer_out, input_back, shares, sums):
    shape = jax.ShapeDtypeStruct
    outs = [shape((1, 2 * ROWS, D), BF16), shape((1, 2 * ROWS, D), F32), shape((1, SHARE, 3 * D), F32)]
    outs += [shape((1, SHARE, D), F32), shape((1, SHARE, FF), F32), shape((1, SHARE, FF), F32)]
    outs += [shape((1, 4, SHARE), F32), shape((1, D), F32), shape((1, 2, SHARE), F32), shape((1, 2, SHARE), F32)]
    return pl.pallas_call(
        finish_step,
        out_shape=outs,
        in_specs=[any_space()] * 3 + [in_vmem()],
        out_specs=[any_space()] * 6 + [in_vmem()] * 4,
        scratch_shapes=[
            pltpu.VMEM((SHARE, LAYER_TILES * TILE), BF16),
            pltpu.VMEM((SHARE, 3 * D), F32),
            pltpu.VMEM((SHARE, D), F32),
            pltpu.VMEM((SHARE, FF), F32),
            pltpu.VMEM((SHARE, FF), F32),
            pltpu.VMEM((2 * ROWS, D), BF16),
            pltpu.VMEM((2 * ROWS, D), F32),
            pltpu.SemaphoreType.DMA((12,)),
        ],
        compiler_params=pltpu.CompilerParams(vmem_limit_bytes=64 * 2**20 - 2**17),
        name="finish_step",
    )(layer_out, input_back, shares, sums)


def on_device_block(
    frames, cotangent, segments, layer_keep, joint_weight, output_weight, up_weight, down_weight,
    width_bias, hidden_bias, norm_gain, norm_shift,
):
    got = run_whole(
        frames, cotangent, segments.reshape(8, 128), layer_keep, width_bias, hidden_bias, norm_gain, norm_shift,
        joint_weight, output_weight, up_weight, down_weight,
    )
    outs = list(run_finish(*got))
    outs[5] = jnp.transpose(outs[5], (0, 2, 1))
    return tuple(outs)


def solution(mesh):
    sizes = dict(mesh.shape)
    fits = sizes == {SECTION_AXIS: 2, SHARD_AXIS: 4, REPLICA_AXIS: 4}
    placed = (
        P((SHARD_AXIS, REPLICA_AXIS), None),
        P((SHARD_AXIS, REPLICA_AXIS), None),
        P((SHARD_AXIS, REPLICA_AXIS)),
        P(SECTION_AXIS, (SHARD_AXIS, REPLICA_AXIS)),
        P(SECTION_AXIS, None, None),
        P(SECTION_AXIS, None, None),
        P(SECTION_AXIS, None, None),
        P(SECTION_AXIS, None, None),
        P(SECTION_AXIS, None, None),
        P(SECTION_AXIS, None),
        P(SECTION_AXIS, None, None),
        P(SECTION_AXIS, None, None),
    )
    return jax.shard_map(
        on_device_block if fits else on_device_general,
        mesh=mesh,
        in_specs=placed,
        out_specs=(
            P(SECTION_AXIS, (SHARD_AXIS, REPLICA_AXIS), None),
            P(SECTION_AXIS, (SHARD_AXIS, REPLICA_AXIS), None),
            P(SECTION_AXIS, SHARD_AXIS, None),
            P(SECTION_AXIS, SHARD_AXIS, None),
            P(SECTION_AXIS, SHARD_AXIS, None),
            P(SECTION_AXIS, None, SHARD_AXIS),
            P(SECTION_AXIS, None, SHARD_AXIS),
            P(SECTION_AXIS, SHARD_AXIS),
            P(SECTION_AXIS, None, SHARD_AXIS),
            P(SECTION_AXIS, None, SHARD_AXIS),
        ),
        check_vma=False,
    )
```

```python
import functools

import jax
import jax.numpy as jnp
from jax import lax
from jax.experimental import pallas as pl
from jax.experimental.pallas import tpu as pltpu
from jax.sharding import PartitionSpec as P

SECTION_AXIS, SHARD_AXIS, REPLICA_AXIS = "section", "shard", "replica"
QKV, DOWN = "qkv", "down"

HEADS = 12
HEAD_SIZE = 64
BATCH_ROWS = 512
BATCHES = 2


epsilon = 1e-05
masked_score = -1e30


def shifted(block, axis, distance):
    devices = range(lax.axis_size(axis))
    route = [(i - distance, i) for i in devices if i - distance in devices]
    return lax.ppermute(block, axis, route)


def layer_norm(value, gain, shift):
    centre = value - jnp.mean(value, axis=-1, keepdims=True)
    spread = jnp.mean(centre * centre, axis=-1, keepdims=True)
    return centre * lax.rsqrt(spread + epsilon) * gain + shift


def exact_gelu(value):
    return jax.nn.gelu(value, approximate=False)


def over_rows(left, right):
    return lax.dot_general(
        left, right, (((0,), (0,)), ((), ())), preferred_element_type=jnp.float32
    )


def against(left, right):
    return lax.dot_general(
        left, right, (((1,), (1,)), ((), ())), preferred_element_type=jnp.float32
    )


def split_heads(joint_low):
    rows = joint_low.shape[0]
    width = joint_low.shape[1] // 3
    query = joint_low[:, :width].reshape(rows, HEADS, HEAD_SIZE)
    keys = joint_low[:, width : 2 * width].reshape(rows, HEADS, HEAD_SIZE)
    values = joint_low[:, 2 * width :].reshape(rows, HEADS, HEAD_SIZE)
    return (query, keys, values)


def block_scores(query_part, keys, label_part, labels):
    scores = jnp.einsum(
        "qhd,khd->hqk", query_part, keys, preferred_element_type=jnp.float32
    ) * HEAD_SIZE ** (-0.5)
    allowed = label_part[:, None] == labels[None, :]
    return jnp.where(allowed[None], scores, masked_score)


def attend_forward(joint_low, labels):
    query, keys, values = split_heads(joint_low)
    rows = query.shape[0]
    block = min(512, rows)

    def one_block(start):
        scores = block_scores(query, keys, labels, labels)
        peak = jnp.max(scores, axis=-1, keepdims=True)
        raised = jnp.exp(scores - peak)
        total = jnp.sum(raised, axis=-1, keepdims=True)
        probs_low = (raised / total).astype(jnp.bfloat16)
        mixed = jnp.einsum("hqk,khd->qhd", probs_low, values, preferred_element_type=jnp.float32)
        return (mixed.reshape(block, HEADS * HEAD_SIZE), (peak + jnp.log(total))[..., 0])

    starts = jnp.arange(rows // block, dtype=jnp.int32) * block
    mixed, log_totals = lax.map(one_block, starts)
    return (mixed.reshape(rows, HEADS * HEAD_SIZE), log_totals)


def attend_backward(joint_low, labels, log_totals, mixed_back):
    query, keys, values = split_heads(joint_low)
    rows = query.shape[0]
    block = min(512, rows)
    back_heads = mixed_back.reshape(rows, HEADS, HEAD_SIZE)
    factor = HEAD_SIZE ** (-0.5)

    def one_block(carry, items):
        key_sum, value_sum = carry
        start, log_part = items
        scores = block_scores(query, keys, labels, labels)
        probs = jnp.exp(scores - log_part[..., None])
        probs_low = probs.astype(jnp.bfloat16)
        prob_back = jnp.einsum(
            "qhd,khd->hqk", back_heads, values, preferred_element_type=jnp.float32
        )
        inner = jnp.sum(prob_back * probs, axis=-1, keepdims=True)
        score_back = (probs * (prob_back - inner)).astype(jnp.bfloat16)
        query_back = (
            jnp.einsum("hqk,khd->qhd", score_back, keys, preferred_element_type=jnp.float32)
            * factor
        )
        key_sum = (
            key_sum
            + jnp.einsum("hqk,qhd->khd", score_back, query, preferred_element_type=jnp.float32)
            * factor
        )
        value_sum = value_sum + jnp.einsum(
            "hqk,qhd->khd", probs_low, back_heads, preferred_element_type=jnp.float32
        )
        return ((key_sum, value_sum), query_back.reshape(block, HEADS * HEAD_SIZE))

    starts = jnp.arange(rows // block, dtype=jnp.int32) * block
    empty = jnp.zeros((rows, HEADS, HEAD_SIZE), jnp.float32)
    (key_sum, value_sum), query_back = lax.scan(one_block, (empty, empty), (starts, log_totals))
    width = HEADS * HEAD_SIZE
    return jnp.concatenate(
        [
            query_back.reshape(rows, width),
            key_sum.reshape(rows, width),
            value_sum.reshape(rows, width),
        ],
        axis=1,
    )


def layer_forward(inputs, labels, params):
    (
        joint_weight,
        output_weight,
        up_weight,
        down_weight,
        width_bias,
        hidden_bias,
        norm_gain,
        norm_shift,
    ) = params
    width = inputs.shape[1]
    joint_bias = jnp.concatenate([width_bias[0], jnp.zeros((width,), jnp.float32), width_bias[1]])
    joint_low = (
        jnp.dot(inputs, joint_weight, preferred_element_type=jnp.float32) + joint_bias
    ).astype(jnp.bfloat16)
    mixed, log_totals = attend_forward(joint_low, labels)
    mixed_low = mixed.astype(jnp.bfloat16)
    first_sum = inputs.astype(jnp.float32) + (
        jnp.dot(mixed_low, output_weight, preferred_element_type=jnp.float32) + width_bias[2]
    )
    hidden = layer_norm(first_sum, norm_gain[0], norm_shift[0])
    hidden_low = hidden.astype(jnp.bfloat16)
    up_value = jnp.dot(hidden_low, up_weight, preferred_element_type=jnp.float32) + hidden_bias
    active_low = exact_gelu(up_value).astype(jnp.bfloat16)
    second_sum = hidden + (
        jnp.dot(active_low, down_weight, preferred_element_type=jnp.float32) + width_bias[3]
    )
    result = layer_norm(second_sum, norm_gain[1], norm_shift[1])
    return (
        result,
        (joint_low, log_totals, mixed_low, first_sum, hidden_low, up_value, active_low, second_sum),
    )


def empty_kept(rows, width, hidden_width):
    block = min(512, rows)
    return (
        jnp.zeros((rows, 3 * width), jnp.bfloat16),
        jnp.zeros((rows // block, HEADS, block), jnp.float32),
        jnp.zeros((rows, width), jnp.bfloat16),
        jnp.zeros((rows, width), jnp.float32),
        jnp.zeros((rows, width), jnp.bfloat16),
        jnp.zeros((rows, hidden_width), jnp.float32),
        jnp.zeros((rows, hidden_width), jnp.bfloat16),
        jnp.zeros((rows, width), jnp.float32),
    )


def layer_backward(inputs, labels, params, kept, upstream):
    (
        joint_weight,
        output_weight,
        up_weight,
        down_weight,
        width_bias,
        hidden_bias,
        norm_gain,
        norm_shift,
    ) = params
    joint_low, log_totals, mixed_low, first_sum, hidden_low, up_value, active_low, second_sum = kept
    width = inputs.shape[1]
    second_norm, second_pull = jax.vjp(layer_norm, second_sum, norm_gain[1], norm_shift[1])
    second_back, second_gain, second_shift = second_pull(upstream)
    branch_back = second_back.astype(jnp.bfloat16)
    down_part = over_rows(active_low, branch_back)
    down_bias = jnp.sum(branch_back.astype(jnp.float32), axis=0)
    active_back = against(branch_back, down_weight)
    gelu_value, gelu_pull = jax.vjp(exact_gelu, up_value)
    up_back = gelu_pull(active_back)[0].astype(jnp.bfloat16)
    up_part = over_rows(hidden_low, up_back)
    up_bias = jnp.sum(up_back.astype(jnp.float32), axis=0)
    hidden_back = second_back + against(up_back, up_weight)
    first_norm, first_pull = jax.vjp(layer_norm, first_sum, norm_gain[0], norm_shift[0])
    first_back, first_gain, first_shift = first_pull(hidden_back)
    attention_back = first_back.astype(jnp.bfloat16)
    output_part = over_rows(mixed_low, attention_back)
    output_bias = jnp.sum(attention_back.astype(jnp.float32), axis=0)
    mixed_back = against(attention_back, output_weight).astype(jnp.bfloat16)
    joint_back = attend_backward(joint_low, labels, log_totals, mixed_back).astype(jnp.bfloat16)
    joint_part = over_rows(inputs, joint_back)
    joint_bias = jnp.sum(joint_back.astype(jnp.float32), axis=0)
    passed = first_back + against(joint_back, joint_weight)
    width_part = jnp.stack([joint_bias[:width], joint_bias[2 * width :], output_bias, down_bias])
    gain_part = jnp.stack([first_gain, second_gain])
    shift_part = jnp.stack([first_shift, second_shift])
    return (
        passed,
        (joint_part, output_part, up_part, down_part, width_part, up_bias, gain_part, shift_part),
    )


def on_device_general(
    frames,
    cotangent,
    segments,
    layer_keep,
    joint_weight,
    output_weight,
    up_weight,
    down_weight,
    width_bias,
    hidden_bias,
    norm_gain,
    norm_shift,
):
    params = tuple(
        (
            array[0]
            for array in (
                joint_weight,
                output_weight,
                up_weight,
                down_weight,
                width_bias,
                hidden_bias,
                norm_gain,
                norm_shift,
            )
        )
    )
    section = lax.axis_index(SECTION_AXIS)
    rows = BATCH_ROWS
    number = BATCHES
    width = frames.shape[1]
    hidden_width = up_weight.shape[2]
    layer_out = jnp.zeros(frames.shape, jnp.bfloat16)
    stored = []
    previous = jnp.zeros((rows, width), jnp.bfloat16)
    for step in range(number + 1):
        arrived = shifted(previous, SECTION_AXIS, 1) if step > 0 else previous
        batch = step - section
        within = (batch >= 0) & (batch < number)
        place = jnp.clip(batch, 0, number - 1)
        start = place * rows
        inputs = jnp.where(section == 0, lax.dynamic_slice_in_dim(frames, start, rows, 0), arrived)
        labels = lax.dynamic_slice_in_dim(segments, start, rows, 0)
        valid = (labels >= 0).astype(jnp.float32)[:, None]
        flag = lax.dynamic_slice_in_dim(layer_keep[0], place, 1, 0)[0]
        running = within & (flag == 1)
        result, kept = lax.cond(
            running,
            lambda: layer_forward(inputs, labels, params),
            lambda: (inputs.astype(jnp.float32), empty_kept(rows, width, hidden_width)),
        )
        output = (valid * result).astype(jnp.bfloat16)
        earlier = lax.dynamic_slice_in_dim(layer_out, start, rows, 0)
        layer_out = lax.dynamic_update_slice_in_dim(
            layer_out, jnp.where(within, output, earlier), start, 0
        )
        previous = output
        stored.append((inputs, labels, running, start, within, kept))
    input_back = jnp.zeros(frames.shape, jnp.float32)
    totals = None
    sending = jnp.zeros((rows, width), jnp.float32)
    for step in range(number + 1):
        arrived = (
            shifted(sending.astype(jnp.bfloat16), SECTION_AXIS, -1).astype(sending.dtype)
            if step > 0
            else sending
        )
        entry = stored[number - step]
        inputs, labels, running, start, within = (entry[0], entry[1], entry[2], entry[3], entry[4])
        valid = (labels >= 0).astype(jnp.float32)[:, None]
        given = lax.dynamic_slice_in_dim(cotangent, start, rows, 0).astype(jnp.float32)
        upstream = valid * jnp.where(section == 1, given, arrived)

        def run_back():
            kept = entry[5]
            return layer_backward(inputs, labels, params, kept, upstream)

        def skip_back():
            return (upstream, tuple((jnp.zeros(item.shape, jnp.float32) for item in params)))

        passed, pieces = lax.cond(running, run_back, skip_back)
        earlier = lax.dynamic_slice_in_dim(input_back, start, rows, 0)
        input_back = lax.dynamic_update_slice_in_dim(
            input_back, jnp.where(within, passed, earlier), start, 0
        )
        sending = passed
        shares = pieces
        totals = (
            tuple(shares)
            if totals is None
            else tuple((left + right for left, right in zip(totals, shares)))
        )
    shares = (
        lax.psum_scatter(
            totals[0][None].astype(jnp.bfloat16), SHARD_AXIS, scatter_dimension=1, tiled=True
        ).astype(jnp.float32),
        lax.psum_scatter(
            totals[1][None].astype(jnp.bfloat16), SHARD_AXIS, scatter_dimension=1, tiled=True
        ).astype(jnp.float32),
        lax.psum_scatter(
            totals[2][None].astype(jnp.bfloat16), SHARD_AXIS, scatter_dimension=1, tiled=True
        ).astype(jnp.float32),
        lax.psum_scatter(
            totals[3][None].astype(jnp.bfloat16), SHARD_AXIS, scatter_dimension=2, tiled=True
        ).astype(jnp.float32),
        lax.psum_scatter(
            totals[4][None].astype(jnp.bfloat16), SHARD_AXIS, scatter_dimension=2, tiled=True
        ).astype(jnp.float32),
        lax.psum_scatter(
            totals[5][None].astype(jnp.bfloat16), SHARD_AXIS, scatter_dimension=1, tiled=True
        ).astype(jnp.float32),
        lax.psum_scatter(
            totals[6][None].astype(jnp.bfloat16), SHARD_AXIS, scatter_dimension=2, tiled=True
        ).astype(jnp.float32),
        lax.psum_scatter(
            totals[7][None].astype(jnp.bfloat16), SHARD_AXIS, scatter_dimension=2, tiled=True
        ).astype(jnp.float32),
    )
    reduced = (
        lax.psum(shares[0].astype(jnp.bfloat16), REPLICA_AXIS).astype(jnp.float32),
        lax.psum(shares[1].astype(jnp.bfloat16), REPLICA_AXIS).astype(jnp.float32),
        lax.psum(shares[2].astype(jnp.bfloat16), REPLICA_AXIS).astype(jnp.float32),
        lax.psum(shares[3].astype(jnp.bfloat16), REPLICA_AXIS).astype(jnp.float32),
        lax.psum(shares[4].astype(jnp.bfloat16), REPLICA_AXIS).astype(jnp.float32),
        lax.psum(shares[5].astype(jnp.bfloat16), REPLICA_AXIS).astype(jnp.float32),
        lax.psum(shares[6].astype(jnp.bfloat16), REPLICA_AXIS).astype(jnp.float32),
        lax.psum(shares[7].astype(jnp.bfloat16), REPLICA_AXIS).astype(jnp.float32),
    )
    return (
        layer_out[None],
        input_back[None],
        reduced[0],
        reduced[1],
        reduced[2],
        reduced[3],
        reduced[4],
        reduced[5],
        reduced[6],
        reduced[7],
    )


F32, BF16 = jnp.float32, jnp.bfloat16
MESH = pl.DeviceIdType.MESH
D, FF, ROWS, PAIRS = 768, 3072, 512, 6
SHARE = D // 4
TILE = 256
FIRST_TILE = {DOWN: 0, "up": 12, "o": 24, QKV: 27}
TILES = {DOWN: 12, "up": 12, "o": 3, QKV: 9}
LAYER_TILES = 36
LAYER_CHUNKS = LAYER_TILES // 2
CHUNKS = 2 * LAYER_CHUNKS
GAP = 3
STEP = [1 + GAP * i for i in range(5)]
SLOTS = 2 * GAP + 1
KEPT = 8
FAR_SLOTS = 3 * GAP + 1
WEIGHTS = (QKV, "o", "up", DOWN)
WEIGHT_SHAPE = {QKV: (D, 3 * D), "o": (D, D), "up": (D, FF), DOWN: (FF, D)}
SAVED = {
    QKV: ((ROWS, 3 * D), BF16),
    "mixed": ((ROWS, D), BF16),
    "aug": ((PAIRS, ROWS, 128), BF16),
    "n1": ((ROWS, D), F32),
    "scales": ((2, ROWS, 128), F32),
    "hid": ((ROWS, D), BF16),
    "act": ((ROWS, FF), BF16),
    "slope": ((ROWS, FF), BF16),
    "n2": ((ROWS, D), F32),
}
TEMPORARY = {
    "big": ((ROWS, D), F32),
    "low": ((ROWS, D), BF16),
    "left": ((D, ROWS), BF16),
    "mb": ((ROWS, D), BF16),
    "qb": ((ROWS, 3 * D), BF16),
}


def nn(a, b):
    return lax.dot_general(a, b, (((1,), (0,)), ((), ())), preferred_element_type=F32)


def nt(a, b):
    return lax.dot_general(a, b, (((1,), (1,)), ((), ())), preferred_element_type=F32)


def tn(a, b):
    return lax.dot_general(a, b, (((0,), (0,)), ((), ())), preferred_element_type=F32)


def half_lanes():
    return lax.broadcasted_iota(jnp.int32, (ROWS, 128), 1) < 64


def lane_place():
    return lax.broadcasted_iota(jnp.int32, (ROWS, 128), 1) % 64


def label_columns(rows):
    return jnp.concatenate([jnp.transpose(jnp.broadcast_to(row, (128, 128))) for row in rows], axis=0)


def mask_columns(label):
    place = lane_place()
    mine = place.astype(F32) == label + 1.0
    within = place < 17
    query = jnp.where(mine & within, 1.0, 0.0)
    keys = jnp.where(within & jnp.logical_not(mine), -1e30, 0.0)
    ones = jnp.where((place >= 20) & (place < 23), 1.0, 0.0)
    return query, keys + ones, ones


def three_parts(column, base):
    place = lane_place()
    first = column.astype(BF16).astype(F32)
    rest = column - first
    second = rest.astype(BF16).astype(F32)
    third = rest - second
    out = jnp.where(place == 20, first, base)
    out = jnp.where(place == 21, second, out)
    return jnp.where(place == 22, third, out)


def norm(total):
    mean = jnp.mean(total, axis=1, keepdims=True)
    centre = total - mean
    spread = jnp.mean(centre * centre, axis=1, keepdims=True)
    scale = lax.rsqrt(spread + 1e-05)
    return centre * scale, scale


def norm_back(upstream, normed, scale, gain):
    e = upstream * gain
    first = jnp.mean(e, axis=1, keepdims=True)
    second = jnp.mean(e * normed, axis=1, keepdims=True)
    return scale * (e - first - normed * second)


def gelu_both(v):
    cdf = 0.5 * (1.0 + lax.erf(v * 0.7071067811865476))
    return v * cdf, cdf + v * (jnp.exp(-0.5 * v * v) * 0.3989422804014327)


def column_sum(value):
    return jnp.sum(value, axis=0, keepdims=True)


def times(start, stop, body):
    lax.fori_loop(start, stop, lambda i, _: (body(i), 0)[1], 0)


def forward(x, label, w, sm, out, hook):
    for part in range(3):
        hook("part", part)
        acc = nn(x[...], w[QKV][:, part * D : part * D + D])
        if part == 0:
            acc = (acc + sm[0:1, :]).astype(BF16) * jnp.bfloat16(0.125)
        elif part == 2:
            acc = (acc + sm[1:2, :]).astype(BF16)
        else:
            acc = acc.astype(BF16)
        out[QKV][:, part * D : part * D + D] = acc
    hook(QKV)
    aq, ak, _ = mask_columns(label)
    aq16, ak16 = aq.astype(BF16), ak.astype(BF16)
    low = half_lanes()

    masks = [low, jnp.logical_not(low)]

    def pair(p):
        at = pl.multiple_of(p * 128, 128)
        qp = out[QKV][:, pl.ds(at, 128)]
        kp = out[QKV][:, pl.ds(D + at, 128)]
        vp = out[QKV][:, pl.ds(2 * D + at, 128)]
        scores = [nt(jnp.where(m, qp, aq16), jnp.where(m, kp, ak16)) for m in masks]
        res, lse = [], []
        for e in range(2):
            top = jnp.max(scores[e], axis=1, keepdims=True)
            raised = jnp.exp(scores[e] - top).astype(BF16)
            o = nn(raised, jnp.where(masks[e], vp, jnp.bfloat16(1.0)))
            total = o[:, 64:65] if e == 0 else o[:, 0:1]
            res.append(o * (1.0 / total))
            lse.append(-(top + jnp.log(total)))
        out["mixed"][:, pl.ds(at, 128)] = jnp.where(low, res[0], res[1]).astype(BF16)
        out["aug"][p] = three_parts(jnp.where(low, lse[1], lse[0]), aq).astype(BF16)

    def two_pairs(i):
        pair(2 * i)
        pair(2 * i + 1)

    times(0, PAIRS // 2, two_pairs)
    hook("attention")
    first = x[...].astype(F32) + nn(out["mixed"][...], w["o"][...]) + sm[2:3, :]
    n1, r1 = norm(first)
    out["n1"][...] = n1
    out["scales"][0] = jnp.broadcast_to(r1, (ROWS, 128))
    out["hid"][...] = (n1 * sm[8:9, :] + sm[10:11, :]).astype(BF16)
    hook("first")

    for j in range(4):
        hook("up_part", j)
        cols = slice(j * D, j * D + D)
        act, slope = gelu_both(nn(out["hid"][...], w["up"][:, cols]) + sm[4 + j : 5 + j, :])
        out["act"][:, cols] = act.astype(BF16)
        out["slope"][:, cols] = slope.astype(BF16)
    hook("up")
    hidden = out["n1"][...] * sm[8:9, :] + sm[10:11, :]
    second = hidden + nn(out["act"][...], w[DOWN][...]) + sm[3:4, :]
    n2, r2 = norm(second)
    out["n2"][...] = n2
    out["scales"][1] = jnp.broadcast_to(r2, (ROWS, 128))
    hook("second")
    return n2 * sm[9:10, :] + sm[11:12, :]


def backward(upstream, label, w, sm, s, x, t, sums, grad, tick, wait, done, last):
    wait("n2")
    wait("scales")
    u = upstream()
    n2 = s["n2"][...]
    back = norm_back(u, n2, s["scales"][1][:, 0:1], sm[9:10, :])
    sums[9:10, :] = column_sum(u * n2)
    sums[11:12, :] = column_sum(u)
    t["big"][...] = back
    low16 = back.astype(BF16)
    t["low"][...] = low16
    sums[3:4, :] = column_sum(low16.astype(F32))
    t["left"][...] = jnp.transpose(low16)
    done("n2")
    wait("act")
    grad(DOWN, t["left"], s["act"])
    done("act")
    wait(DOWN)
    wait("slope")

    for j in range(4):
        cols = slice(j * D, j * D + D)
        ub = (nt(t["low"][...], w[DOWN][cols, :]) * s["slope"][:, cols].astype(F32)).astype(BF16)
        s["slope"][:, cols] = ub
        sums[4 + j : 5 + j, :] = column_sum(ub.astype(F32))
        tick("up_back", j)
    done(DOWN)
    wait("hid")
    t["left"][...] = jnp.transpose(s["hid"][...])
    done("hid")
    grad("up", t["left"], s["slope"])
    wait("up")
    hb = t["big"][...] + nt(s["slope"][...], w["up"][...])
    done("up")
    done("slope")
    wait("n1")
    n1 = s["n1"][...]
    sums[8:9, :] = column_sum(hb * n1)
    sums[10:11, :] = column_sum(hb)
    fb = norm_back(hb, n1, s["scales"][0][:, 0:1], sm[8:9, :])
    t["big"][...] = fb
    low16 = fb.astype(BF16)
    t["low"][...] = low16
    sums[2:3, :] = column_sum(low16.astype(F32))
    done("n1")
    done("scales")
    tick("hidden")
    wait("mixed")
    t["left"][...] = jnp.transpose(s["mixed"][...])
    grad("o", t["left"], t["low"])
    wait("o")
    t["mb"][...] = nt(t["low"][...], w["o"][...]).astype(BF16)
    done("o")
    tick("mixed")
    _, ak, av = mask_columns(label)
    ak16, av16 = ak.astype(BF16), av.astype(BF16)
    low = half_lanes()
    masks = [low, jnp.logical_not(low)]
    wait("saved_qkv")
    wait("aug")

    def pair(p):
        at = pl.multiple_of(p * 128, 128)
        qp = s[QKV][:, pl.ds(at, 128)]
        kp = s[QKV][:, pl.ds(D + at, 128)]
        vp = s[QKV][:, pl.ds(2 * D + at, 128)]
        dp = t["mb"][:, pl.ds(at, 128)]
        aq16 = s["aug"][p]
        product = dp.astype(F32) * s["mixed"][:, pl.ds(at, 128)].astype(F32)
        even = -jnp.sum(jnp.where(low, product, 0.0), axis=1, keepdims=True)
        odd = -jnp.sum(jnp.where(low, 0.0, product), axis=1, keepdims=True)
        ad16 = three_parts(jnp.where(low, odd, even), jnp.zeros((ROWS, 128), F32)).astype(BF16)
        scores = [nt(jnp.where(m, kp, ak16), jnp.where(m, qp, aq16)) for m in masks]
        prob_back = [nt(jnp.where(m, vp, av16), jnp.where(m, dp, ad16)) for m in masks]
        probs = [jnp.exp(score) for score in scores]
        score_back = [(probs[e] * prob_back[e]).astype(BF16) for e in range(2)]
        value_part = [nn(probs[e].astype(BF16), dp) for e in range(2)]
        key_part = [nn(score_back[e], qp) for e in range(2)]
        query_part = [tn(score_back[e], kp) * 0.125 for e in range(2)]
        for k, (even, odd) in enumerate((query_part, key_part, value_part)):
            t["qb"][:, pl.ds(k * D + at, 128)] = jnp.where(low, even, odd).astype(BF16)

    def two_pairs(i):
        pair(2 * i)
        pair(2 * i + 1)
        tick("pairs", i)

    times(0, PAIRS // 2, two_pairs)
    done("saved_qkv")
    done("aug")
    done("mixed")
    sums[0:1, :] = column_sum(t["qb"][:, 0:D].astype(F32))
    sums[1:2, :] = column_sum(t["qb"][:, 2 * D :].astype(F32))
    t["left"][...] = jnp.transpose(x[...])
    grad(QKV, t["left"], t["qb"])
    wait(QKV)
    last(t["big"][...] + nt(t["qb"][...], w[QKV][...]))
    done(QKV)
    tick("end")


def whole_step(*refs):
    it = iter(refs)
    take = lambda n: [next(it) for _ in range(n)]
    frames, cotangent, segments, keep_in, width_in, hidden_in, gain_in, shift_in = take(8)
    weight_in = dict(zip(WEIGHTS, take(4)))
    layer_out, input_back, shares, small_out = take(4)
    weight_far = dict(zip(WEIGHTS, take(4)))
    (given,) = take(1)
    spill = dict(zip(SAVED, take(len(SAVED))))
    w = dict(zip(WEIGHTS, take(4)))
    s = dict(zip(SAVED, take(len(SAVED))))
    t = dict(zip(TEMPORARY, take(len(TEMPORARY))))
    x0, x1, x2, cot, dx1, small, sums, keep_tile, give_tile = take(9)
    rb, sbuf, kbuf, r1, zbuf, zr1, part, zs2, zr2, ybuf, r3, fbuf, sb, sr = take(14)
    (
        load_sem, piece_sem, store_sem, spill_sem, in_sem, out_sem, out_recv, w_send, w_recv, small_sem,
        give_send, give_recv, rb_sem, s1_send, s1_recv, z1_send, z1_recv,
        z2_send, z2_recv, s3_send, s3_recv, push_send, push_recv, sum_send, sum_recv, back_sem, back_recv,
    ) = take(27)

    me = lax.axis_index(SECTION_AXIS)
    z = lax.axis_index(SHARD_AXIS)
    r = lax.axis_index(REPLICA_AXIS)
    other = 1 - me
    x_at, y_at = lax.rem(r, 2), lax.div(r, 2)
    x_near, y_near = r + 1 - 2 * x_at, r + 2 - 4 * y_at
    half = (1 - me) * x_at + me * y_at
    first_near = (1 - me) * x_near + me * y_near
    second_near = (1 - me) * y_near + me * x_near
    is_end = lax.rem(z, 3) == 0
    is_middle = jnp.logical_not(is_end)
    partner = (other, z, r)
    z_near = z + 1 - 2 * lax.rem(z, 2)

    def local(src, dst, sem):
        return pltpu.make_async_copy(src, dst, sem)

    def remote(src, dst, send, recv, device):
        return pltpu.make_async_remote_copy(
            src_ref=src, dst_ref=dst, send_sem=send, recv_sem=recv, device_id=device, device_id_type=MESH
        )

    own_rows = pl.ds(pl.multiple_of(me * ROWS, ROWS), ROWS)
    load_frames = local(frames.at[own_rows], x0, in_sem.at[0])
    load_cot = local(cotangent.at[own_rows], cot, in_sem.at[1])

    def weight_near(k):
        return local(weight_in[k].at[0], w[k], load_sem.at[WEIGHTS.index(k)])

    def weight_got(k):
        return local(weight_far[k], w[k], load_sem.at[WEIGHTS.index(k)])

    def piece(ref, k, i):
        if k == "o":
            return ref
        if k == DOWN:
            return ref.at[i * D : (i + 1) * D]
        return ref.at[:, i * D : (i + 1) * D]

    near_piece, far_piece, far_store = {}, {}, {}
    for number, (k, i) in enumerate(PIECES):
        source = piece(weight_in[k].at[0], k, i)
        near_piece[k, i] = local(source, piece(w[k], k, i), piece_sem.at[number])
        device = partner if k != DOWN else [partner, (other, z, x_near), (other, z, y_near), (other, z_near, r)][i]
        far_piece[k, i] = remote(source, piece(w[k], k, i), w_send.at[number], w_recv.at[number], device)
        far_store[k, i] = remote(source, piece(weight_far[k], k, i), w_send.at[number], w_recv.at[number], partner)
    small_send = remote(small.at[me], small.at[me], small_sem.at[0], small_sem.at[1], partner)

    load_frames.start()

    @pl.when(me == 0)
    def _():
        for key in PIECES:
            near_piece[key].start()

    small[me, 0:4] = width_in[0]
    for i in range(4):
        small[me, 4 + i : 5 + i] = hidden_in[0:1, i * D : (i + 1) * D]
    small[me, 8:10] = gain_in[0]
    small[me, 10:12] = shift_in[0]
    for i in range(2):
        small[me, 12 + i : 13 + i] = jnp.broadcast_to(keep_in[0:1, i : i + 1].astype(F32), (1, D))
    small[me, 14:16] = jnp.zeros((2, D), F32)

    barrier = pltpu.get_barrier_semaphore()
    greeted = [partner, (me, z, x_near), (me, z, y_near), (other, z, x_near), (other, z, y_near), (other, z_near, r)]
    for device in greeted:
        pl.semaphore_signal(barrier, inc=1, device_id=device, device_id_type=MESH)
    for step in (1, 2):

        @pl.when(z + step < 4)
        def _(step=step):
            pl.semaphore_signal(barrier, inc=1, device_id=(me, z + step, r), device_id_type=MESH)

        @pl.when(z >= step)
        def _(step=step):
            pl.semaphore_signal(barrier, inc=1, device_id=(me, z - step, r), device_id_type=MESH)

    pl.semaphore_wait(barrier, len(greeted) + 2 + lax.rem(lax.div(z + 1, 2), 2))

    small_send.start()

    @pl.when(me == 0)
    def _():
        for key in PIECES:
            far_piece[key].start()

    @pl.when(me == 1)
    def _():
        for key in PIECES:
            far_store[key].start()

    load_cot.start()
    sums[...] = jnp.zeros_like(sums)
    label = label_columns([segments[pl.ds(4 * me + i, 1), :].astype(F32) for i in range(4)])
    valid = jnp.where(label[:, 0:1] >= 0.0, 1.0, 0.0)

    def spilled(k):
        return local(s[k], spill[k], spill_sem.at[list(SAVED).index(k)])

    def saved_load(k):
        return local(spill[k], s[k], spill_sem.at[list(SAVED).index(k)])

    def store_weight(k):
        return local(w[k], weight_far[k], store_sem.at[WEIGHTS.index(k)])

    def store_start(k):
        @pl.when(me == 1)
        def _():
            store_weight(k).start()

    def next_weight(k):
        @pl.when(me == 0)
        def _():
            for key in PIECES:
                if key[0] == k:
                    far_store[key].wait_recv()
            weight_got(k).start()

        @pl.when(me == 1)
        def _():
            store_weight(k).wait()
            weight_near(k).start()

    def first_weight(k):
        @pl.when(me == 0)
        def _():
            weight_near(k).start()

        @pl.when(me == 1)
        def _():
            weight_got(k).start()

    def weight_wait(k):
        weight_near(k).wait()

    def piece_wait(k, i):
        @pl.when(me == 0)
        def _():
            near_piece[k, i].wait()

        @pl.when(me == 1)
        def _():
            far_piece[k, i].wait_recv()

    def hook0(point, i=None):
        if point == "part":
            if i == 0:
                load_frames.wait()
                small_send.wait()
            piece_wait(QKV, i)
        elif point == QKV:
            store_start(QKV)
            spilled(QKV).start()
        elif point == "attention":
            next_weight(QKV)
            spilled("mixed").start()
            spilled("aug").start()
            piece_wait("o", 0)
        elif point == "first":
            store_start("o")
            spilled("n1").start()
            spilled("hid").start()
        elif point == "up_part":
            piece_wait("up", i)
        elif point == "up":
            next_weight("o")
            store_start("up")
            spilled("act").start()
            spilled("slope").start()
            for i in range(4):
                piece_wait(DOWN, i)
        elif point == "second":
            store_start(DOWN)
            spilled("n2").start()
            spilled("scales").start()

    def hook1(point, i=None):
        if point == "part":
            if i == 0:
                spilled(QKV).wait()
                weight_wait(QKV)
        elif point == QKV:
            next_weight("up")
            spilled("mixed").wait()
            spilled("aug").wait()
        elif point == "attention":
            next_weight(DOWN)
            spilled("n1").wait()
            spilled("hid").wait()
            spilled("scales").wait()
            weight_wait("o")
        elif point == "first":
            spilled("act").wait()
            spilled("slope").wait()
            weight_wait("up")
        elif point == "up":
            spilled("n2").wait()
            weight_wait(DOWN)

    def keep_of(layer):
        return jnp.where(me == 0, small[layer, 12:13, 0:1], small[layer, 13:14, 0:1])

    def out_copy(src, layer, buffer, send, recv, start):
        here = local(src, buffer.at[own_rows], send.at[layer])
        there = remote(src, buffer.at[own_rows], send.at[layer], recv, partner)

        @pl.when(me == layer)
        def _():
            here.start() if start else here.wait()

        @pl.when(me != layer)
        def _():
            there.start() if start else there.wait_send()

    def layer_result(result, x, layer):
        kept = jnp.where(keep_of(layer) > 0.5, result, x[...].astype(F32))
        return (valid * kept).astype(BF16)

    x1[...] = layer_result(forward(x0, label, w, small.at[0], s, hook0), x0, 0)
    out_copy(x1, 0, layer_out, out_sem, out_recv.at[0], True)
    x2[...] = layer_result(forward(x1, label, w, small.at[1], s, hook1), x1, 1)
    out_copy(x2, 1, layer_out, out_sem, out_recv.at[0], True)

    def give_copy(c):
        slot = lax.rem(c, 4)
        return remote(give_tile.at[slot], given.at[c], give_send.at[slot], give_recv.at[c], partner)

    def load_given(c):
        return local(given.at[c], rb.at[lax.rem(c, 2)], rb_sem.at[lax.rem(c, 2)])

    def copy_first(c):
        a, b = lax.rem(c, 4), lax.rem(c, SLOTS)
        return remote(sbuf.at[a], r1.at[b], s1_send.at[a], s1_recv.at[b], (me, z, first_near))

    def copy_end(c):
        a, b = lax.rem(c, 4), lax.rem(c, SLOTS)
        rows = pl.ds(pl.multiple_of(SHARE - SHARE * lax.div(z, 3), SHARE), 3 * SHARE)
        return remote(zbuf.at[a, rows], zr1.at[b], z1_send.at[a], z1_recv.at[b], (me, 1 + lax.div(z, 3), r))

    def copy_middle(c):
        a, b = lax.rem(c, 4), lax.rem(c, SLOTS)
        rows = pl.ds(pl.multiple_of(3 * SHARE * lax.div(z, 2), SHARE), SHARE)
        return remote(
            zbuf.at[a, rows], zr1.at[b, pl.ds(0, SHARE)], z1_send.at[a], z1_recv.at[b], (me, 3 * lax.div(z, 2), r)
        )

    def copy_across(c, which):
        a, b = lax.rem(c, 4), lax.rem(c, FAR_SLOTS)
        far = 3 - z if which == 0 else 3 - 3 * lax.div(z, 2)
        return remote(zs2.at[a, which], zr2.at[b], z2_send.at[a, which], z2_recv.at[b], (me, far, r))

    def copy_second(c):
        a, b = lax.rem(c, 4), lax.rem(c, SLOTS)
        return remote(ybuf.at[a], r3.at[b], s3_send.at[a], s3_recv.at[b], (me, z, second_near))

    def push(c, start):
        a = lax.rem(c, 4)
        layer = 1 - lax.div(c, LAYER_CHUNKS)
        place = lax.rem(c, LAYER_CHUNKS)
        cols = pl.ds(pl.multiple_of((2 * (2 * place + me) + half) * 128, 128), 128)
        here = local(fbuf.at[a], shares.at[:, cols], push_send.at[a, 0])
        beside = remote(fbuf.at[a], shares.at[:, cols], push_send.at[a, 0], push_recv.at[0, place], partner)
        near_same = remote(
            fbuf.at[a], shares.at[:, cols], push_send.at[a, 1], push_recv.at[1, place], (me, z, first_near)
        )
        near_other = remote(
            fbuf.at[a], shares.at[:, cols], push_send.at[a, 1], push_recv.at[2, place], (other, z, first_near)
        )

        @pl.when(layer == me)
        def _():
            here.start() if start else here.wait()
            near_same.start() if start else near_same.wait_send()

        @pl.when(layer != me)
        def _():
            beside.start() if start else beside.wait_send()
            near_other.start() if start else near_other.wait_send()

    def at_stage(c):
        return (c >= 0) & (c < CHUNKS)

    def comm(now):
        @pl.when(at_stage(now - STEP[4]))
        def _():
            c = now - STEP[4]
            a, b = lax.rem(c, 4), lax.rem(c, SLOTS)
            copy_second(c).wait()

            @pl.when(c >= 4)
            def _():
                push(c - 4, False)

            fbuf[a] = ybuf[a] + r3[b]
            push(c, True)

        @pl.when(at_stage(now - STEP[3]))
        def _():
            c = now - STEP[3]
            a, b = lax.rem(c, 4), lax.rem(c, FAR_SLOTS)

            @pl.when(is_middle)
            def _():
                copy_across(c, 0).wait_send()
                copy_across(c, 1).wait_send()

            copy_across(c, 0).wait_recv()
            ybuf[a] = (part[a] + zr2[b].astype(F32)).astype(BF16)
            copy_second(c).start()

        @pl.when(at_stage(now - STEP[2]))
        def _():
            c = now - STEP[2]
            a, b = lax.rem(c, 4), lax.rem(c, SLOTS)

            @pl.when(is_end)
            def _():
                copy_end(c).wait_send()
                copy_middle(c).wait_recv()
                own = pl.ds(pl.multiple_of(z * SHARE, SHARE), SHARE)
                part[a] = kbuf[b, own] + zr1[b, 0:SHARE].astype(F32)

            @pl.when(is_middle)
            def _():
                copy_middle(c).wait_send()
                copy_end(c).wait_recv()
                low_row = SHARE * (2 - z)

                def sum_of(row):
                    row = pl.multiple_of(row, SHARE)
                    return (
                        kbuf[b, pl.ds(pl.multiple_of(low_row + row, SHARE), SHARE)]
                        + zr1[b, pl.ds(row, SHARE)].astype(F32)
                    )

                zs2[a, 0] = sum_of(jnp.int32(SHARE)).astype(BF16)
                zs2[a, 1] = sum_of(2 * SHARE * (2 - z)).astype(BF16)
                copy_across(c, 0).start()
                copy_across(c, 1).start()
                part[a] = sum_of(2 * SHARE * (z - 1))

        @pl.when(at_stage(now - STEP[1]))
        def _():
            c = now - STEP[1]
            a, b = lax.rem(c, 4), lax.rem(c, SLOTS)
            copy_first(c).wait()
            total = kbuf[b] + r1[b].astype(F32)
            kbuf[b] = total
            zbuf[a] = total.astype(BF16)

            @pl.when(is_end)
            def _():
                copy_end(c).start()

            @pl.when(is_middle)
            def _():
                copy_middle(c).start()

        @pl.when(at_stage(now - STEP[0]))
        def _():
            c = now - STEP[0]
            a, b, d = lax.rem(c, 4), lax.rem(c, SLOTS), lax.rem(c, 2)
            e = lax.rem(c, KEPT)
            load_given(c).wait()
            sbuf[a] = keep_tile[e, 1 - half] + rb[d, 1 - half]
            copy_first(c).start()
            kbuf[b] = keep_tile[e, half].astype(F32) + rb[d, half].astype(F32)

        @pl.when(at_stage(now))
        def _():
            give_copy(now).wait_recv()
            load_given(now).start()

    def run_layer(layer, upstream, passed, x, ticks, wait, done):
        first_tile = 0 if layer == 1 else LAYER_TILES

        def put(c, tile, value):
            @pl.when(me == tile)
            def _():
                for i in range(2):
                    keep_tile[lax.rem(c, KEPT), i] = value[:, i * 128 : (i + 1) * 128]

            @pl.when(me != tile)
            def _():
                @pl.when(c >= 4)
                def _():
                    give_copy(c - 4).wait_send()

                for i in range(2):
                    give_tile[lax.rem(c, 4), i] = value[:, i * 128 : (i + 1) * 128]
                give_copy(c).start()

        def single(k, left, right, j):
            q = first_tile + FIRST_TILE[k] + j
            put(q // 2, q % 2, nn(left[...], right[:, j * TILE : (j + 1) * TILE]).astype(BF16))

        def grad(k, left, right):
            marks = ticks.get(k, {})
            first = FIRST_TILE[k] % 2
            begin = (first_tile + FIRST_TILE[k] + first) // 2
            n = (TILES[k] - first) // 2
            if first:
                single(k, left, right, 0)

            def chunk(j):
                c = begin + j
                cols = pl.ds(pl.multiple_of((2 * j + first) * TILE, TILE), 2 * TILE)
                g = nn(left[...], right[:, cols]).astype(BF16)
                put(c, 0, g[:, :TILE])
                put(c, 1, g[:, TILE:])
                for at, number in marks.items():

                    @pl.when(j == at)
                    def _(number=number):
                        comm(jnp.int32(number))

            times(0, n, chunk)
            if (TILES[k] - first) % 2:
                single(k, left, right, TILES[k] - 1)

        def tick(point, index=None):
            marks = ticks.get(point)
            if marks is None:
                return
            if index is None:
                comm(jnp.int32(marks))
            elif isinstance(marks, dict):
                if index in marks:
                    comm(jnp.int32(marks[index]))
            else:
                comm(marks + index)

        sm = small.at[layer]
        keep = keep_of(layer)

        def masked():
            return upstream[...].astype(F32) * (valid * keep)

        def last(value):
            passed[...] = value + upstream[...].astype(F32) * (valid * (1.0 - keep))

        backward(masked, label, w, sm, s, x, t, sums.at[layer], grad, tick, wait, done, last)

    def wait1(k):
        pass

    def done1(k):
        if k in WEIGHTS:
            first_weight(k)
        elif k == "saved_qkv":
            saved_load(QKV).start()
        else:
            saved_load(k).start()

    def wait0(k):
        if k in WEIGHTS:
            weight_wait(k)
        elif k == "saved_qkv":
            saved_load(QKV).wait()
        else:
            saved_load(k).wait()

    load_cot.wait()
    run_layer(1, cot, dx1, x1, TICKS[0], wait1, done1)
    out_copy(dx1, 1, input_back, back_sem, back_recv.at[0], True)
    run_layer(0, dx1, s["n1"], x0, TICKS[1], wait0, lambda k: None)
    out_copy(s["n1"], 0, input_back, back_sem, back_recv.at[0], True)

    def sum_copy(step):
        if step == 0:
            return remote(sums.at[other], sr.at[0], sum_send.at[0], sum_recv.at[0], partner)
        z_two = lax.rem(z + 2, 4)
        device = [(me, z, x_near), (me, z, y_near), (me, z_near, r), (me, z_two, r)][step - 1]
        return remote(sb.at[step - 1], sr.at[step], sum_send.at[step], sum_recv.at[step], device)

    sum_copy(0).start()

    def final(now):
        for step in range(5):

            @pl.when(now == SUM_TICKS[step])
            def _(step=step):
                sum_copy(step).wait()
                if step == 0:
                    sb[0] = sums[me] + sr[0]
                else:
                    sb[step] = sb[step - 1] + sr[step]
                if step < 4:
                    sum_copy(step + 1).start()

        comm(now)

    times(SUM_TICKS[0], CHUNKS + STEP[-1], final)
    small_out[...] = sb[4]

    times(CHUNKS - 4, CHUNKS, lambda c: push(c, False))
    for stream in range(3):

        def arrived(place, stream=stream):
            remote(
                fbuf.at[0], shares.at[:, pl.ds(0, 128)], push_send.at[0, 0], push_recv.at[stream, place], partner
            ).wait_recv()

        times(0, LAYER_CHUNKS, arrived)
    times(CHUNKS - 4, CHUNKS, lambda c: give_copy(c).wait_send())
    for key in PIECES:
        far_piece[key].wait_send()
    out_copy(x1, 0, layer_out, out_sem, out_recv.at[0], False)
    out_copy(x2, 1, layer_out, out_sem, out_recv.at[0], False)
    out_copy(dx1, 1, input_back, back_sem, back_recv.at[0], False)
    out_copy(s["n1"], 0, input_back, back_sem, back_recv.at[0], False)
    remote(x1, layer_out.at[own_rows], out_sem.at[0], out_recv.at[0], partner).wait_recv()
    remote(dx1, input_back.at[own_rows], back_sem.at[0], back_recv.at[0], partner).wait_recv()


TICKS = (
    {DOWN: {1: 0, 3: 1, 5: 2}, "up_back": {1: 3, 3: 4}, "up": {1: 5, 3: 6, 5: 7}, "hidden": 8, "mixed": 9,
     "pairs": 10, QKV: {1: 13, 3: 14}, "end": 15},
    {DOWN: {1: 16, 3: 17, 5: 18}, "up_back": {1: 19, 3: 20}, "up": {1: 21, 3: 22, 5: 23}, "hidden": 24, "mixed": 25,
     "pairs": 26, QKV: {1: 29, 3: 30}, "end": 31},
)
SUM_TICKS = (32, 37, 40, 43, 46)
PIECES = [(QKV, 0), (QKV, 1), (QKV, 2), ("o", 0)] + [("up", i) for i in range(4)] + [(DOWN, i) for i in range(4)]


def any_space():
    return pl.BlockSpec(memory_space=pl.ANY)


def in_vmem():
    return pl.BlockSpec(memory_space=pltpu.VMEM)


def run_whole(*arguments):
    shape = jax.ShapeDtypeStruct
    outs = [
        shape((2 * ROWS, D), BF16),
        shape((2 * ROWS, D), F32),
        shape((SHARE, LAYER_TILES * TILE), BF16),
        shape((16, D), F32),
    ]
    outs += [shape(WEIGHT_SHAPE[k], BF16) for k in WEIGHTS]
    outs += [shape((CHUNKS, 2, D, 128), BF16)]
    outs += [shape(*SAVED[k]) for k in SAVED]
    out_specs = [any_space()] * 3 + [in_vmem()] + [any_space()] * (len(outs) - 4)
    dma = pltpu.SemaphoreType.DMA
    scratch = [pltpu.VMEM(WEIGHT_SHAPE[k], BF16) for k in WEIGHTS]
    scratch += [pltpu.VMEM(*SAVED[k]) for k in SAVED]
    scratch += [pltpu.VMEM(*TEMPORARY[k]) for k in TEMPORARY]
    scratch += [pltpu.VMEM((ROWS, D), BF16)] * 4
    scratch += [
        pltpu.VMEM((ROWS, D), F32),
        pltpu.VMEM((2, 16, D), F32),
        pltpu.VMEM((2, 16, D), F32),
        pltpu.VMEM((KEPT, 2, D, 128), BF16),
        pltpu.VMEM((4, 2, D, 128), BF16),
        pltpu.VMEM((2, 2, D, 128), BF16),
        pltpu.VMEM((4, D, 128), BF16),
        pltpu.VMEM((SLOTS, D, 128), F32),
        pltpu.VMEM((SLOTS, D, 128), BF16),
        pltpu.VMEM((4, D, 128), BF16),
        pltpu.VMEM((SLOTS, 3 * SHARE, 128), BF16),
        pltpu.VMEM((4, SHARE, 128), F32),
        pltpu.VMEM((4, 2, SHARE, 128), BF16),
        pltpu.VMEM((FAR_SLOTS, SHARE, 128), BF16),
        pltpu.VMEM((4, SHARE, 128), BF16),
        pltpu.VMEM((SLOTS, SHARE, 128), BF16),
        pltpu.VMEM((4, SHARE, 128), BF16),
        pltpu.VMEM((5, 16, D), F32),
        pltpu.VMEM((5, 16, D), F32),
    ]
    n = len(PIECES)
    sems = [
        (4,), (n,), (4,), (len(SAVED),), (2,), (2,), (1,), (n,), (n,), (2,),
        (4,), (CHUNKS,), (2,), (4,), (SLOTS,), (4,), (SLOTS,),
        (4, 2), (FAR_SLOTS,), (4,), (SLOTS,), (4, 2), (3, LAYER_CHUNKS), (5,), (5,), (2,), (1,),
    ]
    scratch += [dma(n) for n in sems]
    got = pl.pallas_call(
        whole_step,
        out_shape=outs,
        in_specs=[any_space()] * 2 + [in_vmem()] * 6 + [any_space()] * 4,
        out_specs=out_specs,
        scratch_shapes=scratch,
        compiler_params=pltpu.CompilerParams(
            collective_id=0, has_side_effects=True, vmem_limit_bytes=64 * 2**20 - 2**17
        ),
        name="whole_step",
    )(*arguments)
    return got[:4]


def finish_step(layer_out, input_back, shares, sums, *refs):
    out_layer, out_back, out_qkv, out_o, out_up, out_down, width, hidden, gain, shift = refs[:10]
    held, big_qkv, big_o, big_up, big_down, rows_low, rows_wide, sem = refs[10:]
    big = {QKV: big_qkv, "o": big_o, "up": big_up, DOWN: big_down}
    out = {QKV: out_qkv, "o": out_o, "up": out_up, DOWN: out_down}
    order = (DOWN, "up", QKV, "o")
    cols = {k: slice(FIRST_TILE[k] * TILE, (FIRST_TILE[k] + TILES[k]) * TILE) for k in order}
    load = {k: pltpu.make_async_copy(shares.at[:, cols[k]], held.at[:, cols[k]], sem.at[i]) for i, k in enumerate(order)}
    store = {k: pltpu.make_async_copy(big[k], out[k].at[0], sem.at[4 + i]) for i, k in enumerate(order)}
    through = [(layer_out, rows_low, out_layer), (input_back, rows_wide, out_back)]
    into = [pltpu.make_async_copy(a, b, sem.at[8 + i]) for i, (a, b, _) in enumerate(through)]
    onward = [pltpu.make_async_copy(b, c.at[0], sem.at[10 + i]) for i, (_, b, c) in enumerate(through)]
    for k in order:
        load[k].start()
    for copy in into:
        copy.start()
    for k in order:
        load[k].wait()
        big[k][...] = held[:, cols[k]].astype(F32)
        store[k].start()
    for one, two in zip(into, onward):
        one.wait()
        two.start()
    z = lax.axis_index(SHARD_AXIS)
    for i in range(4):

        @pl.when(z == i)
        def _(i=i):
            mine = slice(i * SHARE, (i + 1) * SHARE)
            width[0] = sums[0:4, mine]
            hidden[...] = sums[4 + i : 5 + i, :]
            gain[0] = sums[8:10, mine]
            shift[0] = sums[10:12, mine]

    for k in order:
        store[k].wait()
    for copy in onward:
        copy.wait()


def run_finish(layer_out, input_back, shares, sums):
    shape = jax.ShapeDtypeStruct
    outs = [shape((1, 2 * ROWS, D), BF16), shape((1, 2 * ROWS, D), F32), shape((1, SHARE, 3 * D), F32)]
    outs += [shape((1, SHARE, D), F32), shape((1, SHARE, FF), F32), shape((1, SHARE, FF), F32)]
    outs += [shape((1, 4, SHARE), F32), shape((1, D), F32), shape((1, 2, SHARE), F32), shape((1, 2, SHARE), F32)]
    return pl.pallas_call(
        finish_step,
        out_shape=outs,
        in_specs=[any_space()] * 3 + [in_vmem()],
        out_specs=[any_space()] * 6 + [in_vmem()] * 4,
        scratch_shapes=[
            pltpu.VMEM((SHARE, LAYER_TILES * TILE), BF16),
            pltpu.VMEM((SHARE, 3 * D), F32),
            pltpu.VMEM((SHARE, D), F32),
            pltpu.VMEM((SHARE, FF), F32),
            pltpu.VMEM((SHARE, FF), F32),
            pltpu.VMEM((2 * ROWS, D), BF16),
            pltpu.VMEM((2 * ROWS, D), F32),
            pltpu.SemaphoreType.DMA((12,)),
        ],
        compiler_params=pltpu.CompilerParams(vmem_limit_bytes=64 * 2**20 - 2**17),
        name="finish_step",
    )(layer_out, input_back, shares, sums)


def on_device_block(
    frames, cotangent, segments, layer_keep, joint_weight, output_weight, up_weight, down_weight,
    width_bias, hidden_bias, norm_gain, norm_shift,
):
    got = run_whole(
        frames, cotangent, segments.reshape(8, 128), layer_keep, width_bias, hidden_bias, norm_gain, norm_shift,
        joint_weight, output_weight, up_weight, down_weight,
    )
    outs = list(run_finish(*got))
    outs[5] = jnp.transpose(outs[5], (0, 2, 1))
    return tuple(outs)


def solution(mesh):
    sizes = dict(mesh.shape)
    fits = sizes == {SECTION_AXIS: 2, SHARD_AXIS: 4, REPLICA_AXIS: 4}
    placed = (
        P((SHARD_AXIS, REPLICA_AXIS), None),
        P((SHARD_AXIS, REPLICA_AXIS), None),
        P((SHARD_AXIS, REPLICA_AXIS)),
        P(SECTION_AXIS, (SHARD_AXIS, REPLICA_AXIS)),
        P(SECTION_AXIS, None, None),
        P(SECTION_AXIS, None, None),
        P(SECTION_AXIS, None, None),
        P(SECTION_AXIS, None, None),
        P(SECTION_AXIS, None, None),
        P(SECTION_AXIS, None),
        P(SECTION_AXIS, None, None),
        P(SECTION_AXIS, None, None),
    )
    return jax.shard_map(
        on_device_block if fits else on_device_general,
        mesh=mesh,
        in_specs=placed,
        out_specs=(
            P(SECTION_AXIS, (SHARD_AXIS, REPLICA_AXIS), None),
            P(SECTION_AXIS, (SHARD_AXIS, REPLICA_AXIS), None),
            P(SECTION_AXIS, SHARD_AXIS, None),
            P(SECTION_AXIS, SHARD_AXIS, None),
            P(SECTION_AXIS, SHARD_AXIS, None),
            P(SECTION_AXIS, None, SHARD_AXIS),
            P(SECTION_AXIS, None, SHARD_AXIS),
            P(SECTION_AXIS, SHARD_AXIS),
            P(SECTION_AXIS, None, SHARD_AXIS),
            P(SECTION_AXIS, None, SHARD_AXIS),
        ),
        check_vma=False,
    )
```
